128 devices in a mesh: gx: 8 (over y_lo, x), gy: 16 (over y_hi, z, core).
Axes of the slice: x: 4, y: 4 (y_hi: 2, y_lo: 2; y = y_hi * 2 + y_lo), z: 4, core: 2. Of those that a mesh axis runs over, the one named last changes fastest.
Arguments:
- tokens: bfloat16 [512, 8192], P('gx', 'gy'), may hold values from -12 to 12
- segment_ids: int32 [512], P('gy'), may hold values from 0 to 3, never falling along the last dimension, each value on 1 to 384 neighbouring positions
- attn_gain: bfloat16 [8192], P('gy'), may hold values from 0.5 to 1.5
- query_weight: bfloat16 [8192, 8192], P(('gx', 'gy')), may hold values from -1 to 1
- query_bias: bfloat16 [8192], P('gx'), may hold values from -3 to 3
- key_weight: bfloat16 [1024, 8192], P(('gx', 'gy')), may hold values from -20 to 20
- value_weight: bfloat16 [1024, 8192], P(('gx', 'gy')), may hold values from -0.0625 to 0.0625
- value_bias: bfloat16 [1024], P('gx'), may hold values from -3 to 3
- out_weight: bfloat16 [8192, 8192], P(('gx', 'gy')), may hold values from -0.0625 to 0.0625
- ffn_gain: bfloat16 [8192], P('gy'), may hold values from 0.5 to 1.5
- gate_weight: bfloat16 [29568, 8192], P(('gx', 'gy')), may hold values from -0.0625 to 0.0625
- up_weight: bfloat16 [29568, 8192], P(('gx', 'gy')), may hold values from -0.0625 to 0.0625
- down_weight: bfloat16 [29568, 8192], P(('gx', 'gy')), may hold values from -0.03125 to 0.03125
Outputs:
- mixed: bfloat16 [512, 8192], P('gx', 'gy')
The draws below stay inside these ranges and needn't reach their ends.
Inputs may be any that keep to these rules, and one draw needn't show every extreme that they name: `segment_ids`: documents occupy consecutive positions, numbers never fall, and one document spans exactly 384 positions.
All inputs are finite; a program needn't handle non-finite values.
Results may differ from the reference program's by a relative error of at most 0.012.
The reference program's roundings to bfloat16 on the way count: a program that leaves them out, or rounds other values in their place, can miss the bound.
Values may be sent and summed in bfloat16 or wider, within the bound.
A program may use at most 128 MiB of HBM per device.

```python
import math
import jax
import jax.numpy as jnp
import numpy as np
from jax import lax

D = 8192
HEADS = 64
KV_HEADS = 8
HEAD_DIM = 128
FF = 29568
TOKENS = 512
DOCS = 4
Q_DIM = 8192
KV_DIM = 1024


def draw_tokens(key, part):
    key_row = jax.random.fold_in(key, 21)
    key_col = jax.random.fold_in(key, 22)
    key_main = jax.random.fold_in(key, 23)
    col_pos = jnp.arange(D, dtype=jnp.float32) / D
    row_scale = 10.0 ** (jax.random.uniform(key_row, (TOKENS, 1), dtype=jnp.float32) - 1.0)
    col_scale = 10.0 ** (jax.random.uniform(key_col, (1, D), dtype=jnp.float32) - 1.0) * 3.0 ** (0.5 * col_pos[None, :] - 0.25)
    values = jax.random.truncated_normal(key_main, -6.0, 6.0, (TOKENS, D), dtype=jnp.float32)
    return jnp.clip(values * row_scale * col_scale, -12.0, 12.0).astype(jnp.bfloat16)


def query_values(key):
    return jax.random.truncated_normal(jax.random.fold_in(key, 31), -6.0, 6.0, (Q_DIM, D), dtype=jnp.float32) * D ** (-0.5)


def draw_query_weight(key, part):
    return query_values(key).astype(jnp.bfloat16)


def draw_key_weight(key, part):
    fresh = jax.random.truncated_normal(jax.random.fold_in(key, 33), -6.0, 6.0, (KV_DIM, D), dtype=jnp.float32)
    return (fresh * D ** (-0.5)).astype(jnp.bfloat16)


def level_of(own_key, dims, cuts, low, high):
    loudness, own = 1.0, jax.random.fold_in(own_key, 6)
    for dim, shards_of in cuts:
        draws = jnp.exp(jax.random.uniform(jax.random.fold_in(own, dim), (shards_of,), jnp.float32, low / len(cuts), high / len(cuts)))
        loudness = loudness * jnp.repeat(draws, dims[dim] // shards_of).reshape([-1 if axis == dim else 1 for axis in range(len(dims))])
    return loudness


def length_profile(amount, total, bound, lean):
    loads = [(1 << 20) // math.isqrt(grade ** lean) + 1 for grade in range(2, amount + 1)]
    spare, holding = total - bound - (amount - 1), [1] * (amount - 1)
    while spare > 0:
        candidates = [i for i in range(amount - 1) if holding[i] < bound]
        whole, remaining = sum([loads[i] for i in candidates]), spare
        for i in candidates:
            extra = min(bound - holding[i], max(1, remaining * loads[i] // whole), spare)
            holding[i] = holding[i] + extra
            spare = spare - extra
    return np.array([bound] + holding)


def ragged(key, count, total, reach, skew):
    if count == 2:
        one = jax.random.randint(key, (), max(1, total - reach), min(reach, total - 1) + 1)
        return jnp.stack([one, total - one])
    lengths = jnp.asarray(length_profile(count, total, reach, skew), jnp.int32)
    couples = (count - 1) // 2
    donor, sink = lengths[1:1 + 2 * couples:2], lengths[2:2 + 2 * couples:2]
    margin = jnp.minimum(donor - 1, reach - sink)
    moved = jax.random.randint(jax.random.fold_in(key, 1), (couples,), 0, 1 << 20) % (margin + 1)
    lengths = lengths.at[1:1 + 2 * couples:2].set(donor - moved).at[2:2 + 2 * couples:2].set(sink + moved)
    return lengths[jax.random.permutation(jax.random.fold_in(key, 2), count)]


def gaussian(stream_key, shape, width, bound, pieces=(), kind=jnp.bfloat16):
    array = width * jax.random.normal(stream_key, shape, jnp.float32)
    if pieces:
        array = array * level_of(stream_key, shape, pieces, -0.22, 0.18)
    return jnp.clip(array, -bound, bound).astype(kind)


def setup_inputs(seed: int = 0) -> dict:
    key_list = jax.random.split(jax.random.key(seed), 14)
    return {
        "tokens": draw_tokens(jax.random.fold_in(key_list[13], 71), 0),
        "segment_ids": jnp.searchsorted(jnp.cumsum(ragged(key_list[1], DOCS, TOKENS, TOKENS * 3 // 4, 0)), jnp.arange(TOKENS), side="right").astype(jnp.int32),
        "attn_gain": jnp.clip(1.0 + 0.1 * jax.random.normal(key_list[2], (D,), jnp.float32), 0.5, 1.5).astype(jnp.bfloat16),
        "query_weight": draw_query_weight(jax.random.fold_in(key_list[13], 71), 0),
        "query_bias": gaussian(key_list[4], (Q_DIM,), 0.5, 3.0, ((0, 8),)),
        "key_weight": draw_key_weight(jax.random.fold_in(key_list[13], 71), 0),
        "value_weight": gaussian(key_list[6], (KV_DIM, D), D ** -0.5, 0.0625, ((0, 128),)),
        "value_bias": gaussian(key_list[7], (KV_DIM,), 0.5, 3.0, ((0, 8),)),
        "out_weight": gaussian(key_list[8], (Q_DIM, D), Q_DIM ** -0.5, 0.0625, ((0, 128),)),
        "ffn_gain": jnp.clip(1.0 + 0.1 * jax.random.normal(key_list[9], (D,), jnp.float32), 0.5, 1.5).astype(jnp.bfloat16),
        "gate_weight": gaussian(key_list[10], (FF, D), D ** -0.5, 0.0625, ((0, 128),)),
        "up_weight": gaussian(key_list[11], (FF, D), D ** -0.5, 0.0625, ((0, 128),)),
        "down_weight": gaussian(key_list[12], (FF, D), FF ** -0.5, 0.03125, ((0, 128),)),
    }


EPSILON = 1e-06
ROTARY_BASE = 1000000.0

def project_rows(row_block, weight_rows):
    return lax.dot_general(row_block, weight_rows, (((1,), (1,)), ((), ())), preferred_element_type=jnp.float32)

def normalize(values, feature_gain):
    floats = values.astype(jnp.float32)
    inverse = lax.rsqrt(lax.optimization_barrier(jnp.mean(floats * floats, axis=-1, keepdims=True)) + EPSILON)
    return (floats * inverse * feature_gain.astype(jnp.float32)[None, :]).astype(jnp.bfloat16)

def rotate(values, positions):
    row_count = values.shape[0]
    shaped = values.reshape(row_count, -1, HEAD_DIM)
    half_dim = HEAD_DIM // 2
    frequency = jnp.power(jnp.float32(ROTARY_BASE), -(jnp.arange(half_dim, dtype=jnp.float32) * 2.0) / HEAD_DIM)
    angles = positions[:, None] * frequency[None, :]
    cosine = jnp.cos(angles)[:, None, :]
    sine_part = jnp.sin(angles)[:, None, :]
    first_half = shaped[..., :half_dim]
    second_half = shaped[..., half_dim:]
    turned = jnp.concatenate([first_half * cosine - second_half * sine_part, second_half * cosine + first_half * sine_part], axis=-1)
    return turned.reshape(row_count, -1)

def reference(tokens, segment_ids, attn_gain, query_weight, query_bias, key_weight, value_weight, value_bias, out_weight, ffn_gain, gate_weight, up_weight, down_weight):
    attn_in = normalize(tokens, attn_gain)
    positions = jnp.arange(TOKENS).astype(jnp.float32)
    queries = rotate(project_rows(attn_in, query_weight) + query_bias.astype(jnp.float32)[None, :], positions).astype(jnp.bfloat16)
    keys_all = rotate(project_rows(attn_in, key_weight), positions).astype(jnp.bfloat16)
    values_all = (project_rows(attn_in, value_weight) + value_bias.astype(jnp.float32)[None, :]).astype(jnp.bfloat16)
    group_size = HEADS // KV_HEADS
    heads_q = queries.reshape(TOKENS, KV_HEADS, group_size, HEAD_DIM).transpose(1, 2, 0, 3)
    heads_k = keys_all.reshape(TOKENS, KV_HEADS, HEAD_DIM).transpose(1, 0, 2)
    heads_v = values_all.reshape(TOKENS, KV_HEADS, HEAD_DIM).transpose(1, 0, 2)
    index_row = jnp.arange(TOKENS)
    allowed = (index_row[None, :] <= index_row[:, None]) & (segment_ids[None, :] == segment_ids[:, None])

    def one_group(operands):
        group_q, group_k, group_v = operands
        scores = jnp.einsum('gtd,sd->gts', group_q.astype(jnp.float32), group_k.astype(jnp.float32)) / math.sqrt(HEAD_DIM)
        scores = jnp.where(allowed[None], scores, -jnp.inf)
        row_max = lax.optimization_barrier(jnp.max(scores, axis=-1, keepdims=True))
        weights = jnp.where(allowed[None], jnp.exp(scores - row_max), 0.0)
        denominator = lax.optimization_barrier(jnp.sum(weights, axis=-1, keepdims=True))
        rounded = weights.astype(jnp.bfloat16)
        return jnp.einsum('gts,sd->gtd', rounded.astype(jnp.float32), group_v.astype(jnp.float32)) / denominator
    attended = lax.map(one_group, (heads_q, heads_k, heads_v))
    attended = attended.transpose(2, 0, 1, 3).reshape(TOKENS, HEADS * HEAD_DIM).astype(jnp.bfloat16)
    resid = (tokens.astype(jnp.float32) + jnp.dot(attended, out_weight, preferred_element_type=jnp.float32)).astype(jnp.bfloat16)
    ffn_in = normalize(resid, ffn_gain)
    gate = project_rows(ffn_in, gate_weight)
    up_part = project_rows(ffn_in, up_weight)
    hidden = (jax.nn.silu(gate) * up_part).astype(jnp.bfloat16)
    return (resid.astype(jnp.float32) + jnp.dot(hidden, down_weight, preferred_element_type=jnp.float32)).astype(jnp.bfloat16)
```

```python
import math

import jax
import jax.numpy as jnp
from jax import lax
from jax.sharding import PartitionSpec as P

HEAD_DIM = 128


EPSILON = 1e-06
ROTARY_BASE = 1000000.0


def project_rows(row_block, weight_rows):
    return lax.dot_general(
        row_block, weight_rows, (((1,), (1,)), ((), ())), preferred_element_type=jnp.float32
    )


def rotate(values, positions):
    row_count = values.shape[0]
    shaped = values.reshape(row_count, -1, HEAD_DIM)
    half_dim = HEAD_DIM // 2
    frequency = jnp.power(
        jnp.float32(ROTARY_BASE), -(jnp.arange(half_dim, dtype=jnp.float32) * 2.0) / HEAD_DIM
    )
    angles = positions[:, None] * frequency[None, :]
    cosine = jnp.cos(angles)[:, None, :]
    sine_part = jnp.sin(angles)[:, None, :]
    first_half = shaped[..., :half_dim]
    second_half = shaped[..., half_dim:]
    turned = jnp.concatenate(
        [
            first_half * cosine - second_half * sine_part,
            second_half * cosine + first_half * sine_part,
        ],
        axis=-1,
    )
    return turned.reshape(row_count, -1)


def normalize(values, feature_gain):
    floats = values.astype(jnp.float32)
    squares = lax.psum(jnp.sum(floats * floats, axis=1), "gy")
    feature_total = values.shape[1] * lax.axis_size("gy")
    inverse = lax.rsqrt(squares / feature_total + EPSILON)
    normed = (floats * inverse[:, None] * feature_gain.astype(jnp.float32)[None, :]).astype(
        jnp.bfloat16
    )
    by_row = lax.all_gather(normed, "gx", axis=0, tiled=True)
    return lax.all_gather(by_row, "gy", axis=1, tiled=True)


def scatter_sum(partial):
    by_row = lax.psum_scatter(
        partial.astype(jnp.bfloat16), "gx", scatter_dimension=0, tiled=True
    )
    return lax.psum_scatter(by_row, "gy", scatter_dimension=1, tiled=True).astype(jnp.float32)


def shards(
    tokens,
    segment_ids,
    attn_gain,
    query_weight,
    query_bias,
    key_weight,
    value_weight,
    value_bias,
    out_weight,
    ffn_gain,
    gate_weight,
    up_weight,
    down_weight,
):
    attn_in = normalize(tokens, attn_gain)
    total_rows = attn_in.shape[0]
    local_rows = total_rows // lax.axis_size("gy")
    query_sum = project_rows(attn_in, query_weight)
    keys_own = project_rows(attn_in, key_weight)
    values_own = project_rows(attn_in, value_weight)
    query_sum = lax.all_to_all(query_sum, "gy", split_axis=0, concat_axis=1, tiled=True)
    kv_all = lax.all_gather(
        jnp.stack([keys_own, values_own], axis=0), "gy", axis=2, tiled=True
    )
    query_width = query_sum.shape[1]
    query_index = lax.axis_index("gy") * local_rows + jnp.arange(local_rows, dtype=jnp.int32)
    positions = query_index.astype(jnp.float32)
    queries = rotate(query_sum + query_bias.astype(jnp.float32)[None, :], positions).astype(
        jnp.bfloat16
    )
    key_index = jnp.arange(total_rows, dtype=jnp.int32)
    keys_all = rotate(kv_all[0], key_index.astype(jnp.float32)).astype(jnp.bfloat16)
    values_all = (kv_all[1] + value_bias.astype(jnp.float32)[None, :]).astype(jnp.bfloat16)
    segments_all = lax.all_gather(segment_ids, "gy", axis=0, tiled=True)
    heads_q = queries.reshape(local_rows, -1, HEAD_DIM)
    allowed = (key_index[None, :] <= query_index[:, None]) & (
        segments_all[None, :] == segment_ids[:, None]
    )
    scores = jnp.einsum(
        "tgd,sd->gts", heads_q, keys_all, preferred_element_type=jnp.float32
    ) / math.sqrt(HEAD_DIM)
    scores = jnp.where(allowed, scores, -jnp.inf)
    row_max = jnp.max(scores, axis=-1, keepdims=True)
    weights = jnp.where(allowed, jnp.exp(scores - row_max), 0.0)
    denominator = jnp.sum(weights, axis=-1)
    probabilities = weights.astype(jnp.bfloat16)
    attended = jnp.einsum("gts,sd->tgd", probabilities, values_all, preferred_element_type=jnp.float32)
    attended = attended / denominator.transpose(1, 0)[..., None]
    attended = attended.reshape(local_rows, query_width).astype(jnp.bfloat16)
    attended = lax.all_to_all(attended, "gy", split_axis=1, concat_axis=0, tiled=True)
    attn_out = scatter_sum(jnp.dot(attended, out_weight, preferred_element_type=jnp.float32))
    resid = (tokens.astype(jnp.float32) + attn_out).astype(jnp.bfloat16)
    ffn_in = normalize(resid, ffn_gain)
    gate = project_rows(ffn_in, gate_weight)
    up = project_rows(ffn_in, up_weight)
    hidden = (jax.nn.silu(gate) * up).astype(jnp.bfloat16)
    ffn_out = scatter_sum(jnp.dot(hidden, down_weight, preferred_element_type=jnp.float32))
    return (resid.astype(jnp.float32) + ffn_out).astype(jnp.bfloat16)


def solution(mesh):
    placed = (
        P("gx", "gy"),
        P("gy"),
        P("gy"),
        P(("gx", "gy"), None),
        P("gx"),
        P(("gx", "gy"), None),
        P(("gx", "gy"), None),
        P("gx"),
        P(("gx", "gy"), None),
        P("gy"),
        P(("gx", "gy"), None),
        P(("gx", "gy"), None),
        P(("gx", "gy"), None),
    )
    return jax.shard_map(
        shards, mesh=mesh, in_specs=placed, out_specs=P("gx", "gy"), check_vma=False
    )
```

```python
import functools
import math

import jax
import jax.numpy as jnp
import numpy as np
from jax import lax
from jax.experimental import pallas as pl
from jax.experimental.pallas import tpu as pltpu
from jax.sharding import PartitionSpec as P


HEAD_DIM = 128
EPSILON = 1e-06
ROTARY_BASE = 1000000.0
TOKENS = 512
MODEL = 8192
BLOCK = 512
ROWS = 16
BF = jnp.bfloat16
F32 = jnp.float32
MESH = pl.DeviceIdType.MESH


def dot_nt(left, right):
    return lax.dot_general(left, right, (((1,), (1,)), ((), ())), preferred_element_type=F32)


def dot_nn(left, right):
    return lax.dot_general(left, right, (((1,), (0,)), ((), ())), preferred_element_type=F32)


GATHER = {
    "s1p": (0, 2, 1, 0, 512, 1, 1),
    "s1m": (0, 1, 1, 0, 512, 1, 3),
    "f1m": (1, 3, 1, 0, 256, 1, 3),
    "f1p": (2, 3, 1, 256, 256, 1, 1),
    "o2p": (0, 8, 1, 0, 512, 2, 1),
    "o2m": (0, 4, 1, 0, 512, 2, 3),
    "r2p": (1, 9, 3, 0, 512, 2, 1),
    "r2m": (1, 5, 3, 0, 512, 2, 3),
    "f2m": (4, 12, 2, 0, 512, 2, 3),
    "f2p": (10, 14, 2, 0, 512, 2, 1),
    "o3p": (0, 32, 1, 0, 512, 3, 1),
    "o3m": (0, 16, 1, 0, 512, 3, 3),
    "r3p": (1, 33, 3, 0, 512, 3, 1),
    "r3m": (1, 17, 3, 0, 512, 3, 3),
    "f3m0": (16, 48, 4, 0, 512, 3, 3),
    "f3m1": (20, 52, 4, 0, 512, 3, 3),
    "f3p2": (40, 56, 4, 0, 512, 3, 1),
    "f3p3": (44, 60, 4, 0, 512, 3, 1),
}
for _k in (1, 2, 3):
    GATHER[f"g3p{_k}"] = (4 * _k, 32 + 4 * _k, 4, 0, 512, 3, 1)
    GATHER[f"g3m{_k}"] = (4 * _k, 16 + 4 * _k, 4, 0, 512, 3, 3)
GATHER_ID = {name: i for i, name in enumerate(GATHER)}

SCATTER = {}
for _i, _k in enumerate((3, 2)):
    SCATTER[f"a3{_k}"] = (48 + 4 * _k, 4 * _i, 4, 0, 512, 3, 1)
for _i, _k in enumerate((1, 0)):
    SCATTER[f"b3{_k}"] = (48 + 4 * _k, 8 + 4 * _i, 4, 0, 512, 3, 3)
for _k in range(4):
    SCATTER[f"p3{_k}"] = (16 + 4 * _k, 16 + 4 * _k, 4, 0, 512, 3, 1)
    SCATTER[f"m3{_k}"] = (32 + 4 * _k, 32 + 4 * _k, 4, 0, 512, 3, 3)
SCATTER["a2"] = (14, 48, 2, 0, 512, 2, 1)
SCATTER["b2"] = (12, 50, 2, 0, 512, 2, 3)
SCATTER["p2"] = (4, 52, 4, 0, 512, 2, 1)
SCATTER["m2"] = (8, 56, 4, 0, 512, 2, 3)
SCATTER["a1"] = (3, 60, 1, 0, 256, 1, 1)
SCATTER["b1"] = (3, 60, 1, 256, 256, 1, 3)
SCATTER["p1"] = (1, 61, 1, 0, 512, 1, 1)
SCATTER["m1"] = (2, 62, 1, 0, 512, 1, 3)
SCATTER_ID = {name: i for i, name in enumerate(SCATTER)}


def one_hot3(value):
    second, third = lax.rem(value, 2), lax.div(value, 2)
    return 1 - second - third, second, third


def kernel(
    tok_ref, small_ref, wq_hbm, wkv_hbm, wo_hbm, wg_hbm, wu_hbm, wd_hbm,
    cosk_hbm, sink_hbm, cosq_hbm, sinq_hbm,
    out_ref,
    wq, wkv, wo, wg, wu, wd, cosk, sink, cosq, sinq,
    ag, xb, part, sb, rb, stats, kvall, att, hid, accq, acckv, accg, accu, resid,
    ag_send, ag_recv, px_send, px_recv, rs_send, rs_recv, st_send, st_recv,
    kv_send, kv_recv, kf_send, kf_recv, at_send, at_recv, hd_send, hd_recv,
    wl_sem, ws_sem, wr_sem, ol_sem, os_sem, or_sem, dl_sem, ds_sem, dr_sem,
):
    gx, gy = lax.axis_index("gx"), lax.axis_index("gy")
    x, y_lo = lax.rem(gx, 4), lax.div(gx, 4)
    core, z, y_hi = lax.rem(gy, 2), lax.rem(lax.div(gy, 2), 4), lax.div(gy, 8)
    y = y_hi * 2 + y_lo
    chip = y_hi * 4 + z
    partner = (gx, gy + 1 - 2 * core)

    def device(x, y, z):
        return (lax.rem(y, 2) * 4 + x, lax.div(y, 2) * 8 + z * 2 + core)

    def turn(v):
        group, item = lax.div(v, 2), lax.rem(v, 2)
        return (1 - group) * core * (1 + item) + group * (1 + item - core)

    def toward(v, level, sign):
        e0, e1, e2 = one_hot3(lax.rem(turn(v) + 3 - level, 3))
        return device(lax.rem(x + sign * e0, 4), lax.rem(y + sign * e1, 4), lax.rem(z + sign * e2, 4))

    def slot(position, mine):
        d = lax.rem(position - mine + 4, 4)
        return d + lax.div(d, 2) - 2 * lax.div(d, 3)

    def place(rotation, px, py, pz):
        e0, e1, e2 = one_hot3(rotation)
        return (
            (16 * e0 + e1 + 4 * e2) * slot(px, x)
            + (4 * e0 + 16 * e1 + e2) * slot(py, y)
            + (e0 + 4 * e1 + 16 * e2) * slot(pz, z)
        )

    def remote(src, dst, send, recv, target):
        return pltpu.make_async_remote_copy(
            src_ref=src, dst_ref=dst, send_sem=send, recv_sem=recv, device_id=target, device_id_type=MESH
        )

    barrier = pltpu.get_barrier_semaphore()
    greeted = [
        device(lax.rem(x + 1, 4), y, z), device(lax.rem(x + 3, 4), y, z),
        device(x, lax.rem(y + 1, 4), z), device(x, lax.rem(y + 3, 4), z),
    ] + [(gx, lax.rem(gy + d, 16)) for d in range(1, 16)]
    for target in greeted:
        pl.semaphore_signal(barrier, inc=1, device_id=target, device_id_type=MESH)

    whole = ((wq_hbm, wq), (wkv_hbm, wkv), (wg_hbm, wg), (wu_hbm, wu))
    tables = ((cosk_hbm, cosk), (sink_hbm, sink), (cosq_hbm, cosq), (sinq_hbm, sinq))
    local_copies = [
        pltpu.make_async_copy(src, dst.at[core], wl_sem.at[i]) for i, (src, dst) in enumerate(whole)
    ]
    table_copies = [
        pltpu.make_async_copy(src, dst, wl_sem.at[4 + i]) for i, (src, dst) in enumerate(tables)
    ]
    remote_copies = [
        remote(src, dst.at[core], ws_sem.at[i], wr_sem.at[i], partner) for i, (src, dst) in enumerate(whole)
    ]
    columns = lambda f, side: pl.ds(pl.multiple_of((2 * f + side) * BLOCK, BLOCK), BLOCK)
    out_local = [pltpu.make_async_copy(wo_hbm.at[:, columns(f, core)], wo.at[core, f], ol_sem.at[f]) for f in range(8)]
    down_local = [pltpu.make_async_copy(wd_hbm.at[:, columns(f, core)], wd.at[core, f], dl_sem.at[f]) for f in range(8)]
    out_remote = [remote(wo_hbm.at[:, columns(f, 1 - core)], wo.at[core, f], os_sem.at[f], or_sem.at[f], partner) for f in range(8)]
    down_remote = [remote(wd_hbm.at[:, columns(f, 1 - core)], wd.at[core, f], ds_sem.at[f], dr_sem.at[f], partner) for f in range(8)]
    for copy in local_copies[:2] + table_copies + out_local + local_copies[2:] + down_local:
        copy.start()

    def column_sums(squares):
        folded = squares[:, :128] + squares[:, 128:256] + squares[:, 256:384] + squares[:, 384:]
        return jnp.sum(jnp.transpose(folded), axis=0, keepdims=True)

    def share_stats(phase, values, extra):
        squares = column_sums(values * values)
        row = lax.broadcasted_iota(jnp.int32, (8, 128), 0)
        wide = jnp.concatenate([squares, jnp.zeros((1, 64), F32)], axis=1)
        tile = jnp.where(row == 0, wide, jnp.zeros((8, 128), F32))
        if extra is not None:
            tile = jnp.where(row == 1, extra, tile)
        stats[phase, 0] = tile

    def stat_copy(phase, d):
        return remote(
            stats.at[phase, 0], stats.at[phase, d], st_send.at[phase, d], st_recv.at[phase, d],
            (gx, lax.rem(gy + d, 16)),
        )

    def inverse_root(phase):
        total = jnp.sum(jnp.sum(stats[phase], axis=0), axis=0, keepdims=True) if False else None
        row = lax.broadcasted_iota(jnp.int32, (8, 128), 0)
        summed = jnp.sum(stats[phase], axis=0)
        total = jnp.sum(jnp.where(row == 0, summed, 0.0), axis=0, keepdims=True)[:, :64]
        inverse = lax.rsqrt(total / MODEL + EPSILON)
        tall = jnp.transpose(jnp.broadcast_to(inverse, (128, 64)))
        return jnp.concatenate([tall] * 4, axis=1)

    def normalize_into_gather(phase, values, gain):
        scaled = (values * inverse_root(phase) * gain).astype(BF)
        for u in range(4):
            ag[lax.rem(u + 2 * core, 4), 0] = scaled[16 * u : 16 * u + 16]

    def gather_copy(name, v):
        src, dst, count, col, width, level, sign = GATHER[name]
        i = GATHER_ID[name]
        if width == 512:
            a, b = ag.at[v, pl.ds(src, count)], ag.at[v, pl.ds(dst, count)]
        else:
            a, b = ag.at[v, src, :, pl.ds(col, width)], ag.at[v, dst, :, pl.ds(col, width)]
        return remote(a, b, ag_send.at[v, i], ag_recv.at[v, i], toward(v, level, sign))

    def px_copy(j, k):
        return remote(
            ag.at[2 + j, pl.ds(16 * k, 16)], xb.at[j, pl.ds(16 * k, 16)], px_send.at[j, k], px_recv.at[j, k], partner
        )

    def units(body, first=0, last=4):
        @pl.loop(first, last)
        def _(v):
            body(v)

    def gather():
        start = lambda v, *names: [gather_copy(n, v).start() for n in names]
        arrive = lambda v, *names: [gather_copy(n, v).wait_recv() for n in names]

        def t0(v):
            start(v, "s1p", "s1m", "o2p", "o2m", "o3p", "o3m")

        def t1(v):
            arrive(v, "s1m")
            start(v, "f1m")
            arrive(v, "s1p")
            start(v, "f1p")

        def t2(v):
            arrive(v, "f1m", "f1p")
            start(v, "r2p", "r2m", "r3p", "r3m")

        def t3(v):
            arrive(v, "o2m", "r2m")
            start(v, "f2m", "g3p1", "g3m1")
            arrive(v, "o2p", "r2p")
            start(v, "f2p", "g3p2", "g3m2")

        def t4(v):
            arrive(v, "o3m", "r3m")
            start(v, "f3m0")

        def t5(v):
            arrive(v, "f2m", "f2p")
            start(v, "g3p3", "g3m3")

        def t6(v):
            arrive(v, "g3m1")
            start(v, "f3m1")
            arrive(v, "o3p", "r3p", "g3p1", "g3p2")
            start(v, "f3p2")

        def t7(v):
            arrive(v, "g3p3")
            start(v, "f3p3")
            arrive(v, "g3m2", "g3m3")

        def t8(v):
            arrive(v, "f3m0", "f3m1", "f3p2", "f3p3")

        for step in (t0, t1, t2, t3, t4, t5):
            units(step)
        for j in range(2):
            px_copy(j, 0).start()
        units(t6)
        units(t7, 2, 4)
        for j in range(2):
            px_copy(j, 1).start()
            px_copy(j, 2).start()
        units(t7, 0, 2)
        units(t8, 2, 4)
        for j in range(2):
            px_copy(j, 3).start()
        units(t8, 0, 2)
        for j in range(2):
            for k in range(4):
                px_copy(j, k).wait_recv()

    def gather_drain():
        units(lambda v: [gather_copy(n, v).wait_send() for n in GATHER])
        for j in range(2):
            for k in range(4):
                px_copy(j, k).wait_send()

    def gathered(f, mine):
        fy, fz = lax.div(f, 4), lax.rem(f, 4)
        pieces = []
        for j in range(2):
            rotation = turn(j) if mine else j + core
            for ty in range(2):
                for tx in range(4):
                    at = place(rotation, tx, fy * 2 + ty, fz)
                    pieces.append(ag[j, at] if mine else xb[j, at])
        return jnp.concatenate(pieces, axis=0)

    def feature_columns(f, mine):
        return columns(f, core if mine else 1 - core)

    def scatter_copy(name, v):
        src, dst, count, col, width, level, sign = SCATTER[name]
        i = SCATTER_ID[name]
        if width == 512:
            a, b = sb.at[v, pl.ds(src, count)], rb.at[v, pl.ds(dst, count)]
        else:
            a, b = sb.at[v, src, :, pl.ds(col, width)], rb.at[v, dst, :, pl.ds(col, width)]
        return remote(a, b, rs_send.at[v, i], rs_recv.at[v, i], toward(v, level, sign))

    def rs_start(v, *names):
        for n in names:
            scatter_copy(n, v).start()

    def rs_arrive(v, *names):
        for n in names:
            scatter_copy(n, v).wait_recv()

    def cast(v, src, count=4):
        sb[v, pl.ds(src, count)] = part[v, pl.ds(src, count)].astype(BF)

    def cast_sum(v, src, place_at, count=4):
        sb[v, pl.ds(src, count)] = (
            part[v, pl.ds(src, count)] + rb[v, pl.ds(place_at, count)].astype(F32)
        ).astype(BF)

    def scatter_first(v):
        for k in (3, 2):
            cast(v, 48 + 4 * k)
            rs_start(v, f"a3{k}")
        for k in (1, 0):
            cast(v, 48 + 4 * k)
            rs_start(v, f"b3{k}")
        for k in (3, 2):
            cast(v, 32 + 4 * k)
            rs_start(v, f"m3{k}")

    def scatter_rest():
        def s1(v):
            for k in (3, 2):
                rs_arrive(v, f"a3{k}")
                cast_sum(v, 16 + 4 * k, 4 * (3 - k))
                rs_start(v, f"p3{k}")
            for k in (1, 0):
                cast(v, 16 + 4 * k)
                rs_start(v, f"p3{k}")
                rs_arrive(v, f"b3{k}")
                cast_sum(v, 32 + 4 * k, 8 + 4 * (1 - k))
                rs_start(v, f"m3{k}")

        def total3(v, k):
            rs_arrive(v, f"m3{k}", f"p3{k}")
            return (
                part[v, pl.ds(4 * k, 4)]
                + rb[v, pl.ds(16 + 4 * k, 4)].astype(F32)
                + rb[v, pl.ds(32 + 4 * k, 4)].astype(F32)
            )

        def s2(v):
            sb[v, pl.ds(12, 4)] = total3(v, 3).astype(BF)
            rs_start(v, "a2", "b2")

        def s3(v):
            total = total3(v, 2)
            rs_arrive(v, "b2")
            sb[v, pl.ds(8, 2)] = (total[:2] + rb[v, pl.ds(50, 2)].astype(F32)).astype(BF)
            sb[v, pl.ds(10, 2)] = total[2:].astype(BF)
            rs_start(v, "m2")
            total = total3(v, 1)
            rs_arrive(v, "a2")
            sb[v, pl.ds(6, 2)] = (total[2:] + rb[v, pl.ds(48, 2)].astype(F32)).astype(BF)
            sb[v, pl.ds(4, 2)] = total[:2].astype(BF)
            rs_start(v, "p2")

        def s4(v):
            total = total3(v, 0)
            rs_arrive(v, "m2", "p2")
            total = total + rb[v, pl.ds(52, 4)].astype(F32) + rb[v, pl.ds(56, 4)].astype(F32)
            part[v, pl.ds(0, 4)] = total
            sb[v, 3] = total[3].astype(BF)
            rs_start(v, "a1", "b1")

        def s5(v):
            sb[v, 1, :, 256:] = part[v, 1, :, 256:].astype(BF)
            rs_arrive(v, "a1")
            sb[v, 1, :, :256] = (part[v, 1, :, :256] + rb[v, 60, :, :256].astype(F32)).astype(BF)
            rs_start(v, "p1")
            sb[v, 2, :, :256] = part[v, 2, :, :256].astype(BF)
            rs_arrive(v, "b1")
            sb[v, 2, :, 256:] = (part[v, 2, :, 256:] + rb[v, 60, :, 256:].astype(F32)).astype(BF)
            rs_start(v, "m1")

        def s6(v):
            rs_arrive(v, "m1", "p1")
            part[v, 0] = part[v, 0] + rb[v, 61].astype(F32) + rb[v, 62].astype(F32)

        for step in (s1, s2, s3, s4, s5, s6):
            units(step)
        units(lambda v: [scatter_copy(n, v).wait_send() for n in SCATTER])

    def scattered():
        return jnp.concatenate([part[lax.rem(u + 2 * core, 4), 0] for u in range(4)], axis=0)

    def spread(pair, f, product):
        fy, fz = lax.div(f, 4), lax.rem(f, 4)
        for j in range(2):
            for ty in range(2):
                for tx in range(4):
                    at = place(turn(2 * pair + j), tx, fy * 2 + ty, fz)
                    row = 128 * j + 64 * ty + 16 * tx
                    part[2 * pair + j, at] = product[row : row + 16]

    tokens = tok_ref[...].astype(F32)
    share_stats(0, tokens, small_ref[:, 2176:2304])
    pl.semaphore_wait(barrier, len(greeted))
    for d in range(1, 16):
        stat_copy(0, d).start()
    for copy in remote_copies[:2]:
        copy.start()
    for d in range(1, 16):
        stat_copy(0, d).wait_recv()
    normalize_into_gather(0, tokens, small_ref[:, :512])
    documents = jnp.sum(
        jnp.where(lax.broadcasted_iota(jnp.int32, (16, 8, 128), 1) == 1, stats[0], 0.0), axis=1
    )
    for copy in out_remote + remote_copies[2:] + down_remote:
        copy.start()
    for copy in local_copies[:2] + table_copies:
        copy.wait()
    for copy in remote_copies[:2]:
        copy.wait_recv()
    gather()

    acckv[...] = jnp.zeros_like(acckv)

    @pl.loop(0, 8)
    def _(f):
        for mine in (True, False):
            cols = feature_columns(f, mine)
            weights = jnp.concatenate([wkv[0, :, cols], wkv[1, :, cols]], axis=0)
            acckv[...] += dot_nt(weights, gathered(f, mine))

    kv_sum = acckv[...]
    kvall[core, chip] = jnp.concatenate([kv_sum[0:8], kv_sum[16:24], kv_sum[8:16], kv_sum[24:32]], axis=0)

    def kv_copy(d):
        there = lax.rem(gy + 2 * d, 16)
        return remote(kvall.at[core, chip], kvall.at[core, chip], kv_send.at[d], kv_recv.at[d], (gx, there))

    def kv_arrival(d):
        source = lax.rem(chip + 8 - d, 8)
        return remote(kvall.at[core, source], kvall.at[core, source], kv_send.at[d], kv_recv.at[d], partner)

    for d in range(1, 8):
        kv_copy(d).start()

    accq[...] = jnp.zeros_like(accq)

    @pl.loop(0, 8)
    def _(f):
        for mine in (True, False):
            cols = feature_columns(f, mine)
            weights = jnp.concatenate([wq[0, :, cols], wq[1, :, cols]], axis=0)
            accq[...] += dot_nt(gathered(f, mine), weights)

    bias_at = pl.ds(pl.multiple_of(1024 + 128 * chip, 128), 128)
    query = accq[...] + small_ref[:, bias_at]
    own_rows = pl.ds(pl.multiple_of(256 * core, 256), 256)
    turned = jnp.concatenate([query[:, 64:], query[:, :64]], axis=1)
    queries = (query * cosq[own_rows, :] + turned * sinq[own_rows, :]).astype(BF)

    for d in range(1, 8):
        kv_arrival(d).wait_recv()
    forward = remote(kvall.at[core], kvall.at[core], kf_send, kf_recv, partner)
    forward.start()

    def token_parts(index, own_core):
        item, low, along, row = (
            (index >> 7) & 1, (index >> 6) & 1, (index >> 4) & 3, index & 15,
        )
        return 256 * low + 64 * along + 32 * own_core + 16 * item + row, 8 * low + 2 * along + own_core, 16 * item + row

    def owner(index):
        held = gy - index
        return jnp.where(held < 0, held + 16, held)

    docs = documents.astype(BF)
    key_index = lax.broadcasted_iota(jnp.int32, (128, 512), 1)
    _, _, key_lane = token_parts(key_index, key_index >> 8)
    pick = jnp.where(lax.broadcasted_iota(jnp.int32, (128, 512), 0) == key_lane, 1.0, 0.0).astype(BF)
    key_docs = dot_nn(docs, pick)
    key_index = lax.broadcasted_iota(jnp.int32, (16, 512), 1)
    _, key_owner, _ = token_parts(key_index, key_index >> 8)
    is_owner = owner(lax.broadcasted_iota(jnp.int32, (16, 512), 0)) == key_owner
    key_docs = jnp.sum(jnp.where(is_owner, key_docs, 0.0), axis=0, keepdims=True)
    query_index = lax.broadcasted_iota(jnp.int32, (256, 128), 0)
    _, _, query_lane = token_parts(query_index, core)
    pick = jnp.where(lax.broadcasted_iota(jnp.int32, (256, 128), 1) == query_lane, 1.0, 0.0).astype(BF)
    query_docs = dot_nt(pick, docs)
    query_index = lax.broadcasted_iota(jnp.int32, (256, 16), 0)
    _, query_owner, _ = token_parts(query_index, core)
    is_owner = owner(lax.broadcasted_iota(jnp.int32, (256, 16), 1)) == query_owner
    query_docs = jnp.sum(jnp.where(is_owner, query_docs, 0.0), axis=1, keepdims=True)
    key_index = lax.broadcasted_iota(jnp.int32, (256, 512), 1)
    key_position, _, _ = token_parts(key_index, key_index >> 8)
    query_position, _, _ = token_parts(lax.broadcasted_iota(jnp.int32, (256, 512), 0), core)
    allowed = (key_position <= query_position) & (key_docs == query_docs)

    value_bias = jnp.transpose(jnp.broadcast_to(small_ref[:, 2048:2176], (128, 128)))
    value_bias = jnp.concatenate([value_bias] * 2, axis=1)
    remote(kvall.at[1 - core], kvall.at[1 - core], kf_send, kf_recv, partner).wait_recv()
    key_parts, value_parts = [], []
    for side in range(2):
        held = kvall[side]
        keys = held[:, :16].reshape(128, 256)
        first, second = keys[:64], keys[64:]
        cosine, sine = cosk[:, 256 * side : 256 * side + 256], sink[:, 256 * side : 256 * side + 256]
        key_parts.append(
            jnp.concatenate([first * cosine - second * sine, second * cosine + first * sine], axis=0).astype(BF)
        )
        value_parts.append((held[:, 16:].reshape(128, 256) + value_bias).astype(BF))
    keys = jnp.concatenate(key_parts, axis=1)
    values = jnp.concatenate(value_parts, axis=1)
    scores = dot_nn(queries, keys) / math.sqrt(HEAD_DIM)
    scores = jnp.where(allowed, scores, -jnp.inf)
    weights = jnp.where(allowed, jnp.exp(scores - jnp.max(scores, axis=1, keepdims=True)), 0.0)
    denominator = jnp.sum(weights, axis=1, keepdims=True)
    att[0] = (dot_nt(weights.astype(BF), values) / denominator).astype(BF)
    send_att = remote(att.at[0], att.at[1], at_send, at_recv, partner)
    send_att.start()

    for copy in out_local:
        copy.wait()
    for copy in out_remote:
        copy.wait_recv()
    for pair in range(2):
        if pair == 1:
            send_att.wait_recv()

        @pl.loop(0, 8)
        def _(f):
            weights = jnp.concatenate([wo[0, f], wo[1, f]], axis=0)
            spread(pair, f, dot_nn(att[pair], weights))

        units(scatter_first, 2 * pair, 2 * pair + 2)
    gather_drain()
    scatter_rest()

    resid[...] = (tok_ref[...].astype(F32) + scattered()).astype(BF)

    values = resid[...].astype(F32)
    share_stats(1, values, None)
    for d in range(1, 16):
        stat_copy(1, d).start()
    for copy in local_copies[2:]:
        copy.wait()
    for copy in remote_copies[2:]:
        copy.wait_recv()
    for d in range(1, 16):
        stat_copy(1, d).wait_recv()
    normalize_into_gather(1, values, small_ref[:, 512:1024])
    gather()

    accg[...] = jnp.zeros_like(accg)
    accu[...] = jnp.zeros_like(accu)

    @pl.loop(0, 8)
    def _(f):
        for mine in (True, False):
            cols = feature_columns(f, mine)
            block = gathered(f, mine)
            for side in range(2):
                accg[side] += dot_nt(block, wg[side, :, cols])
                accu[side] += dot_nt(block, wu[side, :, cols])

    for side in range(2):
        gate = accg[side]
        hid[0, side] = (gate / (1.0 + jnp.exp(-gate)) * accu[side]).astype(BF)
    send_hid = remote(hid.at[0], hid.at[1], hd_send, hd_recv, partner)
    send_hid.start()
    for copy in down_local:
        copy.wait()
    for copy in down_remote:
        copy.wait_recv()
    for pair in range(2):
        if pair == 1:
            send_hid.wait_recv()

        @pl.loop(0, 8)
        def _(f):
            product = dot_nn(hid[pair, 0], wd[0, f]) + dot_nn(hid[pair, 1], wd[1, f])
            spread(pair, f, product)

        units(scatter_first, 2 * pair, 2 * pair + 2)
    gather_drain()
    scatter_rest()
    out_ref[...] = (resid[...].astype(F32) + scattered()).astype(BF)

    for d in range(1, 16):
        stat_copy(0, d).wait_send()
        stat_copy(1, d).wait_send()
    for d in range(1, 8):
        kv_copy(d).wait_send()
    forward.wait_send()
    send_att.wait_send()
    send_hid.wait_send()
    for copy in remote_copies + out_remote + down_remote:
        copy.wait_send()


def rotary_tables():
    half = HEAD_DIM // 2
    frequency = np.power(np.float32(ROTARY_BASE), -(np.arange(half, dtype=np.float32) * 2.0) / HEAD_DIM).astype(np.float32)
    index = np.arange(TOKENS)
    side, item, low, along, row = index >> 8, (index >> 7) & 1, (index >> 6) & 1, (index >> 4) & 3, index & 15
    position = 256 * low + 64 * along + 32 * side + 16 * item + row
    angles = (position.astype(np.float32)[:, None] * frequency[None, :]).astype(np.float32)
    cosine, sine = np.cos(angles).astype(np.float32), np.sin(angles).astype(np.float32)
    return (
        np.ascontiguousarray(cosine.T), np.ascontiguousarray(sine.T),
        np.concatenate([cosine, cosine], axis=1), np.concatenate([-sine, sine], axis=1),
    )


def shards(
    tokens, segment_ids, attn_gain, query_weight, query_bias, key_weight, value_weight, value_bias,
    out_weight, ffn_gain, gate_weight, up_weight, down_weight,
):
    small = jnp.concatenate(
        [
            attn_gain.astype(F32), ffn_gain.astype(F32), query_bias.astype(F32), value_bias.astype(F32),
            segment_ids.astype(F32), jnp.zeros((96,), F32),
        ]
    )[None, :]
    kv_weight = jnp.concatenate([key_weight, value_weight], axis=0)
    units = gate_weight.shape[0]
    any_spec = pl.BlockSpec(memory_space=pl.ANY)
    vmem_spec = pl.BlockSpec(memory_space=pltpu.VMEM)
    dma = pltpu.SemaphoreType.DMA
    gathers, scatters = len(GATHER), len(SCATTER)
    return pl.pallas_call(
        kernel,
        out_shape=jax.ShapeDtypeStruct((64, BLOCK), BF),
        in_specs=[vmem_spec] * 2 + [any_spec] * 10,
        out_specs=vmem_spec,
        scratch_shapes=[
            pltpu.VMEM((2, 64, MODEL), BF),
            pltpu.VMEM((2, 16, MODEL), BF),
            pltpu.VMEM((2, 8, 64, BLOCK), BF),
            pltpu.VMEM((2, units, MODEL), BF),
            pltpu.VMEM((2, units, MODEL), BF),
            pltpu.VMEM((2, 8, units, BLOCK), BF),
            pltpu.VMEM((64, 512), F32),
            pltpu.VMEM((64, 512), F32),
            pltpu.VMEM((512, 128), F32),
            pltpu.VMEM((512, 128), F32),
            pltpu.VMEM((4, 64, ROWS, BLOCK), BF),
            pltpu.VMEM((2, 64, ROWS, BLOCK), BF),
            pltpu.VMEM((4, 64, ROWS, BLOCK), F32),
            pltpu.VMEM((4, 64, ROWS, BLOCK), BF),
            pltpu.VMEM((4, 63, ROWS, BLOCK), BF),
            pltpu.VMEM((2, 16, 8, 128), F32),
            pltpu.VMEM((2, 8, 32, 256), F32),
            pltpu.VMEM((2, 256, 128), BF),
            pltpu.VMEM((2, 2, 256, units), BF),
            pltpu.VMEM((256, 128), F32),
            pltpu.VMEM((32, 256), F32),
            pltpu.VMEM((2, 256, units), F32),
            pltpu.VMEM((2, 256, units), F32),
            pltpu.VMEM((64, BLOCK), BF),
            dma((4, gathers)), dma((4, gathers)),
            dma((2, 4)), dma((2, 4)),
            dma((4, scatters)), dma((4, scatters)),
            dma((2, 16)), dma((2, 16)),
            dma((8,)), dma((8,)),
            dma, dma, dma, dma, dma, dma,
            dma((8,)), dma((4,)), dma((4,)),
            dma((8,)), dma((8,)), dma((8,)),
            dma((8,)), dma((8,)), dma((8,)),
        ],
        compiler_params=pltpu.CompilerParams(
            collective_id=0, has_side_effects=True, vmem_limit_bytes=60 * 1024 * 1024
        ),
        name="layer",
    )(
        tokens, small, query_weight, kv_weight, out_weight, gate_weight, up_weight, down_weight, *rotary_tables()
    )


def solution(mesh):
    placed = (
        P("gx", "gy"),
        P("gy"),
        P("gy"),
        P(("gx", "gy"), None),
        P("gx"),
        P(("gx", "gy"), None),
        P(("gx", "gy"), None),
        P("gx"),
        P(("gx", "gy"), None),
        P("gy"),
        P(("gx", "gy"), None),
        P(("gx", "gy"), None),
        P(("gx", "gy"), None),
    )
    return jax.shard_map(
        shards, mesh=mesh, in_specs=placed, out_specs=P("gx", "gy"), check_vma=False
    )
```

```python
import functools
import math

import jax
import jax.numpy as jnp
import numpy as np
from jax import lax
from jax.experimental import pallas as pl
from jax.experimental.pallas import tpu as pltpu
from jax.sharding import PartitionSpec as P


HEAD_DIM = 128
EPSILON = 1e-06
ROTARY_BASE = 1000000.0
TOKENS = 512
MODEL = 8192
BLOCK = 512
ROWS = 16
BF = jnp.bfloat16
F32 = jnp.float32
MESH = pl.DeviceIdType.MESH


def dot_nt(left, right):
    return lax.dot_general(left, right, (((1,), (1,)), ((), ())), preferred_element_type=F32)


def dot_nn(left, right):
    return lax.dot_general(left, right, (((1,), (0,)), ((), ())), preferred_element_type=F32)


GATHER = {
    "s1p": (0, 2, 1, 0, 512, 1, 1),
    "s1m": (0, 1, 1, 0, 512, 1, 3),
    "f1m": (1, 3, 1, 0, 256, 1, 3),
    "f1p": (2, 3, 1, 256, 256, 1, 1),
    "o2p": (0, 8, 1, 0, 512, 2, 1),
    "o2m": (0, 4, 1, 0, 512, 2, 3),
    "r2p": (1, 9, 3, 0, 512, 2, 1),
    "r2m": (1, 5, 3, 0, 512, 2, 3),
    "f2m": (4, 12, 2, 0, 512, 2, 3),
    "f2p": (10, 14, 2, 0, 512, 2, 1),
    "o3p": (0, 32, 1, 0, 512, 3, 1),
    "o3m": (0, 16, 1, 0, 512, 3, 3),
    "r3p": (1, 33, 3, 0, 512, 3, 1),
    "r3m": (1, 17, 3, 0, 512, 3, 3),
    "f3m0": (16, 48, 4, 0, 512, 3, 3),
    "f3m1": (20, 52, 4, 0, 512, 3, 3),
    "f3p2": (40, 56, 4, 0, 512, 3, 1),
    "f3p3": (44, 60, 4, 0, 512, 3, 1),
}
for _k in (1, 2, 3):
    GATHER[f"g3p{_k}"] = (4 * _k, 32 + 4 * _k, 4, 0, 512, 3, 1)
    GATHER[f"g3m{_k}"] = (4 * _k, 16 + 4 * _k, 4, 0, 512, 3, 3)
GATHER_ID = {name: i for i, name in enumerate(GATHER)}

SCATTER = {}
for _i, _k in enumerate((3, 2)):
    SCATTER[f"a3{_k}"] = (48 + 4 * _k, 4 * _i, 4, 0, 512, 3, 1)
for _i, _k in enumerate((1, 0)):
    SCATTER[f"b3{_k}"] = (48 + 4 * _k, 8 + 4 * _i, 4, 0, 512, 3, 3)
for _k in range(4):
    SCATTER[f"p3{_k}"] = (16 + 4 * _k, 16 + 4 * _k, 4, 0, 512, 3, 1)
    SCATTER[f"m3{_k}"] = (32 + 4 * _k, 32 + 4 * _k, 4, 0, 512, 3, 3)
SCATTER["a2"] = (14, 48, 2, 0, 512, 2, 1)
SCATTER["b2"] = (12, 50, 2, 0, 512, 2, 3)
SCATTER["p2"] = (4, 52, 4, 0, 512, 2, 1)
SCATTER["m2"] = (8, 56, 4, 0, 512, 2, 3)
SCATTER["a1"] = (3, 60, 1, 0, 256, 1, 1)
SCATTER["b1"] = (3, 60, 1, 256, 256, 1, 3)
SCATTER["p1"] = (1, 61, 1, 0, 512, 1, 1)
SCATTER["m1"] = (2, 62, 1, 0, 512, 1, 3)
SCATTER_ID = {name: i for i, name in enumerate(SCATTER)}


def one_hot3(value):
    second, third = lax.rem(value, 2), lax.div(value, 2)
    return 1 - second - third, second, third


def kernel(
    tok_ref, small_ref, wq_hbm, wkv_hbm, wo_hbm, wg_hbm, wu_hbm, wd_hbm,
    cosk_hbm, sink_hbm, cosq_hbm, sinq_hbm,
    out_ref,
    wq, wkv, wo, wg, wu, wd, cosk, sink, cosq, sinq,
    ag, xb, an, part, sb, rb, stats, sums, roots, tall, scale, kvall, att, hid, accq, acckv, accg, accu, resid,
    ag_send, ag_recv, px_send, px_recv, rs_send, rs_recv, st_send, st_recv, su_send, su_recv, ro_send, ro_recv,
    kv_send, kv_recv, kf_send, kf_recv, at_send, at_recv, hd_send, hd_recv,
    wl_sem, ws_sem, wr_sem, ol_sem, os_sem, or_sem, dl_sem, ds_sem, dr_sem,
):
    gx, gy = lax.axis_index("gx"), lax.axis_index("gy")
    x, y_lo = lax.rem(gx, 4), lax.div(gx, 4)
    core, z, y_hi = lax.rem(gy, 2), lax.rem(lax.div(gy, 2), 4), lax.div(gy, 8)
    y = y_hi * 2 + y_lo
    chip = y_hi * 4 + z
    partner = (gx, gy + 1 - 2 * core)

    def device(x, y, z):
        return (lax.rem(y, 2) * 4 + x, lax.div(y, 2) * 8 + z * 2 + core)

    def turn(v):
        group, item = lax.div(v, 2), lax.rem(v, 2)
        return (1 - group) * core * (1 + item) + group * (1 + item - core)

    def neighbour(v, level, sign):
        e0, e1, e2 = one_hot3(lax.rem(turn(v) + 3 - level, 3))
        return device(lax.rem(x + sign * e0, 4), lax.rem(y + sign * e1, 4), lax.rem(z + sign * e2, 4))

    neighbours = {
        (v, level, sign): neighbour(v, level, sign) for v in range(4) for level in (1, 2, 3) for sign in (1, 3)
    }

    def toward(v, level, sign):
        return neighbours[v, level, sign]

    def slot(position, mine):
        d = lax.rem(position - mine + 4, 4)
        return d + lax.div(d, 2) - 2 * lax.div(d, 3)

    def strides(rotation):
        e0, e1, e2 = one_hot3(rotation)
        return 16 * e0 + e1 + 4 * e2, 4 * e0 + 16 * e1 + e2, e0 + 4 * e1 + 16 * e2

    x_slots = [slot(position, x) for position in range(4)]
    unit_strides = [strides(turn(v)) for v in range(4)]
    other_strides = [strides(j + core) for j in range(2)]

    def places(stride, f):
        fy, fz = lax.div(f, 4), lax.rem(f, 4)
        z_part = stride[2] * slot(fz, z)
        y_parts = [stride[1] * slot(fy * 2 + ty, y) + z_part for ty in range(2)]
        return [y_parts[ty] + stride[0] * x_slots[tx] for ty in range(2) for tx in range(4)]

    def remote(src, dst, send, recv, target):
        return pltpu.make_async_remote_copy(
            src_ref=src, dst_ref=dst, send_sem=send, recv_sem=recv, device_id=target, device_id_type=MESH
        )

    barrier = pltpu.get_barrier_semaphore()
    greeted = (
        [device(x, lax.rem(y + 3 + 2 * y_lo, 4), z)]
        + [(lax.rem(gx + e, 8), gy) for e in range(1, 8)]
        + [(gx, lax.rem(gy + d, 16)) for d in range(1, 16)]
    )
    for target in greeted:
        pl.semaphore_signal(barrier, inc=1, device_id=target, device_id_type=MESH)

    whole = ((wq_hbm, wq), (wkv_hbm, wkv), (wg_hbm, wg), (wu_hbm, wu))
    tables = ((cosk_hbm, cosk), (sink_hbm, sink), (cosq_hbm, cosq), (sinq_hbm, sinq))
    local_copies = [
        pltpu.make_async_copy(src, dst.at[core], wl_sem.at[i]) for i, (src, dst) in enumerate(whole)
    ]
    table_copies = [
        pltpu.make_async_copy(src, dst, wl_sem.at[4 + i]) for i, (src, dst) in enumerate(tables)
    ]
    remote_copies = [
        remote(src, dst.at[core], ws_sem.at[i], wr_sem.at[i], partner) for i, (src, dst) in enumerate(whole)
    ]
    columns = lambda f, side: pl.ds(pl.multiple_of((2 * f + side) * BLOCK, BLOCK), BLOCK)
    out_local = [pltpu.make_async_copy(wo_hbm.at[:, columns(f, core)], wo.at[core, f], ol_sem.at[f]) for f in range(8)]
    down_local = [pltpu.make_async_copy(wd_hbm.at[:, columns(f, core)], wd.at[core, f], dl_sem.at[f]) for f in range(8)]
    out_remote = [remote(wo_hbm.at[:, columns(f, 1 - core)], wo.at[core, f], os_sem.at[f], or_sem.at[f], partner) for f in range(8)]
    down_remote = [remote(wd_hbm.at[:, columns(f, 1 - core)], wd.at[core, f], ds_sem.at[f], dr_sem.at[f], partner) for f in range(8)]
    for copy in local_copies[:2] + table_copies + out_local + local_copies[2:] + down_local:
        copy.start()

    def token_unit(v):
        return pl.ds(pl.multiple_of(16 * lax.rem(v + 2 * core, 4), 16), 16)

    def square_row(values):
        squares = values * values
        folded = squares[:, :128] + squares[:, 128:256] + squares[:, 256:384] + squares[:, 384:]
        row = jnp.sum(jnp.transpose(folded), axis=0, keepdims=True)
        return jnp.concatenate([row, jnp.zeros((1, 64), F32)], axis=1)

    def stat_copy(phase, d):
        there = (gx, lax.rem(gy + d, 16))
        if phase == 0:
            return remote(stats.at[0], stats.at[d], st_send.at[d], st_recv.at[d], there)
        return remote(sums.at[0], sums.at[d], su_send.at[d], su_recv.at[d], there)

    def root_copy(phase, e):
        return remote(
            roots.at[phase, 0], roots.at[phase, e], ro_send.at[phase, e], ro_recv.at[phase, e], (lax.rem(gx + e, 8), gy)
        )

    def spread_roots(phase):
        for d in range(1, 16):
            stat_copy(phase, d).wait_recv()
        summed = jnp.sum(stats[:, :8] if phase == 0 else sums[...], axis=0)
        inverse = lax.rsqrt(summed / MODEL + EPSILON)
        roots[phase, 0] = inverse
        for e in range(1, 8):
            root_copy(phase, e).start()

    def collect_roots(phase):
        for e in range(1, 8):
            root_copy(phase, e).wait_recv()
        factors = jnp.concatenate([roots[phase, e, :1] for e in range(8)], axis=0)
        tall[...] = jnp.transpose(jnp.concatenate([factors] * 16, axis=0))
        lane = lax.broadcasted_iota(jnp.int32, (16, 128), 1)
        for j in range(2):
            rows = tall[pl.ds(pl.multiple_of(32 * core + 16 * j, 16), 16), :]
            for owner_gx in range(8):
                column = jnp.sum(jnp.where(lane == lax.rem(gx + 8 - owner_gx, 8), rows, 0.0), axis=1, keepdims=True)
                scale[128 * j + 16 * owner_gx : 128 * j + 16 * owner_gx + 16] = jnp.broadcast_to(column, (16, 128))

    def normalized(f, mine, first_row):
        block = gathered(f, mine).astype(F32)
        held = lax.rem(gy + 16 - (2 * f + (core if mine else 1 - core)), 16)
        gains = stats[held, first_row : first_row + 4]
        gain = jnp.concatenate([gains[i : i + 1] for i in range(4)], axis=1)
        factor = scale[...]
        return (block * jnp.concatenate([factor] * 4, axis=1) * gain).astype(BF)

    def gather_copy(name, v):
        src, dst, count, col, width, level, sign = GATHER[name]
        i = GATHER_ID[name]
        if width == 512:
            a, b = ag.at[v, pl.ds(src, count)], ag.at[v, pl.ds(dst, count)]
        else:
            a, b = ag.at[v, src, :, pl.ds(col, width)], ag.at[v, dst, :, pl.ds(col, width)]
        return remote(a, b, ag_send.at[v, i], ag_recv.at[v, i], toward(v, level, sign))

    def px_copy(j, k):
        return remote(
            ag.at[2 + j, pl.ds(16 * k, 16)], xb.at[j, pl.ds(16 * k, 16)], px_send.at[j, k], px_recv.at[j, k], partner
        )

    def units(body, first=0, last=4):
        for v in range(first, last):
            body(v)

    def gather_begin(v):
        for name in ("s1p", "s1m", "o2p", "o2m", "o3p", "o3m"):
            gather_copy(name, v).start()

    def gather(beside):
        start = lambda v, *names: [gather_copy(n, v).start() for n in names]
        arrive = lambda v, *names: [gather_copy(n, v).wait_recv() for n in names]

        def t1(v):
            arrive(v, "s1m")
            start(v, "f1m")
            arrive(v, "s1p")
            start(v, "f1p")

        def t2(v):
            arrive(v, "f1m", "f1p")
            start(v, "r2p", "r2m", "r3p", "r3m")

        def t3(v):
            arrive(v, "o2m", "r2m")
            start(v, "f2m", "g3p1", "g3m1")
            arrive(v, "o2p", "r2p")
            start(v, "f2p", "g3p2", "g3m2")

        def t4(v):
            arrive(v, "o3m", "r3m")
            start(v, "f3m0")

        def t5(v):
            arrive(v, "f2m", "f2p")
            start(v, "g3p3", "g3m3")

        def t6(v):
            arrive(v, "g3m1")
            start(v, "f3m1")
            arrive(v, "o3p", "r3p", "g3p1", "g3p2")
            start(v, "f3p2")

        def t7(v):
            arrive(v, "g3p3")
            start(v, "f3p3")
            arrive(v, "g3m2", "g3m3")

        def t8(v):
            arrive(v, "f3m0", "f3m1", "f3p2", "f3p3")

        for i, step in enumerate((t1, t2, t3, t4, t5)):
            units(step)
            beside(i)
        for j in range(2):
            px_copy(j, 0).start()
        units(t6)
        units(t7, 2, 4)
        for j in range(2):
            px_copy(j, 1).start()
            px_copy(j, 2).start()
        units(t7, 0, 2)
        units(t8, 2, 4)
        for j in range(2):
            px_copy(j, 3).start()
        units(t8, 0, 2)
        for j in range(2):
            for k in range(4):
                px_copy(j, k).wait_recv()

    def gather_drain():
        units(lambda v: [gather_copy(n, v).wait_send() for n in GATHER])
        for j in range(2):
            for k in range(4):
                px_copy(j, k).wait_send()

    def gathered(f, mine):
        pieces = []
        for j in range(2):
            for at in places(unit_strides[j] if mine else other_strides[j], f):
                pieces.append(ag[j, at] if mine else xb[j, at])
        return jnp.concatenate(pieces, axis=0)

    def feature_columns(f, mine):
        return columns(f, core if mine else 1 - core)

    def scatter_copy(name, v):
        src, dst, count, col, width, level, sign = SCATTER[name]
        i = SCATTER_ID[name]
        if width == 512:
            a, b = sb.at[v, pl.ds(src, count)], rb.at[v, pl.ds(dst, count)]
        else:
            a, b = sb.at[v, src, :, pl.ds(col, width)], rb.at[v, dst, :, pl.ds(col, width)]
        return remote(a, b, rs_send.at[v, i], rs_recv.at[v, i], toward(v, level, sign))

    def rs_start(v, *names):
        for n in names:
            scatter_copy(n, v).start()

    def rs_arrive(v, *names):
        for n in names:
            scatter_copy(n, v).wait_recv()

    def cast(v, src, count=4):
        sb[v, pl.ds(src, count)] = part[v, pl.ds(src, count)].astype(BF)

    def cast_sum(v, src, place_at, count=4):
        sb[v, pl.ds(src, count)] = (
            part[v, pl.ds(src, count)] + rb[v, pl.ds(place_at, count)].astype(F32)
        ).astype(BF)

    def scatter_first(v):
        for k in (3, 2):
            cast(v, 48 + 4 * k)
            rs_start(v, f"a3{k}")
        for k in (1, 0):
            cast(v, 48 + 4 * k)
            rs_start(v, f"b3{k}")
        for k in (3, 2):
            cast(v, 32 + 4 * k)
            rs_start(v, f"m3{k}")

    def scatter_rest(finish):
        def s1(v):
            for k in (3, 2):
                rs_arrive(v, f"a3{k}")
                cast_sum(v, 16 + 4 * k, 4 * (3 - k))
                rs_start(v, f"p3{k}")
            for k in (1, 0):
                cast(v, 16 + 4 * k)
                rs_start(v, f"p3{k}")
                rs_arrive(v, f"b3{k}")
                cast_sum(v, 32 + 4 * k, 8 + 4 * (1 - k))
                rs_start(v, f"m3{k}")

        def total3(v, k):
            rs_arrive(v, f"m3{k}", f"p3{k}")
            return (
                part[v, pl.ds(4 * k, 4)]
                + rb[v, pl.ds(16 + 4 * k, 4)].astype(F32)
                + rb[v, pl.ds(32 + 4 * k, 4)].astype(F32)
            )

        def s2(v):
            sb[v, pl.ds(12, 4)] = total3(v, 3).astype(BF)
            rs_start(v, "a2", "b2")

        def s3(v):
            total = total3(v, 2)
            rs_arrive(v, "b2")
            sb[v, pl.ds(8, 2)] = (total[:2] + rb[v, pl.ds(50, 2)].astype(F32)).astype(BF)
            sb[v, pl.ds(10, 2)] = total[2:].astype(BF)
            rs_start(v, "m2")
            total = total3(v, 1)
            rs_arrive(v, "a2")
            sb[v, pl.ds(6, 2)] = (total[2:] + rb[v, pl.ds(48, 2)].astype(F32)).astype(BF)
            sb[v, pl.ds(4, 2)] = total[:2].astype(BF)
            rs_start(v, "p2")

        def s4(v):
            total = total3(v, 0)
            rs_arrive(v, "m2", "p2")
            total = total + rb[v, pl.ds(52, 4)].astype(F32) + rb[v, pl.ds(56, 4)].astype(F32)
            part[v, pl.ds(0, 4)] = total
            sb[v, 3] = total[3].astype(BF)
            rs_start(v, "a1", "b1")

        def s5(v):
            sb[v, 1, :, 256:] = part[v, 1, :, 256:].astype(BF)
            rs_arrive(v, "a1")
            sb[v, 1, :, :256] = (part[v, 1, :, :256] + rb[v, 60, :, :256].astype(F32)).astype(BF)
            rs_start(v, "p1")
            sb[v, 2, :, :256] = part[v, 2, :, :256].astype(BF)
            rs_arrive(v, "b1")
            sb[v, 2, :, 256:] = (part[v, 2, :, 256:] + rb[v, 60, :, 256:].astype(F32)).astype(BF)
            rs_start(v, "m1")

        def s6(v):
            rs_arrive(v, "m1", "p1")
            finish(v, part[v, 0] + rb[v, 61].astype(F32) + rb[v, 62].astype(F32))

        for step in (s1, s2, s3, s4, s5, s6):
            units(step)

    def scatter_drain():
        units(lambda v: [scatter_copy(n, v).wait_send() for n in SCATTER])

    def spread(pair, f, product):
        for j in range(2):
            v = 2 * pair + j
            for i, at in enumerate(places(unit_strides[v], f)):
                row = 128 * j + 16 * i
                part[v, at] = product[row : row + 16]

    for v in range(4):
        ag[v, 0] = tok_ref[token_unit(v), :]
    square_sums = square_row(tok_ref[...].astype(F32))
    blank = jnp.zeros((2, 128), F32)
    stats[0] = jnp.concatenate(
        [square_sums, small_ref[17:18], blank, small_ref[0:8], blank, blank], axis=0
    )
    pl.semaphore_wait(barrier, len(greeted))
    units(gather_begin)
    for d in range(1, 16):
        stat_copy(0, d).start()
    for copy in remote_copies[:2]:
        copy.start()

    def beside_first(i):
        if i == 0:
            spread_roots(0)
            for copy in out_remote + remote_copies[2:] + down_remote:
                copy.start()
        elif i == 4:
            collect_roots(0)

    gather(beside_first)
    documents = jnp.sum(
        jnp.where(lax.broadcasted_iota(jnp.int32, (16, 16, 128), 1) == 1, stats[...], 0.0), axis=1
    )
    for copy in local_copies[:2] + table_copies:
        copy.wait()
    for copy in remote_copies[:2]:
        copy.wait_recv()

    acckv[...] = jnp.zeros_like(acckv)

    @pl.loop(0, 8)
    def _(f):
        for mine in (True, False):
            cols = feature_columns(f, mine)
            weights = jnp.concatenate([wkv[0, :, cols], wkv[1, :, cols]], axis=0)
            block = normalized(f, mine, 4)
            an[2 * f + (0 if mine else 1)] = block
            acckv[...] += dot_nt(weights, block)

    kv_sum = acckv[...]
    kvall[core, chip] = jnp.concatenate([kv_sum[0:8], kv_sum[16:24], kv_sum[8:16], kv_sum[24:32]], axis=0)

    def kv_copy(d):
        there = lax.rem(gy + 2 * d, 16)
        return remote(kvall.at[core, chip], kvall.at[core, chip], kv_send.at[d], kv_recv.at[d], (gx, there))

    def kv_arrival(d):
        source = lax.rem(chip + 8 - d, 8)
        return remote(kvall.at[core, source], kvall.at[core, source], kv_send.at[d], kv_recv.at[d], partner)

    for d in range(1, 8):
        kv_copy(d).start()

    accq[...] = jnp.zeros_like(accq)

    @pl.loop(0, 8)
    def _(f):
        for mine in (True, False):
            cols = feature_columns(f, mine)
            weights = jnp.concatenate([wq[0, :, cols], wq[1, :, cols]], axis=0)
            accq[...] += dot_nt(an[2 * f + (0 if mine else 1)], weights)

    query = accq[...] + small_ref[pl.ds(8 + chip, 1), :]
    own_rows = pl.ds(pl.multiple_of(256 * core, 256), 256)
    turned = jnp.concatenate([query[:, 64:], query[:, :64]], axis=1)
    queries = (query * cosq[own_rows, :] + turned * sinq[own_rows, :]).astype(BF)

    for d in range(1, 8):
        kv_arrival(d).wait_recv()
    forward = remote(kvall.at[core], kvall.at[core], kf_send, kf_recv, partner)
    forward.start()

    def token_parts(index, own_core):
        item, low, along, row = (
            (index >> 7) & 1, (index >> 6) & 1, (index >> 4) & 3, index & 15,
        )
        return 256 * low + 64 * along + 32 * own_core + 16 * item + row, 8 * low + 2 * along + own_core, 16 * item + row

    def owner(index):
        held = gy - index
        return jnp.where(held < 0, held + 16, held)

    docs = documents.astype(BF)
    key_index = lax.broadcasted_iota(jnp.int32, (128, 512), 1)
    _, _, key_lane = token_parts(key_index, key_index >> 8)
    pick = jnp.where(lax.broadcasted_iota(jnp.int32, (128, 512), 0) == key_lane, 1.0, 0.0).astype(BF)
    key_docs = dot_nn(docs, pick)
    key_index = lax.broadcasted_iota(jnp.int32, (16, 512), 1)
    _, key_owner, _ = token_parts(key_index, key_index >> 8)
    is_owner = owner(lax.broadcasted_iota(jnp.int32, (16, 512), 0)) == key_owner
    key_docs = jnp.sum(jnp.where(is_owner, key_docs, 0.0), axis=0, keepdims=True)
    query_index = lax.broadcasted_iota(jnp.int32, (256, 128), 0)
    _, _, query_lane = token_parts(query_index, core)
    pick = jnp.where(lax.broadcasted_iota(jnp.int32, (256, 128), 1) == query_lane, 1.0, 0.0).astype(BF)
    query_docs = dot_nt(pick, docs)
    query_index = lax.broadcasted_iota(jnp.int32, (256, 16), 0)
    _, query_owner, _ = token_parts(query_index, core)
    is_owner = owner(lax.broadcasted_iota(jnp.int32, (256, 16), 1)) == query_owner
    query_docs = jnp.sum(jnp.where(is_owner, query_docs, 0.0), axis=1, keepdims=True)
    key_index = lax.broadcasted_iota(jnp.int32, (256, 512), 1)
    key_position, _, _ = token_parts(key_index, key_index >> 8)
    query_position, _, _ = token_parts(lax.broadcasted_iota(jnp.int32, (256, 512), 0), core)
    allowed = (key_position <= query_position) & (key_docs == query_docs)

    value_bias = jnp.transpose(jnp.broadcast_to(small_ref[16:17], (128, 128)))
    value_bias = jnp.concatenate([value_bias] * 2, axis=1)
    remote(kvall.at[1 - core], kvall.at[1 - core], kf_send, kf_recv, partner).wait_recv()
    key_parts, value_parts = [], []
    for side in range(2):
        held = kvall[side]
        keys = held[:, :16].reshape(128, 256)
        first, second = keys[:64], keys[64:]
        cosine, sine = cosk[:, 256 * side : 256 * side + 256], sink[:, 256 * side : 256 * side + 256]
        key_parts.append(
            jnp.concatenate([first * cosine - second * sine, second * cosine + first * sine], axis=0).astype(BF)
        )
        value_parts.append((held[:, 16:].reshape(128, 256) + value_bias).astype(BF))
    keys = jnp.concatenate(key_parts, axis=1)
    values = jnp.concatenate(value_parts, axis=1)
    scores = dot_nn(queries, keys) / math.sqrt(HEAD_DIM)
    scores = jnp.where(allowed, scores, -jnp.inf)
    weights = jnp.where(allowed, jnp.exp(scores - jnp.max(scores, axis=1, keepdims=True)), 0.0)
    denominator = jnp.sum(weights, axis=1, keepdims=True)
    att[0] = (dot_nt(weights.astype(BF), values) / denominator).astype(BF)
    send_att = remote(att.at[0], att.at[1], at_send, at_recv, partner)
    send_att.start()

    for copy in out_local:
        copy.wait()
    for copy in out_remote:
        copy.wait_recv()
    for pair in range(2):
        if pair == 1:
            send_att.wait_recv()

        @pl.loop(0, 8)
        def _(f):
            weights = jnp.concatenate([wo[0, f], wo[1, f]], axis=0)
            spread(pair, f, dot_nn(att[pair], weights))

        units(scatter_first, 2 * pair, 2 * pair + 2)
    gather_drain()

    def finish_first(v, total):
        block = (tok_ref[token_unit(v), :].astype(F32) + total).astype(BF)
        resid[token_unit(v), :] = block
        ag[v, 0] = block
        gather_begin(v)

    scatter_rest(finish_first)
    square_sums = square_row(resid[...].astype(F32))
    row = lax.broadcasted_iota(jnp.int32, (8, 128), 0)
    sums[0] = jnp.where(row == 0, square_sums, jnp.zeros((8, 128), F32))
    for d in range(1, 16):
        stat_copy(1, d).start()

    def beside_second(i):
        if i == 1:
            spread_roots(1)
        elif i == 3:
            scatter_drain()
        elif i == 4:
            collect_roots(1)

    gather(beside_second)
    for copy in local_copies[2:]:
        copy.wait()
    for copy in remote_copies[2:]:
        copy.wait_recv()

    accg[...] = jnp.zeros_like(accg)
    accu[...] = jnp.zeros_like(accu)

    @pl.loop(0, 8)
    def _(f):
        blocks = [normalized(f, mine, 8) for mine in (True, False)]
        cols = [feature_columns(f, mine) for mine in (True, False)]
        for side in range(2):
            accg[side] += dot_nt(blocks[0], wg[side, :, cols[0]]) + dot_nt(blocks[1], wg[side, :, cols[1]])
            accu[side] += dot_nt(blocks[0], wu[side, :, cols[0]]) + dot_nt(blocks[1], wu[side, :, cols[1]])

    for side in range(2):
        gate = accg[side]
        hid[0, side] = (gate / (1.0 + jnp.exp(-gate)) * accu[side]).astype(BF)
    send_hid = remote(hid.at[0], hid.at[1], hd_send, hd_recv, partner)
    send_hid.start()
    for copy in down_local:
        copy.wait()
    for copy in down_remote:
        copy.wait_recv()
    for pair in range(2):
        if pair == 1:
            send_hid.wait_recv()

        @pl.loop(0, 8)
        def _(f):
            product = dot_nn(hid[pair, 0], wd[0, f]) + dot_nn(hid[pair, 1], wd[1, f])
            spread(pair, f, product)

        units(scatter_first, 2 * pair, 2 * pair + 2)
    gather_drain()

    def finish_second(v, total):
        out_ref[token_unit(v), :] = (resid[token_unit(v), :].astype(F32) + total).astype(BF)

    scatter_rest(finish_second)
    scatter_drain()
    for d in range(1, 16):
        stat_copy(0, d).wait_send()
        stat_copy(1, d).wait_send()
    for e in range(1, 8):
        root_copy(0, e).wait_send()
        root_copy(1, e).wait_send()
    for d in range(1, 8):
        kv_copy(d).wait_send()
    forward.wait_send()
    send_att.wait_send()
    send_hid.wait_send()
    for copy in remote_copies + out_remote + down_remote:
        copy.wait_send()


def rotary_tables():
    half = HEAD_DIM // 2
    frequency = np.power(np.float32(ROTARY_BASE), -(np.arange(half, dtype=np.float32) * 2.0) / HEAD_DIM).astype(np.float32)
    index = np.arange(TOKENS)
    side, item, low, along, row = index >> 8, (index >> 7) & 1, (index >> 6) & 1, (index >> 4) & 3, index & 15
    position = 256 * low + 64 * along + 32 * side + 16 * item + row
    angles = (position.astype(np.float32)[:, None] * frequency[None, :]).astype(np.float32)
    cosine, sine = np.cos(angles).astype(np.float32), np.sin(angles).astype(np.float32)
    return (
        np.ascontiguousarray(cosine.T), np.ascontiguousarray(sine.T),
        np.concatenate([cosine, cosine], axis=1), np.concatenate([-sine, sine], axis=1),
    )


def shards(
    tokens, segment_ids, attn_gain, query_weight, query_bias, key_weight, value_weight, value_bias,
    out_weight, ffn_gain, gate_weight, up_weight, down_weight,
):
    small = jnp.concatenate(
        [
            attn_gain.astype(F32), ffn_gain.astype(F32), query_bias.astype(F32), value_bias.astype(F32),
            segment_ids.astype(F32), jnp.zeros((96,), F32),
        ]
    ).reshape(18, 128)
    kv_weight = jnp.concatenate([key_weight, value_weight], axis=0)
    units = gate_weight.shape[0]
    any_spec = pl.BlockSpec(memory_space=pl.ANY)
    vmem_spec = pl.BlockSpec(memory_space=pltpu.VMEM)
    dma = pltpu.SemaphoreType.DMA
    gathers, scatters = len(GATHER), len(SCATTER)
    return pl.pallas_call(
        kernel,
        out_shape=jax.ShapeDtypeStruct((64, BLOCK), BF),
        in_specs=[vmem_spec] * 2 + [any_spec] * 10,
        out_specs=vmem_spec,
        scratch_shapes=[
            pltpu.VMEM((2, 64, MODEL), BF),
            pltpu.VMEM((2, 16, MODEL), BF),
            pltpu.VMEM((2, 8, 64, BLOCK), BF),
            pltpu.VMEM((2, units, MODEL), BF),
            pltpu.VMEM((2, units, MODEL), BF),
            pltpu.VMEM((2, 8, units, BLOCK), BF),
            pltpu.VMEM((64, 512), F32),
            pltpu.VMEM((64, 512), F32),
            pltpu.VMEM((512, 128), F32),
            pltpu.VMEM((512, 128), F32),
            pltpu.VMEM((4, 64, ROWS, BLOCK), BF),
            pltpu.VMEM((2, 64, ROWS, BLOCK), BF),
            pltpu.VMEM((16, 256, BLOCK), BF),
            pltpu.VMEM((4, 64, ROWS, BLOCK), F32),
            pltpu.VMEM((4, 64, ROWS, BLOCK), BF),
            pltpu.VMEM((4, 63, ROWS, BLOCK), BF),
            pltpu.VMEM((16, 16, 128), F32),
            pltpu.VMEM((16, 8, 128), F32),
            pltpu.VMEM((2, 8, 8, 128), F32),
            pltpu.VMEM((128, 128), F32),
            pltpu.VMEM((256, 128), F32),
            pltpu.VMEM((2, 8, 32, 256), F32),
            pltpu.VMEM((2, 256, 128), BF),
            pltpu.VMEM((2, 2, 256, units), BF),
            pltpu.VMEM((256, 128), F32),
            pltpu.VMEM((32, 256), F32),
            pltpu.VMEM((2, 256, units), F32),
            pltpu.VMEM((2, 256, units), F32),
            pltpu.VMEM((64, BLOCK), BF),
            dma((4, gathers)), dma((4, gathers)),
            dma((2, 4)), dma((2, 4)),
            dma((4, scatters)), dma((4, scatters)),
            dma((16,)), dma((16,)), dma((16,)), dma((16,)), dma((2, 8)), dma((2, 8)),
            dma((8,)), dma((8,)),
            dma, dma, dma, dma, dma, dma,
            dma((8,)), dma((4,)), dma((4,)),
            dma((8,)), dma((8,)), dma((8,)),
            dma((8,)), dma((8,)), dma((8,)),
        ],
        compiler_params=pltpu.CompilerParams(
            collective_id=0, has_side_effects=True, vmem_limit_bytes=60 * 1024 * 1024
        ),
        name="layer",
    )(
        tokens, small, query_weight, kv_weight, out_weight, gate_weight, up_weight, down_weight, *rotary_tables()
    )


def solution(mesh):
    placed = (
        P("gx", "gy"),
        P("gy"),
        P("gy"),
        P(("gx", "gy"), None),
        P("gx"),
        P(("gx", "gy"), None),
        P(("gx", "gy"), None),
        P("gx"),
        P(("gx", "gy"), None),
        P("gy"),
        P(("gx", "gy"), None),
        P(("gx", "gy"), None),
        P(("gx", "gy"), None),
    )
    return jax.shard_map(
        shards, mesh=mesh, in_specs=placed, out_specs=P("gx", "gy"), check_vma=False
    )
```

```python
import functools
import math

import jax
import jax.numpy as jnp
import numpy as np
from jax import lax
from jax.experimental import pallas as pl
from jax.experimental.pallas import tpu as pltpu
from jax.sharding import PartitionSpec as P


HEAD_DIM = 128
EPSILON = 1e-06
ROTARY_BASE = 1000000.0
TOKENS = 512
MODEL = 8192
BLOCK = 512
ROWS = 16
BF = jnp.bfloat16
F32 = jnp.float32
MESH = pl.DeviceIdType.MESH


def dot_nt(left, right):
    return lax.dot_general(left, right, (((1,), (1,)), ((), ())), preferred_element_type=F32)


def dot_nn(left, right):
    return lax.dot_general(left, right, (((1,), (0,)), ((), ())), preferred_element_type=F32)


GATHER = {}
for _sign, _seen in ((1, 2), (3, 1), (2, 3)):
    GATHER[f"own1_{_sign}"] = (0, _seen, 1, 1, _sign, 0)
    GATHER[f"own2_{_sign}"] = (0, 4 * _seen, 1, 2, _sign, 1)
    GATHER[f"row2_{_sign}"] = (1, 4 * _seen + 1, 3, 2, _sign, 2)
for _sign, _seen in ((1, 2), (3, 1)):
    for _k in range(4):
        GATHER[f"one3_{_k}_{_sign}"] = (4 * _k, 16 * _seen + 4 * _k, 1, 3, _sign, 4 * _seen + _k)
        GATHER[f"row3_{_k}_{_sign}"] = (4 * _k + 1, 16 * _seen + 4 * _k + 1, 3, 3, _sign, 4 * _seen + _k)
for _k in range(4):
    GATHER[f"pass3_{_k}_3"] = (16 + 4 * _k, 48 + 4 * _k, 2, 3, 3, 3)
    GATHER[f"pass3_{_k}_1"] = (32 + 4 * _k + 2, 48 + 4 * _k + 2, 2, 3, 1, 3)
ARRIVING = {0: 3, 1: 3, 2: 9, 3: 16, **{i: 4 for i in range(4, 12)}}

SCATTER = {}
for _k in (3, 2):
    SCATTER[f"far3_{_k}"] = (48 + 4 * _k, 4 * (3 - _k), 4, 3, 1, _k)
for _k in (1, 0):
    SCATTER[f"far3_{_k}"] = (48 + 4 * _k, 8 + 4 * (1 - _k), 4, 3, 3, _k)
for _k in range(4):
    SCATTER[f"up3_{_k}"] = (16 + 4 * _k, 16 + 4 * _k, 4, 3, 1, 4 + _k)
    SCATTER[f"down3_{_k}"] = (32 + 4 * _k, 32 + 4 * _k, 4, 3, 3, 4 + _k)
for _k, _sign in ((1, 1), (2, 3), (3, 2)):
    SCATTER[f"to2_{_k}"] = (4 * _k, 44 + 4 * _k, 4, 2, _sign, 8)
    SCATTER[f"to1_{_k}"] = (_k, 59 + _k, 1, 1, _sign, 9)
SUMMED = {**{i: 4 for i in range(4)}, **{i: 8 for i in range(4, 8)}, 8: 12, 9: 3}


def one_hot3(value):
    second, third = lax.rem(value, 2), lax.div(value, 2)
    return 1 - second - third, second, third


def kernel(
    tok_ref, segment_ref, gain_ref, ffn_gain_ref, query_bias_ref, value_bias_ref,
    wq_hbm, wk_hbm, wv_hbm, wo_hbm, wg_hbm, wu_hbm, wd_hbm,
    cosk_hbm, sink_hbm, cosq_hbm, sinq_hbm,
    out_ref,
    wq, wkv, wo, wg, wu, wd, cosk, sink, cosq, sinq,
    ag, xb, an, part, sb, rb, stats, sums, roots, tall, scale, bias, kvall, att, hid, accq, acckv, accg, accu, resid,
    ag_send, ag_recv, px_send, px_recv, rs_send, rs_recv, st_send, st_recv, su_send, su_recv, ro_send, ro_recv,
    kv_send, kv_recv, kf_send, kf_recv, at_send, at_recv, hd_send, hd_recv,
    wl_sem, ws_sem, wr_sem, ol_sem, os_sem, or_sem, dl_sem, ds_sem, dr_sem,
):
    gx, gy = lax.axis_index("gx"), lax.axis_index("gy")
    x, y_lo = lax.rem(gx, 4), lax.div(gx, 4)
    core, z, y_hi = lax.rem(gy, 2), lax.rem(lax.div(gy, 2), 4), lax.div(gy, 8)
    y = y_hi * 2 + y_lo
    chip = y_hi * 4 + z
    partner = (gx, gy + 1 - 2 * core)

    def device(x, y, z):
        return (lax.rem(y, 2) * 4 + x, lax.div(y, 2) * 8 + z * 2 + core)

    def turn(v):
        group, item = lax.div(v, 2), lax.rem(v, 2)
        return (1 - group) * core * (1 + item) + group * (1 + item - core)

    def neighbour(v, level, sign):
        e0, e1, e2 = one_hot3(lax.rem(turn(v) + 3 - level, 3))
        return device(lax.rem(x + sign * e0, 4), lax.rem(y + sign * e1, 4), lax.rem(z + sign * e2, 4))

    neighbours = {
        (v, level, sign): neighbour(v, level, sign) for v in range(4) for level in (1, 2, 3) for sign in (1, 2, 3)
    }

    def toward(v, level, sign):
        return neighbours[v, level, sign]

    def slot(position, mine):
        d = lax.rem(position - mine + 4, 4)
        return d + lax.div(d, 2) - 2 * lax.div(d, 3)

    def strides(rotation):
        e0, e1, e2 = one_hot3(rotation)
        return 16 * e0 + e1 + 4 * e2, 4 * e0 + 16 * e1 + e2, e0 + 4 * e1 + 16 * e2

    x_slots = [slot(position, x) for position in range(4)]
    unit_strides = [strides(turn(v)) for v in range(4)]
    other_strides = [strides(j + core) for j in range(2)]

    def places(stride, f):
        fy, fz = lax.div(f, 4), lax.rem(f, 4)
        z_part = stride[2] * slot(fz, z)
        y_parts = [stride[1] * slot(fy * 2 + ty, y) + z_part for ty in range(2)]
        return [y_parts[ty] + stride[0] * x_slots[tx] for ty in range(2) for tx in range(4)]

    def remote(src, dst, send, recv, target):
        return pltpu.make_async_remote_copy(
            src_ref=src, dst_ref=dst, send_sem=send, recv_sem=recv, device_id=target, device_id_type=MESH
        )

    barrier = pltpu.get_barrier_semaphore()
    greeted = (
        [device(x, lax.rem(y + 3 + 2 * y_lo, 4), z)]
        + [(lax.rem(gx + e, 8), gy) for e in range(1, 8)]
        + [(gx, lax.rem(gy + d, 16)) for d in range(1, 16)]
    )
    for target in greeted:
        pl.semaphore_signal(barrier, inc=1, device_id=target, device_id_type=MESH)

    whole = (
        (wq_hbm, wq.at[core]), (wk_hbm, wkv.at[core, 0]), (wv_hbm, wkv.at[core, 1]),
        (wg_hbm, wg.at[core]), (wu_hbm, wu.at[core]),
    )
    tables = ((cosk_hbm, cosk), (sink_hbm, sink), (cosq_hbm, cosq), (sinq_hbm, sinq))
    local_copies = [
        pltpu.make_async_copy(src, dst, wl_sem.at[i]) for i, (src, dst) in enumerate(whole)
    ]
    table_copies = [
        pltpu.make_async_copy(src, dst, wl_sem.at[5 + i]) for i, (src, dst) in enumerate(tables)
    ]
    remote_copies = [
        remote(src, dst, ws_sem.at[i], wr_sem.at[i], partner) for i, (src, dst) in enumerate(whole)
    ]
    columns = lambda f, side: pl.ds(pl.multiple_of((2 * f + side) * BLOCK, BLOCK), BLOCK)
    out_local = [pltpu.make_async_copy(wo_hbm.at[:, columns(f, core)], wo.at[core, f], ol_sem.at[f]) for f in range(8)]
    down_local = [pltpu.make_async_copy(wd_hbm.at[:, columns(f, core)], wd.at[core, f], dl_sem.at[f]) for f in range(8)]
    out_remote = [remote(wo_hbm.at[:, columns(f, 1 - core)], wo.at[core, f], os_sem.at[f], or_sem.at[f], partner) for f in range(8)]
    down_remote = [remote(wd_hbm.at[:, columns(f, 1 - core)], wd.at[core, f], ds_sem.at[f], dr_sem.at[f], partner) for f in range(8)]
    for copy in local_copies[:3] + table_copies + out_local + local_copies[3:] + down_local:
        copy.start()

    def token_unit(v):
        return pl.ds(pl.multiple_of(16 * lax.rem(v + 2 * core, 4), 16), 16)

    def square_row(values):
        squares = values * values
        folded = squares[:, :128] + squares[:, 128:256] + squares[:, 256:384] + squares[:, 384:]
        row = jnp.sum(jnp.transpose(folded), axis=0, keepdims=True)
        return jnp.concatenate([row, jnp.zeros((1, 64), F32)], axis=1)

    def stat_copy(phase, d):
        there = (gx, lax.rem(gy + d, 16))
        if phase == 0:
            return remote(stats.at[0], stats.at[d], st_send.at[d], st_recv.at[d], there)
        return remote(sums.at[0], sums.at[d], su_send.at[d], su_recv.at[d], there)

    def root_copy(phase, e):
        return remote(
            roots.at[phase, 0], roots.at[phase, e], ro_send.at[phase, e], ro_recv.at[phase, e], (lax.rem(gx + e, 8), gy)
        )

    def spread_roots(phase):
        for d in range(1, 16):
            stat_copy(phase, d).wait_recv()
        summed = jnp.sum(stats[:, :8] if phase == 0 else sums[...], axis=0)
        inverse = lax.rsqrt(summed / MODEL + EPSILON)
        roots[phase, 0] = inverse
        for e in range(1, 8):
            root_copy(phase, e).start()

    def collect_roots(phase):
        for e in range(1, 8):
            root_copy(phase, e).wait_recv()
        factors = jnp.concatenate([roots[phase, e, :1] for e in range(8)], axis=0)
        tall[...] = jnp.transpose(jnp.concatenate([factors] * 16, axis=0))
        lane = lax.broadcasted_iota(jnp.int32, (16, 128), 1)
        for j in range(2):
            rows = tall[pl.ds(pl.multiple_of(32 * core + 16 * j, 16), 16), :]
            for owner_gx in range(8):
                column = jnp.sum(jnp.where(lane == lax.rem(gx + 8 - owner_gx, 8), rows, 0.0), axis=1, keepdims=True)
                scale[128 * j + 16 * owner_gx : 128 * j + 16 * owner_gx + 16] = jnp.broadcast_to(column, (16, 128))

    def normalized(f, mine, first_row):
        block = gathered(f, mine).astype(F32)
        held = lax.rem(gy + 16 - (2 * f + (core if mine else 1 - core)), 16)
        gains = stats[held, first_row : first_row + 4]
        gain = jnp.concatenate([gains[i : i + 1] for i in range(4)], axis=1)
        factor = scale[...]
        return (block * jnp.concatenate([factor] * 4, axis=1) * gain).astype(BF)

    def gather_copy(name, v):
        src, dst, count, level, sign, arrival = GATHER[name]
        return remote(
            ag.at[v, pl.ds(src, count)], ag.at[v, pl.ds(dst, count)], ag_send.at[v], ag_recv.at[v, arrival],
            toward(v, level, sign),
        )

    def px_copy(j, k):
        return remote(
            ag.at[2 + j, pl.ds(16 * k, 16)], xb.at[j, pl.ds(16 * k, 16)], px_send.at[j], px_recv.at[j], partner
        )

    def units(body, first=0, last=4):
        for v in range(first, last):
            body(v)

    def gather_begin(v):
        for sign in (1, 3, 2):
            gather_copy(f"own1_{sign}", v).start()
        for sign in (1, 3):
            gather_copy(f"one3_0_{sign}", v).start()
        for sign in (1, 3, 2):
            gather_copy(f"own2_{sign}", v).start()

    def gather(beside):
        def start(v, *names):
            for n in names:
                gather_copy(n, v).start()

        def arrive(v, *arrivals):
            for a in arrivals:
                blocks = ag.at[v, pl.ds(0, ARRIVING[a])]
                pltpu.make_async_copy(blocks, blocks, ag_recv.at[v, a]).wait()

        def t1(v):
            arrive(v, 0)
            start(v, "row2_1", "row2_3", "row2_2", "row3_0_1", "row3_0_3")

        def t2(v):
            arrive(v, 1)
            for k in (1, 2, 3):
                start(v, f"one3_{k}_1", f"one3_{k}_3")

        def t3(v):
            arrive(v, 4, 8)
            start(v, "pass3_0_3", "pass3_0_1")

        def t4(v):
            arrive(v, 2)
            for k in (1, 2, 3):
                start(v, f"row3_{k}_1", f"row3_{k}_3")

        def passing(k):
            def step(v):
                arrive(v, 4 + k, 8 + k)
                start(v, f"pass3_{k}_3", f"pass3_{k}_1")

            return step

        for i, step in enumerate((t1, t2, t3, t4)):
            units(step)
            beside(i)
        for j in range(2):
            px_copy(j, 0).start()
        for k in (1, 2, 3):
            units(passing(k))
        for j in range(2):
            px_copy(j, 1).start()
            px_copy(j, 2).start()
        beside(4)
        for j in range(2):
            arrive(2 + j, 3)
            px_copy(j, 3).start()
        units(lambda v: arrive(v, 3), 0, 2)
        for j in range(2):
            pltpu.make_async_copy(xb.at[j], xb.at[j], px_recv.at[j]).wait()

    def gather_drain():
        for v in range(4):
            blocks = ag.at[v, pl.ds(0, 63)]
            pltpu.make_async_copy(blocks, blocks, ag_send.at[v]).wait()
        for j in range(2):
            pltpu.make_async_copy(xb.at[j], xb.at[j], px_send.at[j]).wait()

    def gathered(f, mine):
        pieces = []
        for j in range(2):
            for at in places(unit_strides[j] if mine else other_strides[j], f):
                pieces.append(ag[j, at] if mine else xb[j, at])
        return jnp.concatenate(pieces, axis=0)

    def feature_columns(f, mine):
        return columns(f, core if mine else 1 - core)

    def scatter_copy(name, v):
        src, dst, count, level, sign, arrival = SCATTER[name]
        return remote(
            sb.at[v, pl.ds(src, count)], rb.at[v, pl.ds(dst, count)], rs_send.at[v], rs_recv.at[v, arrival],
            toward(v, level, sign),
        )

    def rs_start(v, *names):
        for n in names:
            scatter_copy(n, v).start()

    def rs_arrive(v, *arrivals):
        for a in arrivals:
            blocks = rb.at[v, pl.ds(0, SUMMED[a])]
            pltpu.make_async_copy(blocks, blocks, rs_recv.at[v, a]).wait()

    def cast(v, src, count=4):
        sb[v, pl.ds(src, count)] = part[v, pl.ds(src, count)].astype(BF)

    def cast_sum(v, src, place_at, count=4):
        sb[v, pl.ds(src, count)] = (
            part[v, pl.ds(src, count)] + rb[v, pl.ds(place_at, count)].astype(F32)
        ).astype(BF)

    def scatter_first(v):
        for k in (3, 1, 2, 0):
            cast(v, 48 + 4 * k)
            rs_start(v, f"far3_{k}")
        for k in (3, 2):
            cast(v, 32 + 4 * k)
            rs_start(v, f"down3_{k}")
        cast(v, 16 + 4 * 1)
        rs_start(v, "up3_1")

    def scatter_rest(finish):
        def s1(v):
            for k in (3, 2):
                rs_arrive(v, k)
                cast_sum(v, 16 + 4 * k, 4 * (3 - k))
                rs_start(v, f"up3_{k}")
            for k in (1, 0):
                rs_arrive(v, k)
                cast_sum(v, 32 + 4 * k, 8 + 4 * (1 - k))
                rs_start(v, f"down3_{k}")
            cast(v, 16)
            rs_start(v, "up3_0")

        def total3(v, k):
            rs_arrive(v, 4 + k)
            return (
                part[v, pl.ds(4 * k, 4)]
                + rb[v, pl.ds(16 + 4 * k, 4)].astype(F32)
                + rb[v, pl.ds(32 + 4 * k, 4)].astype(F32)
            )

        def s2(k):
            def step(v):
                sb[v, pl.ds(4 * k, 4)] = total3(v, k).astype(BF)
                rs_start(v, f"to2_{k}")

            return step

        def s3(v):
            total = total3(v, 0)
            rs_arrive(v, 8)
            for place_at in (48, 52, 56):
                total = total + rb[v, pl.ds(place_at, 4)].astype(F32)
            part[v, 0] = total[0]
            sb[v, 1:4] = total[1:].astype(BF)
            rs_start(v, "to1_1", "to1_2", "to1_3")

        def s4(v):
            rs_arrive(v, 9)
            total = part[v, 0]
            for place_at in (60, 61, 62):
                total = total + rb[v, place_at].astype(F32)
            finish(v, total)

        for step in (s1, s2(3), s2(2), s2(1), s3, s4):
            units(step)

    def scatter_drain():
        for v in range(4):
            blocks = sb.at[v, pl.ds(0, 63)]
            pltpu.make_async_copy(blocks, blocks, rs_send.at[v]).wait()

    def spread(pair, f, product):
        for j in range(2):
            v = 2 * pair + j
            for i, at in enumerate(places(unit_strides[v], f)):
                row = 128 * j + 16 * i
                part[v, at] = product[row : row + 16]

    for v in range(4):
        ag[v, 0] = tok_ref[token_unit(v), :]
    square_sums = square_row(tok_ref[...].astype(F32))
    stats[0] = jnp.zeros((16, 128), F32)
    stats[0, 0:1] = square_sums
    stats[0, 1:2, 0:32] = segment_ref[...].astype(F32).reshape(1, 32)
    stats[0, 4:8] = gain_ref[...].astype(F32).reshape(4, 128)
    stats[0, 8:12] = ffn_gain_ref[...].astype(F32).reshape(4, 128)
    bias[0:8] = query_bias_ref[...].astype(F32).reshape(8, 128)
    bias[8:9] = value_bias_ref[...].astype(F32).reshape(1, 128)
    pl.semaphore_wait(barrier, len(greeted))
    units(gather_begin)
    for d in range(1, 16):
        stat_copy(0, d).start()
    for copy in remote_copies[:3]:
        copy.start()

    def beside_first(i):
        if i == 0:
            spread_roots(0)
            for copy in out_remote + remote_copies[3:] + down_remote:
                copy.start()
        elif i == 4:
            collect_roots(0)

    gather(beside_first)
    documents = jnp.sum(
        jnp.where(lax.broadcasted_iota(jnp.int32, (16, 16, 128), 1) == 1, stats[...], 0.0), axis=1
    )
    for copy in local_copies[:3] + table_copies:
        copy.wait()
    for copy in remote_copies[:3]:
        copy.wait_recv()

    acckv[...] = jnp.zeros_like(acckv)

    @pl.loop(0, 8)
    def _(f):
        for mine in (True, False):
            cols = feature_columns(f, mine)
            weights = [wkv[side, kind, :, cols].astype(F32) for kind in range(2) for side in range(2)]
            weights = jnp.concatenate(weights, axis=0).astype(BF)
            block = normalized(f, mine, 4)
            an[2 * f + (0 if mine else 1)] = block
            acckv[...] += dot_nt(weights, block)

    kvall[core, chip] = acckv[...]

    def kv_copy(d):
        there = lax.rem(gy + 2 * d, 16)
        return remote(kvall.at[core, chip], kvall.at[core, chip], kv_send.at[d], kv_recv.at[d], (gx, there))

    def kv_arrival(d):
        source = lax.rem(chip + 8 - d, 8)
        return remote(kvall.at[core, source], kvall.at[core, source], kv_send.at[d], kv_recv.at[d], partner)

    for d in range(1, 8):
        kv_copy(d).start()

    accq[...] = jnp.zeros_like(accq)

    @pl.loop(0, 8)
    def _(f):
        for mine in (True, False):
            cols = feature_columns(f, mine)
            weights = jnp.concatenate([wq[0, :, cols], wq[1, :, cols]], axis=0)
            accq[...] += dot_nt(an[2 * f + (0 if mine else 1)], weights)

    query = accq[...] + bias[pl.ds(chip, 1), :]
    own_rows = pl.ds(pl.multiple_of(256 * core, 256), 256)
    turned = jnp.concatenate([query[:, 64:], query[:, :64]], axis=1)
    queries = (query * cosq[own_rows, :] + turned * sinq[own_rows, :]).astype(BF)

    for d in range(1, 8):
        kv_arrival(d).wait_recv()
    forward = remote(kvall.at[core], kvall.at[core], kf_send, kf_recv, partner)
    forward.start()

    def token_parts(index, own_core):
        item, low, along, row = (
            (index >> 7) & 1, (index >> 6) & 1, (index >> 4) & 3, index & 15,
        )
        return 256 * low + 64 * along + 32 * own_core + 16 * item + row, 8 * low + 2 * along + own_core, 16 * item + row

    def owner(index):
        held = gy - index
        return jnp.where(held < 0, held + 16, held)

    docs = documents.astype(BF)
    key_index = lax.broadcasted_iota(jnp.int32, (128, 512), 1)
    _, _, key_lane = token_parts(key_index, key_index >> 8)
    pick = jnp.where(lax.broadcasted_iota(jnp.int32, (128, 512), 0) == key_lane, 1.0, 0.0).astype(BF)
    key_docs = dot_nn(docs, pick)
    key_index = lax.broadcasted_iota(jnp.int32, (16, 512), 1)
    _, key_owner, _ = token_parts(key_index, key_index >> 8)
    is_owner = owner(lax.broadcasted_iota(jnp.int32, (16, 512), 0)) == key_owner
    key_docs = jnp.sum(jnp.where(is_owner, key_docs, 0.0), axis=0, keepdims=True)
    query_index = lax.broadcasted_iota(jnp.int32, (256, 128), 0)
    _, _, query_lane = token_parts(query_index, core)
    pick = jnp.where(lax.broadcasted_iota(jnp.int32, (256, 128), 1) == query_lane, 1.0, 0.0).astype(BF)
    query_docs = dot_nt(pick, docs)
    query_index = lax.broadcasted_iota(jnp.int32, (256, 16), 0)
    _, query_owner, _ = token_parts(query_index, core)
    is_owner = owner(lax.broadcasted_iota(jnp.int32, (256, 16), 1)) == query_owner
    query_docs = jnp.sum(jnp.where(is_owner, query_docs, 0.0), axis=1, keepdims=True)
    key_index = lax.broadcasted_iota(jnp.int32, (256, 512), 1)
    key_position, _, _ = token_parts(key_index, key_index >> 8)
    query_position, _, _ = token_parts(lax.broadcasted_iota(jnp.int32, (256, 512), 0), core)
    allowed = (key_position <= query_position) & (key_docs == query_docs)

    value_bias = jnp.transpose(jnp.broadcast_to(bias[8:9], (128, 128)))
    value_bias = jnp.concatenate([value_bias] * 2, axis=1)
    remote(kvall.at[1 - core], kvall.at[1 - core], kf_send, kf_recv, partner).wait_recv()
    key_parts, value_parts = [], []
    for side in range(2):
        held = kvall[side]
        keys = held[:, :16].reshape(128, 256)
        first, second = keys[:64], keys[64:]
        cosine, sine = cosk[:, 256 * side : 256 * side + 256], sink[:, 256 * side : 256 * side + 256]
        key_parts.append(
            jnp.concatenate([first * cosine - second * sine, second * cosine + first * sine], axis=0).astype(BF)
        )
        value_parts.append((held[:, 16:].reshape(128, 256) + value_bias).astype(BF))
    keys = jnp.concatenate(key_parts, axis=1)
    values = jnp.concatenate(value_parts, axis=1)
    scores = dot_nn(queries, keys) / math.sqrt(HEAD_DIM)
    scores = jnp.where(allowed, scores, -jnp.inf)
    weights = jnp.where(allowed, jnp.exp(scores - jnp.max(scores, axis=1, keepdims=True)), 0.0)
    denominator = jnp.sum(weights, axis=1, keepdims=True)
    att[0] = (dot_nt(weights.astype(BF), values) / denominator).astype(BF)
    send_att = remote(att.at[0], att.at[1], at_send, at_recv, partner)
    send_att.start()

    for copy in out_local:
        copy.wait()
    for copy in out_remote:
        copy.wait_recv()
    for pair in range(2):
        if pair == 1:
            send_att.wait_recv()

        @pl.loop(0, 8)
        def _(f):
            weights = jnp.concatenate([wo[0, f], wo[1, f]], axis=0)
            spread(pair, f, dot_nn(att[pair], weights))

        units(scatter_first, 2 * pair, 2 * pair + 2)
    gather_drain()

    def finish_first(v, total):
        block = (tok_ref[token_unit(v), :].astype(F32) + total).astype(BF)
        resid[token_unit(v), :] = block
        ag[v, 0] = block
        gather_begin(v)

    scatter_rest(finish_first)
    square_sums = square_row(resid[...].astype(F32))
    row = lax.broadcasted_iota(jnp.int32, (8, 128), 0)
    sums[0] = jnp.where(row == 0, square_sums, jnp.zeros((8, 128), F32))
    for d in range(1, 16):
        stat_copy(1, d).start()

    def beside_second(i):
        if i == 1:
            spread_roots(1)
        elif i == 3:
            scatter_drain()
        elif i == 4:
            collect_roots(1)

    gather(beside_second)
    for copy in local_copies[3:]:
        copy.wait()
    for copy in remote_copies[3:]:
        copy.wait_recv()

    accg[...] = jnp.zeros_like(accg)
    accu[...] = jnp.zeros_like(accu)

    @pl.loop(0, 8)
    def _(f):
        blocks = [normalized(f, mine, 8) for mine in (True, False)]
        cols = [feature_columns(f, mine) for mine in (True, False)]
        for side in range(2):
            accg[side] += dot_nt(blocks[0], wg[side, :, cols[0]]) + dot_nt(blocks[1], wg[side, :, cols[1]])
            accu[side] += dot_nt(blocks[0], wu[side, :, cols[0]]) + dot_nt(blocks[1], wu[side, :, cols[1]])

    for side in range(2):
        gate = accg[side]
        hid[0, side] = (gate / (1.0 + jnp.exp(-gate)) * accu[side]).astype(BF)
    send_hid = remote(hid.at[0], hid.at[1], hd_send, hd_recv, partner)
    send_hid.start()
    for copy in down_local:
        copy.wait()
    for copy in down_remote:
        copy.wait_recv()
    for pair in range(2):
        if pair == 1:
            send_hid.wait_recv()

        @pl.loop(0, 8)
        def _(f):
            product = dot_nn(hid[pair, 0], wd[0, f]) + dot_nn(hid[pair, 1], wd[1, f])
            spread(pair, f, product)

        units(scatter_first, 2 * pair, 2 * pair + 2)
    gather_drain()

    def finish_second(v, total):
        out_ref[token_unit(v), :] = (resid[token_unit(v), :].astype(F32) + total).astype(BF)

    scatter_rest(finish_second)
    scatter_drain()
    for d in range(1, 16):
        stat_copy(0, d).wait_send()
        stat_copy(1, d).wait_send()
    for e in range(1, 8):
        root_copy(0, e).wait_send()
        root_copy(1, e).wait_send()
    for d in range(1, 8):
        kv_copy(d).wait_send()
    forward.wait_send()
    send_att.wait_send()
    send_hid.wait_send()
    for copy in remote_copies + out_remote + down_remote:
        copy.wait_send()


def rotary_tables():
    half = HEAD_DIM // 2
    frequency = np.power(np.float32(ROTARY_BASE), -(np.arange(half, dtype=np.float32) * 2.0) / HEAD_DIM).astype(np.float32)
    index = np.arange(TOKENS)
    side, item, low, along, row = index >> 8, (index >> 7) & 1, (index >> 6) & 1, (index >> 4) & 3, index & 15
    position = 256 * low + 64 * along + 32 * side + 16 * item + row
    angles = (position.astype(np.float32)[:, None] * frequency[None, :]).astype(np.float32)
    cosine, sine = np.cos(angles).astype(np.float32), np.sin(angles).astype(np.float32)
    return (
        np.ascontiguousarray(cosine.T), np.ascontiguousarray(sine.T),
        np.concatenate([cosine, cosine], axis=1), np.concatenate([-sine, sine], axis=1),
    )


def shards(
    tokens, segment_ids, attn_gain, query_weight, query_bias, key_weight, value_weight, value_bias,
    out_weight, ffn_gain, gate_weight, up_weight, down_weight,
):
    units = gate_weight.shape[0]
    any_spec = pl.BlockSpec(memory_space=pl.ANY)
    vmem_spec = pl.BlockSpec(memory_space=pltpu.VMEM)
    dma = pltpu.SemaphoreType.DMA
    return pl.pallas_call(
        kernel,
        out_shape=jax.ShapeDtypeStruct((64, BLOCK), BF),
        in_specs=[vmem_spec] * 6 + [any_spec] * 11,
        out_specs=vmem_spec,
        scratch_shapes=[
            pltpu.VMEM((2, 64, MODEL), BF),
            pltpu.VMEM((2, 2, 8, MODEL), BF),
            pltpu.VMEM((2, 8, 64, BLOCK), BF),
            pltpu.VMEM((2, units, MODEL), BF),
            pltpu.VMEM((2, units, MODEL), BF),
            pltpu.VMEM((2, 8, units, BLOCK), BF),
            pltpu.VMEM((64, 512), F32),
            pltpu.VMEM((64, 512), F32),
            pltpu.VMEM((512, 128), F32),
            pltpu.VMEM((512, 128), F32),
            pltpu.VMEM((4, 64, ROWS, BLOCK), BF),
            pltpu.VMEM((2, 64, ROWS, BLOCK), BF),
            pltpu.VMEM((16, 256, BLOCK), BF),
            pltpu.VMEM((4, 64, ROWS, BLOCK), F32),
            pltpu.VMEM((4, 64, ROWS, BLOCK), BF),
            pltpu.VMEM((4, 63, ROWS, BLOCK), BF),
            pltpu.VMEM((16, 16, 128), F32),
            pltpu.VMEM((16, 8, 128), F32),
            pltpu.VMEM((2, 8, 8, 128), F32),
            pltpu.VMEM((128, 128), F32),
            pltpu.VMEM((256, 128), F32),
            pltpu.VMEM((16, 128), F32),
            pltpu.VMEM((2, 8, 32, 256), F32),
            pltpu.VMEM((2, 256, 128), BF),
            pltpu.VMEM((2, 2, 256, units), BF),
            pltpu.VMEM((256, 128), F32),
            pltpu.VMEM((32, 256), F32),
            pltpu.VMEM((2, 256, units), F32),
            pltpu.VMEM((2, 256, units), F32),
            pltpu.VMEM((64, BLOCK), BF),
            dma((4,)), dma((4, 12)),
            dma((2,)), dma((2,)),
            dma((4,)), dma((4, 10)),
            dma((16,)), dma((16,)), dma((16,)), dma((16,)), dma((2, 8)), dma((2, 8)),
            dma((8,)), dma((8,)),
            dma, dma, dma, dma, dma, dma,
            dma((9,)), dma((5,)), dma((5,)),
            dma((8,)), dma((8,)), dma((8,)),
            dma((8,)), dma((8,)), dma((8,)),
        ],
        compiler_params=pltpu.CompilerParams(
            collective_id=0, has_side_effects=True, vmem_limit_bytes=60 * 1024 * 1024
        ),
        name="layer",
    )(
        tokens, segment_ids, attn_gain, ffn_gain, query_bias, value_bias, query_weight, key_weight, value_weight,
        out_weight, gate_weight, up_weight, down_weight, *rotary_tables(),
    )


def solution(mesh):
    placed = (
        P("gx", "gy"),
        P("gy"),
        P("gy"),
        P(("gx", "gy"), None),
        P("gx"),
        P(("gx", "gy"), None),
        P(("gx", "gy"), None),
        P("gx"),
        P(("gx", "gy"), None),
        P("gy"),
        P(("gx", "gy"), None),
        P(("gx", "gy"), None),
        P(("gx", "gy"), None),
    )
    return jax.shard_map(
        shards, mesh=mesh, in_specs=placed, out_specs=P("gx", "gy"), check_vma=False
    )
```

```python
import functools
import math

import jax
import jax.numpy as jnp
import numpy as np
from jax import lax
from jax.experimental import pallas as pl
from jax.experimental.pallas import tpu as pltpu
from jax.sharding import PartitionSpec as P


HEAD_DIM = 128
EPSILON = 1e-06
ROTARY_BASE = 1000000.0
TOKENS = 512
MODEL = 8192
BLOCK = 512
ROWS = 16
BF = jnp.bfloat16
F32 = jnp.float32
MESH = pl.DeviceIdType.MESH


def dot_nt(left, right):
    return lax.dot_general(left, right, (((1,), (1,)), ((), ())), preferred_element_type=F32)


def dot_nn(left, right):
    return lax.dot_general(left, right, (((1,), (0,)), ((), ())), preferred_element_type=F32)


GATHER = {}
for _sign, _seen in ((1, 2), (3, 1), (2, 3)):
    GATHER[f"own1_{_sign}"] = (0, _seen, 1, 1, _sign, 0)
    GATHER[f"own2_{_sign}"] = (0, 4 * _seen, 1, 2, _sign, 1)
    GATHER[f"row2_{_sign}"] = (1, 4 * _seen + 1, 3, 2, _sign, 2)
for _sign, _seen in ((1, 2), (3, 1)):
    for _k in range(4):
        GATHER[f"one3_{_k}_{_sign}"] = (4 * _k, 16 * _seen + 4 * _k, 1, 3, _sign, 4 * _seen + _k)
        GATHER[f"row3_{_k}_{_sign}"] = (4 * _k + 1, 16 * _seen + 4 * _k + 1, 3, 3, _sign, 4 * _seen + _k)
for _k in range(4):
    GATHER[f"pass3_{_k}_3"] = (16 + 4 * _k, 48 + 4 * _k, 2, 3, 3, 3)
    GATHER[f"pass3_{_k}_1"] = (32 + 4 * _k + 2, 48 + 4 * _k + 2, 2, 3, 1, 3)
ARRIVING = {0: 3, 1: 3, 2: 9, 3: 16, **{i: 4 for i in range(4, 12)}}

SCATTER = {}
for _k in (3, 2):
    SCATTER[f"far3_{_k}"] = (48 + 4 * _k, 4 * (3 - _k), 4, 3, 1, _k)
for _k in (1, 0):
    SCATTER[f"far3_{_k}"] = (48 + 4 * _k, 8 + 4 * (1 - _k), 4, 3, 3, _k)
for _k in range(4):
    SCATTER[f"up3_{_k}"] = (16 + 4 * _k, 16 + 4 * _k, 4, 3, 1, 4 + _k)
    SCATTER[f"down3_{_k}"] = (32 + 4 * _k, 32 + 4 * _k, 4, 3, 3, 4 + _k)
for _k, _sign in ((1, 1), (2, 3), (3, 2)):
    SCATTER[f"to2_{_k}"] = (4 * _k, 44 + 4 * _k, 4, 2, _sign, 8)
    SCATTER[f"to1_{_k}"] = (_k, 59 + _k, 1, 1, _sign, 9)
SUMMED = {**{i: 4 for i in range(4)}, **{i: 8 for i in range(4, 8)}, 8: 12, 9: 3}


def one_hot3(value):
    second, third = lax.rem(value, 2), lax.div(value, 2)
    return 1 - second - third, second, third


def kernel(
    tok_ref, segment_ref, gain_ref, ffn_gain_ref, query_bias_ref, value_bias_ref,
    wq_hbm, wk_hbm, wv_hbm, wo_hbm, wg_hbm, wu_hbm, wd_hbm,
    cosk_hbm, sink_hbm, cosq_hbm, sinq_hbm,
    out_ref,
    wq, wkv, wo, wg, wu, wd, cosk, sink, cosq, sinq,
    ag, xb, an, part, sb, rb, stats, sums, roots, tall, scale, bias, kvall, att, hid, accq, acckv, accg, accu, resid,
    ag_send, ag_recv, px_send, px_recv, rs_send, rs_recv, st_send, st_recv, su_send, su_recv, ro_send, ro_recv,
    kv_send, kv_recv, kf_send, kf_recv, at_send, at_recv, hd_send, hd_recv,
    wl_sem, ws_sem, wr_sem, ol_sem, os_sem, or_sem, dl_sem, ds_sem, dr_sem,
):
    gx, gy = lax.axis_index("gx"), lax.axis_index("gy")
    x, y_lo = lax.rem(gx, 4), lax.div(gx, 4)
    core, z, y_hi = lax.rem(gy, 2), lax.rem(lax.div(gy, 2), 4), lax.div(gy, 8)
    y = y_hi * 2 + y_lo
    chip = y_hi * 4 + z
    partner = (gx, gy + 1 - 2 * core)

    def device(x, y, z):
        return (lax.rem(y, 2) * 4 + x, lax.div(y, 2) * 8 + z * 2 + core)

    own_orders = [(0, 1), (2 * core, 1), (1 + core, 0), (1, core)]
    other_orders = [(2 - core, 0), (1, 1 - core)]

    def neighbour(v, level, sign):
        bulk, choice = own_orders[v]
        step = {3: 0, 2: 1 + choice, 1: 2 - choice}[level]
        e0, e1, e2 = one_hot3(lax.rem(jnp.int32(bulk + step), 3))
        return device(lax.rem(x + sign * e0, 4), lax.rem(y + sign * e1, 4), lax.rem(z + sign * e2, 4))

    neighbours = {
        (v, level, sign): neighbour(v, level, sign) for v in range(4) for level in (1, 2, 3) for sign in (1, 2, 3)
    }

    def toward(v, level, sign):
        return neighbours[v, level, sign]

    def slot(position, mine):
        d = lax.rem(position - mine + 4, 4)
        return d + lax.div(d, 2) - 2 * lax.div(d, 3)

    def strides(order):
        bulk, choice = order
        result = []
        for axis in range(3):
            e0, e1, e2 = one_hot3(lax.rem(jnp.int32(axis + 3 - bulk), 3))
            result.append(16 * e0 + (4 - 3 * choice) * e1 + (1 + 3 * choice) * e2)
        return result

    x_slots = [slot(position, x) for position in range(4)]
    unit_strides = [strides(order) for order in own_orders]
    other_strides = [strides(order) for order in other_orders]

    def places(stride, f):
        fy, fz = lax.div(f, 4), lax.rem(f, 4)
        z_part = stride[2] * slot(fz, z)
        y_parts = [stride[1] * slot(fy * 2 + ty, y) + z_part for ty in range(2)]
        return [y_parts[ty] + stride[0] * x_slots[tx] for ty in range(2) for tx in range(4)]

    def remote(src, dst, send, recv, target):
        return pltpu.make_async_remote_copy(
            src_ref=src, dst_ref=dst, send_sem=send, recv_sem=recv, device_id=target, device_id_type=MESH
        )

    barrier = pltpu.get_barrier_semaphore()
    greeted = (
        [device(x, lax.rem(y + 3 + 2 * y_lo, 4), z)]
        + [(lax.rem(gx + e, 8), gy) for e in range(1, 8)]
        + [(gx, lax.rem(gy + d, 16)) for d in range(1, 16)]
    )
    for target in greeted:
        pl.semaphore_signal(barrier, inc=1, device_id=target, device_id_type=MESH)

    whole = (
        (wq_hbm, wq.at[core]), (wk_hbm, wkv.at[core, 0]), (wv_hbm, wkv.at[core, 1]),
        (wg_hbm, wg.at[core]), (wu_hbm, wu.at[core]),
    )
    tables = ((cosk_hbm, cosk), (sink_hbm, sink), (cosq_hbm, cosq), (sinq_hbm, sinq))
    local_copies = [
        pltpu.make_async_copy(src, dst, wl_sem.at[i]) for i, (src, dst) in enumerate(whole)
    ]
    table_copies = [
        pltpu.make_async_copy(src, dst, wl_sem.at[5 + i]) for i, (src, dst) in enumerate(tables)
    ]
    remote_copies = [
        remote(src, dst, ws_sem.at[i], wr_sem.at[i], partner) for i, (src, dst) in enumerate(whole)
    ]
    def wait_bytes(ref, semaphore):
        pltpu.make_async_copy(ref, ref, semaphore).wait()

    columns = lambda f, side: pl.ds(pl.multiple_of((2 * f + side) * BLOCK, BLOCK), BLOCK)
    out_local = [pltpu.make_async_copy(wo_hbm.at[:, columns(f, core)], wo.at[core, f], ol_sem) for f in range(8)]
    down_local = [pltpu.make_async_copy(wd_hbm.at[:, columns(f, core)], wd.at[core, f], dl_sem) for f in range(8)]
    out_remote = [remote(wo_hbm.at[:, columns(f, 1 - core)], wo.at[core, f], os_sem, or_sem, partner) for f in range(8)]
    down_remote = [remote(wd_hbm.at[:, columns(f, 1 - core)], wd.at[core, f], ds_sem, dr_sem, partner) for f in range(8)]
    for copy in local_copies[:3] + table_copies + out_local + local_copies[3:] + down_local:
        copy.start()

    def token_unit(v):
        return pl.ds(pl.multiple_of(16 * lax.rem(v + 2 * core, 4), 16), 16)

    def square_row(values):
        squares = values * values
        folded = squares[:, :128] + squares[:, 128:256] + squares[:, 256:384] + squares[:, 384:]
        row = jnp.sum(jnp.transpose(folded), axis=0, keepdims=True)
        return jnp.concatenate([row, jnp.zeros((1, 64), F32)], axis=1)

    def stat_copy(phase, d):
        there = (gx, lax.rem(gy + d, 16))
        if phase == 0:
            return remote(stats.at[0], stats.at[d], st_send, st_recv, there)
        return remote(sums.at[0], sums.at[d], su_send, su_recv, there)

    def root_copy(phase, e):
        return remote(
            roots.at[phase, 0], roots.at[phase, e], ro_send.at[phase], ro_recv.at[phase], (lax.rem(gx + e, 8), gy)
        )

    def spread_roots(phase):
        wait_bytes(*((stats.at[pl.ds(1, 15)], st_recv) if phase == 0 else (sums.at[pl.ds(1, 15)], su_recv)))
        summed = jnp.sum(stats[:, :8] if phase == 0 else sums[...], axis=0)
        inverse = lax.rsqrt(summed / MODEL + EPSILON)
        roots[phase, 0] = inverse
        for e in range(1, 8):
            root_copy(phase, e).start()

    def collect_roots(phase):
        wait_bytes(roots.at[phase, pl.ds(1, 7)], ro_recv.at[phase])
        factors = jnp.concatenate([roots[phase, e, :1] for e in range(8)], axis=0)
        tall[...] = jnp.transpose(jnp.concatenate([factors] * 16, axis=0))
        lane = lax.broadcasted_iota(jnp.int32, (16, 128), 1)
        for j in range(2):
            rows = tall[pl.ds(pl.multiple_of(32 * core + 16 * j, 16), 16), :]
            for owner_gx in range(8):
                column = jnp.sum(jnp.where(lane == lax.rem(gx + 8 - owner_gx, 8), rows, 0.0), axis=1, keepdims=True)
                scale[128 * j + 16 * owner_gx : 128 * j + 16 * owner_gx + 16] = jnp.broadcast_to(column, (16, 128))

    def normalized(f, mine, first_row):
        block = gathered(f, mine).astype(F32)
        held = lax.rem(gy + 16 - (2 * f + (core if mine else 1 - core)), 16)
        gains = stats[held, first_row : first_row + 4]
        gain = jnp.concatenate([gains[i : i + 1] for i in range(4)], axis=1)
        factor = scale[...]
        return (block * jnp.concatenate([factor] * 4, axis=1) * gain).astype(BF)

    def gather_copy(name, v):
        src, dst, count, level, sign, arrival = GATHER[name]
        return remote(
            ag.at[v, pl.ds(src, count)], ag.at[v, pl.ds(dst, count)], ag_send.at[v], ag_recv.at[v, arrival],
            toward(v, level, sign),
        )

    def px_copy(j, k):
        return remote(
            ag.at[2 + j, pl.ds(16 * k, 16)], xb.at[j, pl.ds(16 * k, 16)], px_send.at[j], px_recv.at[j], partner
        )

    wave_a, wave_b, in_order = (0, 2), (1, 3), (0, 2, 1, 3)

    def units(body, which=in_order):
        for v in which:
            body(v)

    def gather_begin(v):
        for sign in (1, 3, 2):
            gather_copy(f"own1_{sign}", v).start()
        for sign in (1, 3):
            gather_copy(f"one3_0_{sign}", v).start()
        for sign in (1, 3, 2):
            gather_copy(f"own2_{sign}", v).start()

    def gather_start(v, *names):
        for n in names:
            gather_copy(n, v).start()

    def gather_arrive(v, *arrivals):
        for a in arrivals:
            wait_bytes(ag.at[v, pl.ds(0, ARRIVING[a])], ag_recv.at[v, a])

    def t1(v):
        gather_arrive(v, 0)
        gather_start(v, "row2_1", "row2_3", "row2_2", "row3_0_1", "row3_0_3")

    def t2(v):
        gather_arrive(v, 1)
        for k in (1, 2, 3):
            gather_start(v, f"one3_{k}_1", f"one3_{k}_3")

    def t3(v):
        gather_arrive(v, 4, 8)
        gather_start(v, "pass3_0_3", "pass3_0_1")

    def t4(v):
        gather_arrive(v, 2)
        for k in (1, 2, 3):
            gather_start(v, f"row3_{k}_1", f"row3_{k}_3")
        if v >= 2:
            px_copy(v - 2, 0).start()

    def passing(v):
        for k in (1, 2, 3):
            gather_arrive(v, 4 + k, 8 + k)
            gather_start(v, f"pass3_{k}_3", f"pass3_{k}_1")
        if v >= 2:
            px_copy(v - 2, 1).start()
            px_copy(v - 2, 2).start()

    def t5(v):
        gather_arrive(v, 3)
        if v >= 2:
            px_copy(v - 2, 3).start()

    def gather_end():
        for v in (2, 3, 0, 1):
            t5(v)
        for j in range(2):
            wait_bytes(xb.at[j], px_recv.at[j])

    def gather_drain():
        for v in range(4):
            blocks = ag.at[v, pl.ds(0, 63)]
            pltpu.make_async_copy(blocks, blocks, ag_send.at[v]).wait()
        for j in range(2):
            pltpu.make_async_copy(xb.at[j], xb.at[j], px_send.at[j]).wait()

    def gathered(f, mine):
        pieces = []
        for j in range(2):
            for at in places(unit_strides[j] if mine else other_strides[j], f):
                pieces.append(ag[j, at] if mine else xb[j, at])
        return jnp.concatenate(pieces, axis=0)

    def feature_columns(f, mine):
        return columns(f, core if mine else 1 - core)

    def scatter_copy(name, v):
        src, dst, count, level, sign, arrival = SCATTER[name]
        return remote(
            sb.at[v, pl.ds(src, count)], rb.at[v, pl.ds(dst, count)], rs_send.at[v], rs_recv.at[v, arrival],
            toward(v, level, sign),
        )

    def rs_start(v, *names):
        for n in names:
            scatter_copy(n, v).start()

    def rs_arrive(v, *arrivals):
        for a in arrivals:
            blocks = rb.at[v, pl.ds(0, SUMMED[a])]
            pltpu.make_async_copy(blocks, blocks, rs_recv.at[v, a]).wait()

    def cast(v, src, count=4):
        sb[v, pl.ds(src, count)] = part[v, pl.ds(src, count)].astype(BF)

    def cast_sum(v, src, place_at, count=4):
        sb[v, pl.ds(src, count)] = (
            part[v, pl.ds(src, count)] + rb[v, pl.ds(place_at, count)].astype(F32)
        ).astype(BF)

    def scatter_far(v):
        for k in (3, 1, 2, 0):
            cast(v, 48 + 4 * k)
            rs_start(v, f"far3_{k}")

    def scatter_near(v):
        for k in (3, 2):
            cast(v, 32 + 4 * k)
            rs_start(v, f"down3_{k}")
        cast(v, 16 + 4 * 1)
        rs_start(v, "up3_1")

    def s1(v):
        for k in (3, 2):
            rs_arrive(v, k)
            cast_sum(v, 16 + 4 * k, 4 * (3 - k))
            rs_start(v, f"up3_{k}")
        for k in (1, 0):
            rs_arrive(v, k)
            cast_sum(v, 32 + 4 * k, 8 + 4 * (1 - k))
            rs_start(v, f"down3_{k}")
        cast(v, 16)
        rs_start(v, "up3_0")

    def total3(v, k):
        rs_arrive(v, 4 + k)
        return (
            part[v, pl.ds(4 * k, 4)]
            + rb[v, pl.ds(16 + 4 * k, 4)].astype(F32)
            + rb[v, pl.ds(32 + 4 * k, 4)].astype(F32)
        )

    def s2(k):
        def step(v):
            sb[v, pl.ds(4 * k, 4)] = total3(v, k).astype(BF)
            rs_start(v, f"to2_{k}")

        return step

    def s3(v):
        total = total3(v, 0)
        rs_arrive(v, 8)
        for place_at in (48, 52, 56):
            total = total + rb[v, pl.ds(place_at, 4)].astype(F32)
        part[v, 0] = total[0]
        sb[v, 1:4] = total[1:].astype(BF)
        rs_start(v, "to1_1", "to1_2", "to1_3")

    def final_sum(v):
        rs_arrive(v, 9)
        total = part[v, 0]
        for place_at in (60, 61, 62):
            total = total + rb[v, place_at].astype(F32)
        return total

    def scatter_drain():
        for v in range(4):
            blocks = sb.at[v, pl.ds(0, 63)]
            pltpu.make_async_copy(blocks, blocks, rs_send.at[v]).wait()

    def spread(wave, f, product):
        for j, v in enumerate((wave, 2 + wave)):
            for i, at in enumerate(places(unit_strides[v], f)):
                row = 128 * j + 16 * i
                part[v, at] = product[row : row + 16]

    def wave_rows(ref, wave):
        rows = pl.ds(128 * wave, 128)
        return jnp.concatenate([ref[0, rows], ref[1, rows]], axis=0)

    for v in range(4):
        ag[v, 0] = tok_ref[token_unit(v), :]
    square_sums = square_row(tok_ref[...].astype(F32))
    stats[0] = jnp.zeros((16, 128), F32)
    stats[0, 0:1] = square_sums
    stats[0, 1:2, 0:32] = segment_ref[...].astype(F32).reshape(1, 32)
    stats[0, 4:8] = gain_ref[...].astype(F32).reshape(4, 128)
    stats[0, 8:12] = ffn_gain_ref[...].astype(F32).reshape(4, 128)
    bias[0:8] = query_bias_ref[...].astype(F32).reshape(8, 128)
    bias[8:9] = value_bias_ref[...].astype(F32).reshape(1, 128)
    pl.semaphore_wait(barrier, len(greeted))
    units(gather_begin)
    for d in range(1, 16):
        stat_copy(0, d).start()
    for copy in remote_copies[:3]:
        copy.start()

    units(t1)
    spread_roots(0)
    for copy in out_remote + remote_copies[3:] + down_remote:
        copy.start()
    units(t2)
    units(t3)
    units(t4)
    units(passing)
    collect_roots(0)
    gather_end()
    documents = jnp.sum(
        jnp.where(lax.broadcasted_iota(jnp.int32, (16, 16, 128), 1) == 1, stats[...], 0.0), axis=1
    )
    for copy in local_copies[:3] + table_copies:
        copy.wait()
    for copy in remote_copies[:3]:
        copy.wait_recv()

    acckv[...] = jnp.zeros_like(acckv)

    @pl.loop(0, 8, unroll=2)
    def _(f):
        for mine in (True, False):
            cols = feature_columns(f, mine)
            weights = [wkv[side, kind, :, cols].astype(F32) for kind in range(2) for side in range(2)]
            weights = jnp.concatenate(weights, axis=0).astype(BF)
            block = normalized(f, mine, 4)
            an[2 * f + (0 if mine else 1)] = block
            acckv[...] += dot_nt(weights, block)

    kvall[core, chip] = acckv[...]

    def kv_copy(d):
        there = lax.rem(gy + 2 * d, 16)
        return remote(kvall.at[core, chip], kvall.at[core, chip], kv_send, kv_recv, (gx, there))

    for d in range(1, 8):
        kv_copy(d).start()

    accq[...] = jnp.zeros_like(accq)

    @pl.loop(0, 8, unroll=2)
    def _(f):
        for mine in (True, False):
            cols = feature_columns(f, mine)
            weights = jnp.concatenate([wq[0, :, cols], wq[1, :, cols]], axis=0)
            accq[...] += dot_nt(an[2 * f + (0 if mine else 1)], weights)

    query = accq[...] + bias[pl.ds(chip, 1), :]
    own_rows = pl.ds(pl.multiple_of(256 * core, 256), 256)
    turned = jnp.concatenate([query[:, 64:], query[:, :64]], axis=1)
    queries = (query * cosq[own_rows, :] + turned * sinq[own_rows, :]).astype(BF)

    wait_bytes(kvall.at[core, pl.ds(0, 7)], kv_recv)
    forward = remote(kvall.at[core], kvall.at[core], kf_send, kf_recv, partner)
    forward.start()

    def token_parts(index, own_core):
        item, low, along, row = (
            (index >> 7) & 1, (index >> 6) & 1, (index >> 4) & 3, index & 15,
        )
        return 256 * low + 64 * along + 32 * own_core + 16 * item + row, 8 * low + 2 * along + own_core, 16 * item + row

    def owner(index):
        held = gy - index
        return jnp.where(held < 0, held + 16, held)

    docs = documents.astype(BF)
    key_index = lax.broadcasted_iota(jnp.int32, (128, 512), 1)
    _, _, key_lane = token_parts(key_index, key_index >> 8)
    pick = jnp.where(lax.broadcasted_iota(jnp.int32, (128, 512), 0) == key_lane, 1.0, 0.0).astype(BF)
    key_docs = dot_nn(docs, pick)
    key_index = lax.broadcasted_iota(jnp.int32, (16, 512), 1)
    _, key_owner, _ = token_parts(key_index, key_index >> 8)
    is_owner = owner(lax.broadcasted_iota(jnp.int32, (16, 512), 0)) == key_owner
    key_docs = jnp.sum(jnp.where(is_owner, key_docs, 0.0), axis=0, keepdims=True)
    query_index = lax.broadcasted_iota(jnp.int32, (256, 128), 0)
    _, _, query_lane = token_parts(query_index, core)
    pick = jnp.where(lax.broadcasted_iota(jnp.int32, (256, 128), 1) == query_lane, 1.0, 0.0).astype(BF)
    query_docs = dot_nt(pick, docs)
    query_index = lax.broadcasted_iota(jnp.int32, (256, 16), 0)
    _, query_owner, _ = token_parts(query_index, core)
    is_owner = owner(lax.broadcasted_iota(jnp.int32, (256, 16), 1)) == query_owner
    query_docs = jnp.sum(jnp.where(is_owner, query_docs, 0.0), axis=1, keepdims=True)
    key_index = lax.broadcasted_iota(jnp.int32, (256, 512), 1)
    key_position, _, _ = token_parts(key_index, key_index >> 8)
    query_position, _, _ = token_parts(lax.broadcasted_iota(jnp.int32, (256, 512), 0), core)
    allowed = (key_position <= query_position) & (key_docs == query_docs)

    value_bias = jnp.transpose(jnp.broadcast_to(bias[8:9], (128, 128)))
    value_bias = jnp.concatenate([value_bias] * 2, axis=1)
    remote(kvall.at[1 - core], kvall.at[1 - core], kf_send, kf_recv, partner).wait_recv()
    key_parts, value_parts = [], []
    for side in range(2):
        held = kvall[side]
        keys = held[:, :16].reshape(128, 256)
        first, second = keys[:64], keys[64:]
        cosine, sine = cosk[:, 256 * side : 256 * side + 256], sink[:, 256 * side : 256 * side + 256]
        key_parts.append(
            jnp.concatenate([first * cosine - second * sine, second * cosine + first * sine], axis=0).astype(BF)
        )
        value_parts.append((held[:, 16:].reshape(128, 256) + value_bias).astype(BF))
    keys = jnp.concatenate(key_parts, axis=1)
    values = jnp.concatenate(value_parts, axis=1)
    scores = dot_nn(queries, keys) / math.sqrt(HEAD_DIM)
    scores = jnp.where(allowed, scores, -jnp.inf)
    weights = jnp.where(allowed, jnp.exp(scores - jnp.max(scores, axis=1, keepdims=True)), 0.0)
    denominator = jnp.sum(weights, axis=1, keepdims=True)
    att[0] = (dot_nt(weights.astype(BF), values) / denominator).astype(BF)
    send_att = remote(att.at[0], att.at[1], at_send, at_recv, partner)
    send_att.start()

    wait_bytes(wo.at[core], ol_sem)
    wait_bytes(wo.at[1 - core], or_sem)
    send_att.wait_recv()

    def project_out(wave):
        @pl.loop(0, 8, unroll=2)
        def _(f):
            weights = jnp.concatenate([wo[0, f], wo[1, f]], axis=0)
            spread(wave, f, dot_nn(wave_rows(att, wave), weights))

    def finish_first(v):
        block = (tok_ref[token_unit(v), :].astype(F32) + final_sum(v)).astype(BF)
        resid[token_unit(v), :] = block
        ag[v, 0] = block
        gather_begin(v)

    project_out(0)
    units(scatter_far, wave_a)
    units(scatter_near, wave_a)
    project_out(1)
    units(scatter_far, wave_b)
    units(s1, wave_a)
    units(scatter_near, wave_b)
    gather_drain()
    for k in (3, 2, 1):
        units(s2(k), wave_a)
    units(s1, wave_b)
    units(s3, wave_a)
    for k in (3, 2, 1):
        units(s2(k), wave_b)
    units(finish_first, wave_a)
    units(s3, wave_b)
    units(t1, wave_a)
    units(t2, wave_a)
    units(finish_first, wave_b)
    square_sums = square_row(resid[...].astype(F32))
    row = lax.broadcasted_iota(jnp.int32, (8, 128), 0)
    sums[0] = jnp.where(row == 0, square_sums, jnp.zeros((8, 128), F32))
    for d in range(1, 16):
        stat_copy(1, d).start()
    units(t3, wave_a)
    units(t4, wave_a)
    units(t1, wave_b)
    units(t2, wave_b)
    spread_roots(1)
    units(t3, wave_b)
    scatter_drain()
    units(passing, wave_a)
    units(t4, wave_b)
    collect_roots(1)
    units(passing, wave_b)
    gather_end()
    for copy in local_copies[3:]:
        copy.wait()
    for copy in remote_copies[3:]:
        copy.wait_recv()

    accg[...] = jnp.zeros_like(accg)
    accu[...] = jnp.zeros_like(accu)

    @pl.loop(0, 8, unroll=2)
    def _(f):
        blocks = [normalized(f, mine, 8) for mine in (True, False)]
        cols = [feature_columns(f, mine) for mine in (True, False)]
        for side in range(2):
            accg[side] += dot_nt(blocks[0], wg[side, :, cols[0]]) + dot_nt(blocks[1], wg[side, :, cols[1]])
            accu[side] += dot_nt(blocks[0], wu[side, :, cols[0]]) + dot_nt(blocks[1], wu[side, :, cols[1]])

    for side in range(2):
        gate = accg[side]
        hid[0, side] = (gate / (1.0 + jnp.exp(-gate)) * accu[side]).astype(BF)
    send_hid = remote(hid.at[0], hid.at[1], hd_send, hd_recv, partner)
    send_hid.start()
    wait_bytes(wd.at[core], dl_sem)
    wait_bytes(wd.at[1 - core], dr_sem)
    send_hid.wait_recv()

    def project_down(wave):
        rows = pl.ds(128 * wave, 128)

        @pl.loop(0, 8, unroll=2)
        def _(f):
            left = [jnp.concatenate([hid[0, side, rows], hid[1, side, rows]], axis=0) for side in range(2)]
            spread(wave, f, dot_nn(left[0], wd[0, f]) + dot_nn(left[1], wd[1, f]))

    def finish_second(v):
        out_ref[token_unit(v), :] = (resid[token_unit(v), :].astype(F32) + final_sum(v)).astype(BF)

    project_down(0)
    units(scatter_far, wave_a)
    units(scatter_near, wave_a)
    project_down(1)
    units(scatter_far, wave_b)
    units(s1, wave_a)
    units(scatter_near, wave_b)
    gather_drain()
    units(s1, wave_b)
    for k in (3, 2, 1):
        units(s2(k))
    units(s3)
    units(finish_second)
    scatter_drain()

    wait_bytes(stats.at[pl.ds(1, 15)], st_send)
    wait_bytes(sums.at[pl.ds(1, 15)], su_send)
    for phase in range(2):
        wait_bytes(roots.at[phase, pl.ds(1, 7)], ro_send.at[phase])
    wait_bytes(kvall.at[core, pl.ds(0, 7)], kv_send)
    forward.wait_send()
    send_att.wait_send()
    send_hid.wait_send()
    for copy in remote_copies:
        copy.wait_send()
    wait_bytes(wo.at[core], os_sem)
    wait_bytes(wd.at[core], ds_sem)


def rotary_tables():
    half = HEAD_DIM // 2
    frequency = np.power(np.float32(ROTARY_BASE), -(np.arange(half, dtype=np.float32) * 2.0) / HEAD_DIM).astype(np.float32)
    index = np.arange(TOKENS)
    side, item, low, along, row = index >> 8, (index >> 7) & 1, (index >> 6) & 1, (index >> 4) & 3, index & 15
    position = 256 * low + 64 * along + 32 * side + 16 * item + row
    angles = (position.astype(np.float32)[:, None] * frequency[None, :]).astype(np.float32)
    cosine, sine = np.cos(angles).astype(np.float32), np.sin(angles).astype(np.float32)
    return (
        np.ascontiguousarray(cosine.T), np.ascontiguousarray(sine.T),
        np.concatenate([cosine, cosine], axis=1), np.concatenate([-sine, sine], axis=1),
    )


def shards(
    tokens, segment_ids, attn_gain, query_weight, query_bias, key_weight, value_weight, value_bias,
    out_weight, ffn_gain, gate_weight, up_weight, down_weight,
):
    units = gate_weight.shape[0]
    any_spec = pl.BlockSpec(memory_space=pl.ANY)
    vmem_spec = pl.BlockSpec(memory_space=pltpu.VMEM)
    dma = pltpu.SemaphoreType.DMA
    return pl.pallas_call(
        kernel,
        out_shape=jax.ShapeDtypeStruct((64, BLOCK), BF),
        in_specs=[vmem_spec] * 6 + [any_spec] * 11,
        out_specs=vmem_spec,
        scratch_shapes=[
            pltpu.VMEM((2, 64, MODEL), BF),
            pltpu.VMEM((2, 2, 8, MODEL), BF),
            pltpu.VMEM((2, 8, 64, BLOCK), BF),
            pltpu.VMEM((2, units, MODEL), BF),
            pltpu.VMEM((2, units, MODEL), BF),
            pltpu.VMEM((2, 8, units, BLOCK), BF),
            pltpu.VMEM((64, 512), F32),
            pltpu.VMEM((64, 512), F32),
            pltpu.VMEM((512, 128), F32),
            pltpu.VMEM((512, 128), F32),
            pltpu.VMEM((4, 64, ROWS, BLOCK), BF),
            pltpu.VMEM((2, 64, ROWS, BLOCK), BF),
            pltpu.VMEM((16, 256, BLOCK), BF),
            pltpu.VMEM((4, 64, ROWS, BLOCK), F32),
            pltpu.VMEM((4, 64, ROWS, BLOCK), BF),
            pltpu.VMEM((4, 63, ROWS, BLOCK), BF),
            pltpu.VMEM((16, 16, 128), F32),
            pltpu.VMEM((16, 8, 128), F32),
            pltpu.VMEM((2, 8, 8, 128), F32),
            pltpu.VMEM((128, 128), F32),
            pltpu.VMEM((256, 128), F32),
            pltpu.VMEM((16, 128), F32),
            pltpu.VMEM((2, 8, 32, 256), F32),
            pltpu.VMEM((2, 256, 128), BF),
            pltpu.VMEM((2, 2, 256, units), BF),
            pltpu.VMEM((256, 128), F32),
            pltpu.VMEM((32, 256), F32),
            pltpu.VMEM((2, 256, units), F32),
            pltpu.VMEM((2, 256, units), F32),
            pltpu.VMEM((64, BLOCK), BF),
            dma((4,)), dma((4, 12)),
            dma((2,)), dma((2,)),
            dma((4,)), dma((4, 10)),
            dma, dma, dma, dma, dma((2,)), dma((2,)),
            dma, dma,
            dma, dma, dma, dma, dma, dma,
            dma((9,)), dma((5,)), dma((5,)),
            dma, dma, dma, dma, dma, dma,
        ],
        compiler_params=pltpu.CompilerParams(
            collective_id=0, has_side_effects=True, vmem_limit_bytes=60 * 1024 * 1024
        ),
        name="layer",
    )(
        tokens, segment_ids, attn_gain, ffn_gain, query_bias, value_bias, query_weight, key_weight, value_weight,
        out_weight, gate_weight, up_weight, down_weight, *rotary_tables(),
    )


def solution(mesh):
    placed = (
        P("gx", "gy"),
        P("gy"),
        P("gy"),
        P(("gx", "gy"), None),
        P("gx"),
        P(("gx", "gy"), None),
        P(("gx", "gy"), None),
        P("gx"),
        P(("gx", "gy"), None),
        P("gy"),
        P(("gx", "gy"), None),
        P(("gx", "gy"), None),
        P(("gx", "gy"), None),
    )
    return jax.shard_map(
        shards, mesh=mesh, in_specs=placed, out_specs=P("gx", "gy"), check_vma=False
    )
```

```python
import functools
import math

import jax
import jax.numpy as jnp
import numpy as np
from jax import lax
from jax.experimental import pallas as pl
from jax.experimental.pallas import tpu as pltpu
from jax.sharding import PartitionSpec as P


HEAD_DIM = 128
EPSILON = 1e-06
ROTARY_BASE = 1000000.0
TOKENS = 512
MODEL = 8192
BLOCK = 512
ROWS = 16
BF = jnp.bfloat16
F32 = jnp.float32
MESH = pl.DeviceIdType.MESH


def dot_nt(left, right):
    return lax.dot_general(left, right, (((1,), (1,)), ((), ())), preferred_element_type=F32)


def dot_nn(left, right):
    return lax.dot_general(left, right, (((1,), (0,)), ((), ())), preferred_element_type=F32)


GATHER = {}
for _sign, _seen in ((1, 2), (3, 1), (2, 3)):
    GATHER[f"own1_{_sign}"] = (0, _seen, 1, 1, _sign, 0)
    GATHER[f"own2_{_sign}"] = (0, 4 * _seen, 1, 2, _sign, 1)
    GATHER[f"row2_{_sign}"] = (1, 4 * _seen + 1, 3, 2, _sign, 2)
for _sign, _seen in ((1, 2), (3, 1)):
    for _k in range(4):
        GATHER[f"one3_{_k}_{_sign}"] = (4 * _k, 16 * _seen + 4 * _k, 1, 3, _sign, 4 * _seen + _k)
        GATHER[f"row3_{_k}_{_sign}"] = (4 * _k + 1, 16 * _seen + 4 * _k + 1, 3, 3, _sign, 4 * _seen + _k)
for _k in range(4):
    GATHER[f"pass3_{_k}_3"] = (16 + 4 * _k, 48 + 4 * _k, 2, 3, 3, 3)
    GATHER[f"pass3_{_k}_1"] = (32 + 4 * _k + 2, 48 + 4 * _k + 2, 2, 3, 1, 3)
ARRIVING = {0: 3, 1: 3, 2: 9, 3: 16, **{i: 4 for i in range(4, 12)}}

SCATTER = {}
for _k in (3, 2):
    SCATTER[f"far3_{_k}"] = (48 + 4 * _k, 4 * (3 - _k), 4, 3, 1, _k)
for _k in (1, 0):
    SCATTER[f"far3_{_k}"] = (48 + 4 * _k, 8 + 4 * (1 - _k), 4, 3, 3, _k)
for _k in range(4):
    SCATTER[f"up3_{_k}"] = (16 + 4 * _k, 16 + 4 * _k, 4, 3, 1, 4 + _k)
    SCATTER[f"down3_{_k}"] = (32 + 4 * _k, 32 + 4 * _k, 4, 3, 3, 4 + _k)
for _k, _sign in ((1, 1), (2, 3), (3, 2)):
    SCATTER[f"to2_{_k}"] = (4 * _k, 44 + 4 * _k, 4, 2, _sign, 8)
    SCATTER[f"to1_{_k}"] = (_k, 59 + _k, 1, 1, _sign, 9)
SUMMED = {**{i: 4 for i in range(4)}, **{i: 8 for i in range(4, 8)}, 8: 12, 9: 3}


def one_hot3(value):
    second, third = lax.rem(value, 2), lax.div(value, 2)
    return 1 - second - third, second, third


def kernel(
    tok_ref, segment_ref, gain_ref, ffn_gain_ref, query_bias_ref, value_bias_ref,
    wq_hbm, wk_hbm, wv_hbm, wo_hbm, wg_hbm, wu_hbm, wd_hbm,
    cosk_hbm, sink_hbm, cosq_hbm, sinq_hbm,
    out_ref,
    wq, wkv, wo, wg, wu, wd, cosk, sink, cosq, sinq,
    ag, xb, an, part, sb, rb, stats, sums, roots, tall, scale, bias, kvall, att, hid, accq, acckv, accg, accu, resid,
    ag_send, ag_recv, px_send, px_recv, rs_send, rs_recv, st_send, st_recv, su_send, su_recv, ro_send, ro_recv,
    kv_send, kv_recv, kf_send, kf_recv, at_send, at_recv, hd_send, hd_recv,
    wl_sem, ws_sem, wr_sem, ol_sem, os_sem, or_sem, dl_sem, ds_sem, dr_sem,
):
    gx, gy = lax.axis_index("gx"), lax.axis_index("gy")
    x, y_lo = lax.rem(gx, 4), lax.div(gx, 4)
    core, z, y_hi = lax.rem(gy, 2), lax.rem(lax.div(gy, 2), 4), lax.div(gy, 8)
    y = y_hi * 2 + y_lo
    chip = y_hi * 4 + z
    partner = (gx, gy + 1 - 2 * core)

    def device(x, y, z):
        return (lax.rem(y, 2) * 4 + x, lax.div(y, 2) * 8 + z * 2 + core)

    own_orders = [(lax.rem(bulk + 2, 3), 0) for bulk in (core, 2 * core, 1 - core, 2 - core)]
    other_orders = [(lax.rem(bulk + 2, 3), 0) for bulk in (core, 1 + core)]

    def neighbour(v, level, sign):
        bulk, choice = own_orders[v]
        step = {3: 0, 2: 1 + choice, 1: 2 - choice}[level]
        e0, e1, e2 = one_hot3(lax.rem(jnp.int32(bulk + step), 3))
        return device(lax.rem(x + sign * e0, 4), lax.rem(y + sign * e1, 4), lax.rem(z + sign * e2, 4))

    neighbours = {
        (v, level, sign): neighbour(v, level, sign) for v in range(4) for level in (1, 2, 3) for sign in (1, 2, 3)
    }

    def toward(v, level, sign):
        return neighbours[v, level, sign]

    def slot(position, mine):
        d = lax.rem(position - mine + 4, 4)
        return d + lax.div(d, 2) - 2 * lax.div(d, 3)

    def strides(order):
        bulk, choice = order
        result = []
        for axis in range(3):
            e0, e1, e2 = one_hot3(lax.rem(jnp.int32(axis + 3 - bulk), 3))
            result.append(16 * e0 + (4 - 3 * choice) * e1 + (1 + 3 * choice) * e2)
        return result

    x_slots = [slot(position, x) for position in range(4)]
    unit_strides = [strides(order) for order in own_orders]
    other_strides = [strides(order) for order in other_orders]

    def places(stride, f):
        fy, fz = lax.div(f, 4), lax.rem(f, 4)
        z_part = stride[2] * slot(fz, z)
        y_parts = [stride[1] * slot(fy * 2 + ty, y) + z_part for ty in range(2)]
        return [y_parts[ty] + stride[0] * x_slots[tx] for ty in range(2) for tx in range(4)]

    def remote(src, dst, send, recv, target):
        return pltpu.make_async_remote_copy(
            src_ref=src, dst_ref=dst, send_sem=send, recv_sem=recv, device_id=target, device_id_type=MESH
        )

    barrier = pltpu.get_barrier_semaphore()
    greeted = (
        [device(x, lax.rem(y + 3 + 2 * y_lo, 4), z)]
        + [(lax.rem(gx + e, 8), gy) for e in range(1, 8)]
        + [(gx, lax.rem(gy + d, 16)) for d in range(1, 16)]
    )
    for target in greeted:
        pl.semaphore_signal(barrier, inc=1, device_id=target, device_id_type=MESH)

    whole = (
        (wq_hbm, wq.at[core]), (wk_hbm, wkv.at[core, 0]), (wv_hbm, wkv.at[core, 1]),
        (wg_hbm, wg.at[core]), (wu_hbm, wu.at[core]),
    )
    tables = ((cosk_hbm, cosk), (sink_hbm, sink), (cosq_hbm, cosq), (sinq_hbm, sinq))
    local_copies = [
        pltpu.make_async_copy(src, dst, wl_sem.at[i]) for i, (src, dst) in enumerate(whole)
    ]
    table_copies = [
        pltpu.make_async_copy(src, dst, wl_sem.at[5 + i]) for i, (src, dst) in enumerate(tables)
    ]
    remote_copies = [
        remote(src, dst, ws_sem.at[i], wr_sem.at[i], partner) for i, (src, dst) in enumerate(whole)
    ]
    def wait_bytes(ref, semaphore):
        pltpu.make_async_copy(ref, ref, semaphore).wait()

    columns = lambda f, side: pl.ds(pl.multiple_of((2 * f + side) * BLOCK, BLOCK), BLOCK)
    out_local = [pltpu.make_async_copy(wo_hbm.at[:, columns(f, core)], wo.at[core, f], ol_sem) for f in range(8)]
    down_local = [pltpu.make_async_copy(wd_hbm.at[:, columns(f, core)], wd.at[core, f], dl_sem) for f in range(8)]
    out_remote = [remote(wo_hbm.at[:, columns(f, 1 - core)], wo.at[core, f], os_sem, or_sem, partner) for f in range(8)]
    down_remote = [remote(wd_hbm.at[:, columns(f, 1 - core)], wd.at[core, f], ds_sem, dr_sem, partner) for f in range(8)]
    for copy in local_copies[:3] + table_copies + out_local + local_copies[3:] + down_local:
        copy.start()

    def token_unit(v):
        return pl.ds(pl.multiple_of(16 * lax.rem(v + 2 * core, 4), 16), 16)

    def square_row(values):
        squares = values * values
        folded = squares[:, :128] + squares[:, 128:256] + squares[:, 256:384] + squares[:, 384:]
        row = jnp.sum(jnp.transpose(folded), axis=0, keepdims=True)
        return jnp.concatenate([row, jnp.zeros((1, 64), F32)], axis=1)

    def stat_copy(phase, d):
        there = (gx, lax.rem(gy + d, 16))
        if phase == 0:
            return remote(stats.at[0], stats.at[d], st_send, st_recv, there)
        return remote(sums.at[0], sums.at[d], su_send, su_recv, there)

    def root_copy(phase, e):
        return remote(
            roots.at[phase, 0], roots.at[phase, e], ro_send.at[phase], ro_recv.at[phase], (lax.rem(gx + e, 8), gy)
        )

    def spread_roots(phase):
        wait_bytes(*((stats.at[pl.ds(1, 15)], st_recv) if phase == 0 else (sums.at[pl.ds(1, 15)], su_recv)))
        summed = jnp.sum(stats[:, :8] if phase == 0 else sums[...], axis=0)
        inverse = lax.rsqrt(summed / MODEL + EPSILON)
        roots[phase, 0] = inverse
        for e in range(1, 8):
            root_copy(phase, e).start()

    def collect_roots(phase):
        wait_bytes(roots.at[phase, pl.ds(1, 7)], ro_recv.at[phase])
        factors = jnp.concatenate([roots[phase, e, :1] for e in range(8)], axis=0)
        tall[...] = jnp.transpose(jnp.concatenate([factors] * 16, axis=0))
        lane = lax.broadcasted_iota(jnp.int32, (16, 128), 1)
        for j in range(2):
            rows = tall[pl.ds(pl.multiple_of(32 * core + 16 * j, 16), 16), :]
            for owner_gx in range(8):
                column = jnp.sum(jnp.where(lane == lax.rem(gx + 8 - owner_gx, 8), rows, 0.0), axis=1, keepdims=True)
                scale[128 * j + 16 * owner_gx : 128 * j + 16 * owner_gx + 16] = jnp.broadcast_to(column, (16, 128))

    def normalized(f, mine, first_row):
        block = gathered(f, mine).astype(F32)
        held = lax.rem(gy + 16 - (2 * f + (core if mine else 1 - core)), 16)
        gains = stats[held, first_row : first_row + 4]
        gain = jnp.concatenate([gains[i : i + 1] for i in range(4)], axis=1)
        factor = scale[...]
        return (block * jnp.concatenate([factor] * 4, axis=1) * gain).astype(BF)

    def gather_copy(name, v):
        src, dst, count, level, sign, arrival = GATHER[name]
        return remote(
            ag.at[v, pl.ds(src, count)], ag.at[v, pl.ds(dst, count)], ag_send.at[v], ag_recv.at[v, arrival],
            toward(v, level, sign),
        )

    def px_copy(j, k):
        return remote(
            ag.at[2 + j, pl.ds(16 * k, 16)], xb.at[j, pl.ds(16 * k, 16)], px_send.at[j], px_recv.at[j], partner
        )

    wave_a, wave_b, in_order = (0, 1), (2, 3), (0, 2, 1, 3)

    def units(body, which=in_order):
        for v in which:
            body(v)

    def gather_begin(v):
        for sign in (1, 3, 2):
            gather_copy(f"own1_{sign}", v).start()
        for sign in (1, 3):
            gather_copy(f"one3_0_{sign}", v).start()
        for sign in (1, 3, 2):
            gather_copy(f"own2_{sign}", v).start()

    def gather_start(v, *names):
        for n in names:
            gather_copy(n, v).start()

    def gather_arrive(v, *arrivals):
        for a in arrivals:
            wait_bytes(ag.at[v, pl.ds(0, ARRIVING[a])], ag_recv.at[v, a])

    def t1(v):
        gather_arrive(v, 0)
        gather_start(v, "row2_1", "row2_3", "row2_2", "row3_0_1", "row3_0_3")

    def t2(v):
        gather_arrive(v, 1)
        for k in (1, 2, 3):
            gather_start(v, f"one3_{k}_1", f"one3_{k}_3")

    def t3(v):
        gather_arrive(v, 4, 8)
        gather_start(v, "pass3_0_3", "pass3_0_1")

    def t4(v):
        gather_arrive(v, 2)
        for k in (1, 2, 3):
            gather_start(v, f"row3_{k}_1", f"row3_{k}_3")
        if v >= 2:
            px_copy(v - 2, 0).start()

    def passing(v):
        for k in (1, 2, 3):
            gather_arrive(v, 4 + k, 8 + k)
            gather_start(v, f"pass3_{k}_3", f"pass3_{k}_1")
        if v >= 2:
            px_copy(v - 2, 1).start()
            px_copy(v - 2, 2).start()

    def passing_k(k):
        def step(v):
            gather_arrive(v, 4 + k, 8 + k)
            gather_start(v, f"pass3_{k}_3", f"pass3_{k}_1")
            if v >= 2 and k == 3:
                px_copy(v - 2, 1).start()
                px_copy(v - 2, 2).start()

        return step

    def t5(v):
        gather_arrive(v, 3)
        if v >= 2:
            px_copy(v - 2, 3).start()

    def gather_own():
        for v in (2, 3, 0, 1):
            t5(v)

    def gather_other():
        for j in range(2):
            wait_bytes(xb.at[j], px_recv.at[j])

    def gather_drain():
        for v in range(4):
            blocks = ag.at[v, pl.ds(0, 63)]
            pltpu.make_async_copy(blocks, blocks, ag_send.at[v]).wait()
        for j in range(2):
            pltpu.make_async_copy(xb.at[j], xb.at[j], px_send.at[j]).wait()

    def gathered(f, mine):
        pieces = []
        for j in range(2):
            for at in places(unit_strides[j] if mine else other_strides[j], f):
                pieces.append(ag[j, at] if mine else xb[j, at])
        return jnp.concatenate(pieces, axis=0)

    def feature_columns(f, mine):
        return columns(f, core if mine else 1 - core)

    def scatter_copy(name, v):
        src, dst, count, level, sign, arrival = SCATTER[name]
        return remote(
            sb.at[v, pl.ds(src, count)], rb.at[v, pl.ds(dst, count)], rs_send.at[v], rs_recv.at[v, arrival],
            toward(v, level, sign),
        )

    def rs_start(v, *names):
        for n in names:
            scatter_copy(n, v).start()

    def rs_arrive(v, *arrivals):
        for a in arrivals:
            blocks = rb.at[v, pl.ds(0, SUMMED[a])]
            pltpu.make_async_copy(blocks, blocks, rs_recv.at[v, a]).wait()

    def cast(v, src, count=4):
        sb[v, pl.ds(src, count)] = part[v, pl.ds(src, count)].astype(BF)

    def cast_sum(v, src, place_at, count=4):
        sb[v, pl.ds(src, count)] = (
            part[v, pl.ds(src, count)] + rb[v, pl.ds(place_at, count)].astype(F32)
        ).astype(BF)

    def scatter_far(v):
        for k in (3, 1, 2, 0):
            cast(v, 48 + 4 * k)
            rs_start(v, f"far3_{k}")

    def scatter_near(v):
        for k in (3, 2):
            cast(v, 32 + 4 * k)
            rs_start(v, f"down3_{k}")
        cast(v, 16 + 4 * 1)
        rs_start(v, "up3_1")

    def s1(v):
        for k in (3, 2):
            rs_arrive(v, k)
            cast_sum(v, 16 + 4 * k, 4 * (3 - k))
            rs_start(v, f"up3_{k}")
        for k in (1, 0):
            rs_arrive(v, k)
            cast_sum(v, 32 + 4 * k, 8 + 4 * (1 - k))
            rs_start(v, f"down3_{k}")
        cast(v, 16)
        rs_start(v, "up3_0")

    def total3(v, k):
        rs_arrive(v, 4 + k)
        return (
            part[v, pl.ds(4 * k, 4)]
            + rb[v, pl.ds(16 + 4 * k, 4)].astype(F32)
            + rb[v, pl.ds(32 + 4 * k, 4)].astype(F32)
        )

    def s2(k):
        def step(v):
            sb[v, pl.ds(4 * k, 4)] = total3(v, k).astype(BF)
            rs_start(v, f"to2_{k}")

        return step

    def s3(v):
        total = total3(v, 0)
        rs_arrive(v, 8)
        for place_at in (48, 52, 56):
            total = total + rb[v, pl.ds(place_at, 4)].astype(F32)
        part[v, 0] = total[0]
        sb[v, 1:4] = total[1:].astype(BF)
        rs_start(v, "to1_1", "to1_2", "to1_3")

    def final_sum(v):
        rs_arrive(v, 9)
        total = part[v, 0]
        for place_at in (60, 61, 62):
            total = total + rb[v, place_at].astype(F32)
        return total

    def scatter_drain():
        for v in range(4):
            blocks = sb.at[v, pl.ds(0, 63)]
            pltpu.make_async_copy(blocks, blocks, rs_send.at[v]).wait()

    def spread(wave, f, product):
        for j, v in enumerate((2 * wave, 2 * wave + 1)):
            for i, at in enumerate(places(unit_strides[v], f)):
                row = 128 * j + 16 * i
                part[v, at] = product[row : row + 16]

    for v in range(4):
        ag[v, 0] = tok_ref[token_unit(v), :]
    square_sums = square_row(tok_ref[...].astype(F32))
    stats[0] = jnp.zeros((16, 128), F32)
    stats[0, 0:1] = square_sums
    stats[0, 1:2, 0:32] = segment_ref[...].astype(F32).reshape(1, 32)
    stats[0, 4:8] = gain_ref[...].astype(F32).reshape(4, 128)
    stats[0, 8:12] = ffn_gain_ref[...].astype(F32).reshape(4, 128)
    bias[0:8] = query_bias_ref[...].astype(F32).reshape(8, 128)
    bias[8:9] = value_bias_ref[...].astype(F32).reshape(1, 128)
    pl.semaphore_wait(barrier, len(greeted))
    units(gather_begin)
    for d in range(1, 16):
        stat_copy(0, d).start()
    for copy in remote_copies[:3]:
        copy.start()

    units(t1)
    spread_roots(0)
    for copy in out_remote + remote_copies[3:] + down_remote:
        copy.start()
    units(t2)
    units(t3)
    units(t4)
    for k in (1, 2, 3):
        units(passing_k(k))
    collect_roots(0)
    gather_own()
    documents = jnp.sum(
        jnp.where(lax.broadcasted_iota(jnp.int32, (16, 16, 128), 1) == 1, stats[...], 0.0), axis=1
    )
    for copy in local_copies[:3] + table_copies:
        copy.wait()
    for copy in remote_copies[:3]:
        copy.wait_recv()

    acckv[...] = jnp.zeros_like(acckv)

    for mine in (True, False):
        if not mine:
            gather_other()

        @pl.loop(0, 8, unroll=4)
        def _(f):
            cols = feature_columns(f, mine)
            weights = [wkv[side, kind, :, cols].astype(F32) for kind in range(2) for side in range(2)]
            weights = jnp.concatenate(weights, axis=0).astype(BF)
            block = normalized(f, mine, 4)
            an[2 * f + (0 if mine else 1)] = block
            acckv[...] += dot_nt(weights, block)

    kvall[core, chip] = acckv[...]

    def kv_copy(d):
        there = lax.rem(gy + 2 * d, 16)
        return remote(kvall.at[core, chip], kvall.at[core, chip], kv_send, kv_recv, (gx, there))

    for d in range(1, 8):
        kv_copy(d).start()

    accq[...] = jnp.zeros_like(accq)

    @pl.loop(0, 8, unroll=4)
    def _(f):
        for mine in (True, False):
            cols = feature_columns(f, mine)
            weights = jnp.concatenate([wq[0, :, cols], wq[1, :, cols]], axis=0)
            accq[...] += dot_nt(an[2 * f + (0 if mine else 1)], weights)

    query = accq[...] + bias[pl.ds(chip, 1), :]
    own_rows = pl.ds(pl.multiple_of(256 * core, 256), 256)
    turned = jnp.concatenate([query[:, 64:], query[:, :64]], axis=1)
    queries = (query * cosq[own_rows, :] + turned * sinq[own_rows, :]).astype(BF)

    def token_parts(index, own_core):
        item, low, along, row = (
            (index >> 7) & 1, (index >> 6) & 1, (index >> 4) & 3, index & 15,
        )
        return 256 * low + 64 * along + 32 * own_core + 16 * item + row, 8 * low + 2 * along + own_core, 16 * item + row

    def owner(index):
        held = gy - index
        return jnp.where(held < 0, held + 16, held)

    docs = documents.astype(BF)
    key_index = lax.broadcasted_iota(jnp.int32, (128, 512), 1)
    _, _, key_lane = token_parts(key_index, key_index >> 8)
    pick = jnp.where(lax.broadcasted_iota(jnp.int32, (128, 512), 0) == key_lane, 1.0, 0.0).astype(BF)
    key_docs = dot_nn(docs, pick)
    key_index = lax.broadcasted_iota(jnp.int32, (16, 512), 1)
    _, key_owner, _ = token_parts(key_index, key_index >> 8)
    is_owner = owner(lax.broadcasted_iota(jnp.int32, (16, 512), 0)) == key_owner
    key_docs = jnp.sum(jnp.where(is_owner, key_docs, 0.0), axis=0, keepdims=True)
    query_index = lax.broadcasted_iota(jnp.int32, (256, 128), 0)
    _, _, query_lane = token_parts(query_index, core)
    pick = jnp.where(lax.broadcasted_iota(jnp.int32, (256, 128), 1) == query_lane, 1.0, 0.0).astype(BF)
    query_docs = dot_nt(pick, docs)
    query_index = lax.broadcasted_iota(jnp.int32, (256, 16), 0)
    _, query_owner, _ = token_parts(query_index, core)
    is_owner = owner(lax.broadcasted_iota(jnp.int32, (256, 16), 1)) == query_owner
    query_docs = jnp.sum(jnp.where(is_owner, query_docs, 0.0), axis=1, keepdims=True)
    key_index = lax.broadcasted_iota(jnp.int32, (256, 512), 1)
    key_position, _, _ = token_parts(key_index, key_index >> 8)
    query_position, _, _ = token_parts(lax.broadcasted_iota(jnp.int32, (256, 512), 0), core)
    allowed = (key_position <= query_position) & (key_docs == query_docs)

    value_bias = jnp.transpose(jnp.broadcast_to(bias[8:9], (128, 128)))
    value_bias = jnp.concatenate([value_bias] * 2, axis=1)
    wait_bytes(kvall.at[core, pl.ds(0, 7)], kv_recv)
    forward = remote(kvall.at[core], kvall.at[core], kf_send, kf_recv, partner)
    forward.start()
    remote(kvall.at[1 - core], kvall.at[1 - core], kf_send, kf_recv, partner).wait_recv()
    key_parts, value_parts = [], []
    for side in range(2):
        held = kvall[side]
        keys = held[:, :16].reshape(128, 256)
        first, second = keys[:64], keys[64:]
        cosine, sine = cosk[:, 256 * side : 256 * side + 256], sink[:, 256 * side : 256 * side + 256]
        key_parts.append(
            jnp.concatenate([first * cosine - second * sine, second * cosine + first * sine], axis=0).astype(BF)
        )
        value_parts.append((held[:, 16:].reshape(128, 256) + value_bias).astype(BF))
    keys = jnp.concatenate(key_parts, axis=1)
    values = jnp.concatenate(value_parts, axis=1)
    scores = dot_nn(queries, keys) / math.sqrt(HEAD_DIM)
    scores = jnp.where(allowed, scores, -jnp.inf)
    weights = jnp.where(allowed, jnp.exp(scores - jnp.max(scores, axis=1, keepdims=True)), 0.0)
    denominator = jnp.sum(weights, axis=1, keepdims=True)
    att[0] = (dot_nt(weights.astype(BF), values) / denominator).astype(BF)
    send_att = remote(att.at[0], att.at[1], at_send, at_recv, partner)
    send_att.start()

    wait_bytes(wo.at[core], ol_sem)
    wait_bytes(wo.at[1 - core], or_sem)

    def project_out(wave):
        @pl.loop(0, 8, unroll=4)
        def _(f):
            weights = jnp.concatenate([wo[0, f], wo[1, f]], axis=0)
            spread(wave, f, dot_nn(att[wave], weights))

    def finish_first(v):
        block = (tok_ref[token_unit(v), :].astype(F32) + final_sum(v)).astype(BF)
        resid[token_unit(v), :] = block
        ag[v, 0] = block
        gather_begin(v)

    project_out(0)
    units(scatter_far, wave_a)
    send_att.wait_recv()
    project_out(1)
    units(scatter_far, wave_b)
    units(scatter_near)
    gather_drain()
    units(s1)
    for k in (3, 2, 1):
        units(s2(k))
    units(s3)
    units(finish_first)
    square_sums = square_row(resid[...].astype(F32))
    row = lax.broadcasted_iota(jnp.int32, (8, 128), 0)
    sums[0] = jnp.where(row == 0, square_sums, jnp.zeros((8, 128), F32))
    for d in range(1, 16):
        stat_copy(1, d).start()
    units(t1)
    units(t2)
    spread_roots(1)
    units(t3)
    scatter_drain()
    units(t4)
    for k in (1, 2, 3):
        units(passing_k(k))
    collect_roots(1)
    gather_own()
    for copy in local_copies[3:]:
        copy.wait()
    for copy in remote_copies[3:]:
        copy.wait_recv()

    accg[...] = jnp.zeros_like(accg)
    accu[...] = jnp.zeros_like(accu)

    for mine in (True, False):
        if not mine:
            gather_other()

        @pl.loop(0, 8, unroll=4)
        def _(f):
            block = normalized(f, mine, 8)
            cols = feature_columns(f, mine)
            for side in range(2):
                accg[side] += dot_nt(block, wg[side, :, cols])
                accu[side] += dot_nt(block, wu[side, :, cols])

    for side in range(2):
        gate = accg[side]
        hid[0, side] = (gate / (1.0 + jnp.exp(-gate)) * accu[side]).astype(BF)
    send_hid = remote(hid.at[0], hid.at[1], hd_send, hd_recv, partner)
    send_hid.start()
    wait_bytes(wd.at[core], dl_sem)
    wait_bytes(wd.at[1 - core], dr_sem)

    def project_down(wave):
        @pl.loop(0, 8, unroll=4)
        def _(f):
            spread(wave, f, dot_nn(hid[wave, 0], wd[0, f]) + dot_nn(hid[wave, 1], wd[1, f]))

    def finish_second(v):
        out_ref[token_unit(v), :] = (resid[token_unit(v), :].astype(F32) + final_sum(v)).astype(BF)

    project_down(0)
    units(scatter_far, wave_a)
    send_hid.wait_recv()
    project_down(1)
    units(scatter_far, wave_b)
    units(scatter_near)
    gather_drain()
    units(s1)
    for k in (3, 2, 1):
        units(s2(k))
    units(s3)
    units(finish_second)
    scatter_drain()

    wait_bytes(stats.at[pl.ds(1, 15)], st_send)
    wait_bytes(sums.at[pl.ds(1, 15)], su_send)
    for phase in range(2):
        wait_bytes(roots.at[phase, pl.ds(1, 7)], ro_send.at[phase])
    wait_bytes(kvall.at[core, pl.ds(0, 7)], kv_send)
    forward.wait_send()
    send_att.wait_send()
    send_hid.wait_send()
    for copy in remote_copies:
        copy.wait_send()
    wait_bytes(wo.at[core], os_sem)
    wait_bytes(wd.at[core], ds_sem)


def rotary_tables():
    half = HEAD_DIM // 2
    frequency = np.power(np.float32(ROTARY_BASE), -(np.arange(half, dtype=np.float32) * 2.0) / HEAD_DIM).astype(np.float32)
    index = np.arange(TOKENS)
    side, item, low, along, row = index >> 8, (index >> 7) & 1, (index >> 6) & 1, (index >> 4) & 3, index & 15
    position = 256 * low + 64 * along + 32 * side + 16 * item + row
    angles = (position.astype(np.float32)[:, None] * frequency[None, :]).astype(np.float32)
    cosine, sine = np.cos(angles).astype(np.float32), np.sin(angles).astype(np.float32)
    return (
        np.ascontiguousarray(cosine.T), np.ascontiguousarray(sine.T),
        np.concatenate([cosine, cosine], axis=1), np.concatenate([-sine, sine], axis=1),
    )


def shards(
    tokens, segment_ids, attn_gain, query_weight, query_bias, key_weight, value_weight, value_bias,
    out_weight, ffn_gain, gate_weight, up_weight, down_weight,
):
    units = gate_weight.shape[0]
    any_spec = pl.BlockSpec(memory_space=pl.ANY)
    vmem_spec = pl.BlockSpec(memory_space=pltpu.VMEM)
    dma = pltpu.SemaphoreType.DMA
    return pl.pallas_call(
        kernel,
        out_shape=jax.ShapeDtypeStruct((64, BLOCK), BF),
        in_specs=[vmem_spec] * 6 + [any_spec] * 11,
        out_specs=vmem_spec,
        scratch_shapes=[
            pltpu.VMEM((2, 64, MODEL), BF),
            pltpu.VMEM((2, 2, 8, MODEL), BF),
            pltpu.VMEM((2, 8, 64, BLOCK), BF),
            pltpu.VMEM((2, units, MODEL), BF),
            pltpu.VMEM((2, units, MODEL), BF),
            pltpu.VMEM((2, 8, units, BLOCK), BF),
            pltpu.VMEM((64, 512), F32),
            pltpu.VMEM((64, 512), F32),
            pltpu.VMEM((512, 128), F32),
            pltpu.VMEM((512, 128), F32),
            pltpu.VMEM((4, 64, ROWS, BLOCK), BF),
            pltpu.VMEM((2, 64, ROWS, BLOCK), BF),
            pltpu.VMEM((16, 256, BLOCK), BF),
            pltpu.VMEM((4, 64, ROWS, BLOCK), F32),
            pltpu.VMEM((4, 64, ROWS, BLOCK), BF),
            pltpu.VMEM((4, 63, ROWS, BLOCK), BF),
            pltpu.VMEM((16, 16, 128), F32),
            pltpu.VMEM((16, 8, 128), F32),
            pltpu.VMEM((2, 8, 8, 128), F32),
            pltpu.VMEM((128, 128), F32),
            pltpu.VMEM((256, 128), F32),
            pltpu.VMEM((16, 128), F32),
            pltpu.VMEM((2, 8, 32, 256), F32),
            pltpu.VMEM((2, 256, 128), BF),
            pltpu.VMEM((2, 2, 256, units), BF),
            pltpu.VMEM((256, 128), F32),
            pltpu.VMEM((32, 256), F32),
            pltpu.VMEM((2, 256, units), F32),
            pltpu.VMEM((2, 256, units), F32),
            pltpu.VMEM((64, BLOCK), BF),
            dma((4,)), dma((4, 12)),
            dma((2,)), dma((2,)),
            dma((4,)), dma((4, 10)),
            dma, dma, dma, dma, dma((2,)), dma((2,)),
            dma, dma,
            dma, dma, dma, dma, dma, dma,
            dma((9,)), dma((5,)), dma((5,)),
            dma, dma, dma, dma, dma, dma,
        ],
        compiler_params=pltpu.CompilerParams(
            collective_id=0, has_side_effects=True, vmem_limit_bytes=60 * 1024 * 1024
        ),
        name="layer",
    )(
        tokens, segment_ids, attn_gain, ffn_gain, query_bias, value_bias, query_weight, key_weight, value_weight,
        out_weight, gate_weight, up_weight, down_weight, *rotary_tables(),
    )


def solution(mesh):
    placed = (
        P("gx", "gy"),
        P("gy"),
        P("gy"),
        P(("gx", "gy"), None),
        P("gx"),
        P(("gx", "gy"), None),
        P(("gx", "gy"), None),
        P("gx"),
        P(("gx", "gy"), None),
        P("gy"),
        P(("gx", "gy"), None),
        P(("gx", "gy"), None),
        P(("gx", "gy"), None),
    )
    return jax.shard_map(
        shards, mesh=mesh, in_specs=placed, out_specs=P("gx", "gy"), check_vma=False
    )
```

```python
import functools
import math

import jax
import jax.numpy as jnp
import numpy as np
from jax import lax
from jax.experimental import pallas as pl
from jax.experimental.pallas import tpu as pltpu
from jax.sharding import PartitionSpec as P


HEAD_DIM = 128
EPSILON = 1e-06
ROTARY_BASE = 1000000.0
TOKENS = 512
MODEL = 8192
BLOCK = 512
ROWS = 16
BF = jnp.bfloat16
F32 = jnp.float32
MESH = pl.DeviceIdType.MESH


def dot_nt(left, right):
    return lax.dot_general(left, right, (((1,), (1,)), ((), ())), preferred_element_type=F32)


def dot_nn(left, right):
    return lax.dot_general(left, right, (((1,), (0,)), ((), ())), preferred_element_type=F32)


GATHER = {}
for _sign, _seen in ((1, 2), (3, 1), (2, 3)):
    GATHER[f"own1_{_sign}"] = (0, _seen, 1, 1, _sign, 0)
    GATHER[f"own2_{_sign}"] = (0, 4 * _seen, 1, 2, _sign, 1)
    GATHER[f"row2_{_sign}"] = (1, 4 * _seen + 1, 3, 2, _sign, 2)
for _sign, _seen in ((1, 2), (3, 1)):
    for _k in range(4):
        GATHER[f"one3_{_k}_{_sign}"] = (4 * _k, 16 * _seen + 4 * _k, 1, 3, _sign, 4 * _seen + _k)
        GATHER[f"row3_{_k}_{_sign}"] = (4 * _k + 1, 16 * _seen + 4 * _k + 1, 3, 3, _sign, 4 * _seen + _k)
for _k in range(4):
    GATHER[f"pass3_{_k}_3"] = (16 + 4 * _k, 48 + 4 * _k, 2, 3, 3, 3)
    GATHER[f"pass3_{_k}_1"] = (32 + 4 * _k + 2, 48 + 4 * _k + 2, 2, 3, 1, 3)
ARRIVING = {0: 3, 1: 3, 2: 9, 3: 16, **{i: 4 for i in range(4, 12)}}

SCATTER = {}
for _k in (3, 2):
    SCATTER[f"far3_{_k}"] = (48 + 4 * _k, 4 * (3 - _k), 4, 3, 1, _k)
for _k in (1, 0):
    SCATTER[f"far3_{_k}"] = (48 + 4 * _k, 8 + 4 * (1 - _k), 4, 3, 3, _k)
for _k in range(4):
    SCATTER[f"up3_{_k}"] = (16 + 4 * _k, 16 + 4 * _k, 4, 3, 1, 4 + _k)
    SCATTER[f"down3_{_k}"] = (32 + 4 * _k, 32 + 4 * _k, 4, 3, 3, 4 + _k)
for _k, _sign in ((1, 1), (2, 3), (3, 2)):
    SCATTER[f"to2_{_k}"] = (4 * _k, 44 + 4 * _k, 4, 2, _sign, 8)
    SCATTER[f"to1_{_k}"] = (_k, 59 + _k, 1, 1, _sign, 9)
SUMMED = {**{i: 4 for i in range(4)}, **{i: 8 for i in range(4, 8)}, 8: 12, 9: 3}


def one_hot3(value):
    second, third = lax.rem(value, 2), lax.div(value, 2)
    return 1 - second - third, second, third


def kernel(
    tok_ref, segment_ref, gain_ref, ffn_gain_ref, query_bias_ref, value_bias_ref,
    wq_hbm, wk_hbm, wv_hbm, wo_hbm, wg_hbm, wu_hbm, wd_hbm,
    cosk_hbm, sink_hbm, cosq_hbm, sinq_hbm,
    out_ref,
    wq, wkv, wo, wg, wu, wd, cosk, sink, cosq, sinq,
    ag, xb, an, part, sb, rb, stats, sums, roots, tall, scale, bias, kvall, att, hid, accq, acckv, accg, accu, resid,
    ag_send, ag_recv, px_send, px_recv, rs_send, rs_recv, st_send, st_recv, su_send, su_recv, ro_send, ro_recv,
    kv_send, kv_recv, kf_send, kf_recv, at_send, at_recv, hd_send, hd_recv,
    wl_sem, ws_sem, wr_sem, ol_sem, os_sem, or_sem, dl_sem, ds_sem, dr_sem,
):
    gx, gy = lax.axis_index("gx"), lax.axis_index("gy")
    x, y_lo = lax.rem(gx, 4), lax.div(gx, 4)
    core, z, y_hi = lax.rem(gy, 2), lax.rem(lax.div(gy, 2), 4), lax.div(gy, 8)
    y = y_hi * 2 + y_lo
    chip = y_hi * 4 + z
    partner = (gx, gy + 1 - 2 * core)

    def device(x, y, z):
        return (lax.rem(y, 2) * 4 + x, lax.div(y, 2) * 8 + z * 2 + core)

    own_orders = [(lax.rem(bulk + 2, 3), 0) for bulk in (core, 2 * core, 1 - core, 2 - core)]
    other_orders = [(lax.rem(bulk + 2, 3), 0) for bulk in (core, 1 + core)]

    def neighbour(v, level, sign):
        bulk, choice = own_orders[v]
        step = {3: 0, 2: 1 + choice, 1: 2 - choice}[level]
        e0, e1, e2 = one_hot3(lax.rem(jnp.int32(bulk + step), 3))
        return device(lax.rem(x + sign * e0, 4), lax.rem(y + sign * e1, 4), lax.rem(z + sign * e2, 4))

    neighbours = {
        (v, level, sign): neighbour(v, level, sign) for v in range(4) for level in (1, 2, 3) for sign in (1, 2, 3)
    }

    def toward(v, level, sign):
        return neighbours[v, level, sign]

    def slot(position, mine):
        d = lax.rem(position - mine + 4, 4)
        return d + lax.div(d, 2) - 2 * lax.div(d, 3)

    def strides(order):
        bulk, choice = order
        result = []
        for axis in range(3):
            e0, e1, e2 = one_hot3(lax.rem(jnp.int32(axis + 3 - bulk), 3))
            result.append(16 * e0 + (4 - 3 * choice) * e1 + (1 + 3 * choice) * e2)
        return result

    x_slots = [slot(position, x) for position in range(4)]
    unit_strides = [strides(order) for order in own_orders]
    other_strides = [strides(order) for order in other_orders]

    def places(stride, f):
        fy, fz = lax.div(f, 4), lax.rem(f, 4)
        z_part = stride[2] * slot(fz, z)
        y_parts = [stride[1] * slot(fy * 2 + ty, y) + z_part for ty in range(2)]
        return [y_parts[ty] + stride[0] * x_slots[tx] for ty in range(2) for tx in range(4)]

    def remote(src, dst, send, recv, target):
        return pltpu.make_async_remote_copy(
            src_ref=src, dst_ref=dst, send_sem=send, recv_sem=recv, device_id=target, device_id_type=MESH
        )

    barrier = pltpu.get_barrier_semaphore()
    greeted = (
        [device(x, lax.rem(y + 3 + 2 * y_lo, 4), z)]
        + [(lax.rem(gx + e, 8), gy) for e in range(1, 8)]
        + [(gx, lax.rem(gy + d, 16)) for d in range(1, 16)]
    )
    for target in greeted:
        pl.semaphore_signal(barrier, inc=1, device_id=target, device_id_type=MESH)

    whole = (
        (wq_hbm, wq.at[core]), (wk_hbm, wkv.at[core, 0]), (wv_hbm, wkv.at[core, 1]),
        (wg_hbm, wg.at[core]), (wu_hbm, wu.at[core]),
    )
    tables = ((cosk_hbm, cosk), (sink_hbm, sink), (cosq_hbm, cosq), (sinq_hbm, sinq))
    local_copies = [
        pltpu.make_async_copy(src, dst, wl_sem.at[i]) for i, (src, dst) in enumerate(whole)
    ]
    table_copies = [
        pltpu.make_async_copy(src, dst, wl_sem.at[5 + i]) for i, (src, dst) in enumerate(tables)
    ]
    remote_copies = [
        remote(src, dst, ws_sem.at[i], wr_sem.at[i], partner) for i, (src, dst) in enumerate(whole)
    ]
    def wait_bytes(ref, semaphore):
        pltpu.make_async_copy(ref, ref, semaphore).wait()

    columns = lambda f, side: pl.ds(pl.multiple_of((2 * f + side) * BLOCK, BLOCK), BLOCK)
    out_local = [pltpu.make_async_copy(wo_hbm.at[:, columns(f, core)], wo.at[core, f], ol_sem) for f in range(8)]
    down_local = [pltpu.make_async_copy(wd_hbm.at[:, columns(f, core)], wd.at[core, f], dl_sem) for f in range(8)]
    out_remote = [remote(wo_hbm.at[:, columns(f, 1 - core)], wo.at[core, f], os_sem, or_sem, partner) for f in range(8)]
    down_remote = [remote(wd_hbm.at[:, columns(f, 1 - core)], wd.at[core, f], ds_sem, dr_sem, partner) for f in range(8)]
    for copy in local_copies[:3] + table_copies + out_local + local_copies[3:] + down_local:
        copy.start()

    def token_unit(v):
        return pl.ds(pl.multiple_of(16 * lax.rem(v + 2 * core, 4), 16), 16)

    def square_row(values):
        squares = values * values
        folded = squares[:, :128] + squares[:, 128:256] + squares[:, 256:384] + squares[:, 384:]
        row = jnp.sum(jnp.transpose(folded), axis=0, keepdims=True)
        return jnp.concatenate([row, jnp.zeros((1, 64), F32)], axis=1)

    def stat_copy(phase, d):
        there = (gx, lax.rem(gy + d, 16))
        if phase == 0:
            return remote(stats.at[0], stats.at[d], st_send, st_recv, there)
        return remote(sums.at[0], sums.at[d], su_send, su_recv, there)

    def root_copy(phase, e):
        return remote(
            roots.at[phase, 0], roots.at[phase, e], ro_send.at[phase], ro_recv.at[phase], (lax.rem(gx + e, 8), gy)
        )

    def spread_roots(phase):
        wait_bytes(*((stats.at[pl.ds(1, 15)], st_recv) if phase == 0 else (sums.at[pl.ds(1, 15)], su_recv)))
        summed = jnp.sum(stats[:, :8] if phase == 0 else sums[...], axis=0)
        inverse = lax.rsqrt(summed / MODEL + EPSILON)
        roots[phase, 0] = inverse
        for e in range(1, 8):
            root_copy(phase, e).start()

    def collect_roots(phase):
        wait_bytes(roots.at[phase, pl.ds(1, 7)], ro_recv.at[phase])
        factors = jnp.concatenate([roots[phase, e, :1] for e in range(8)], axis=0)
        tall[...] = jnp.transpose(jnp.concatenate([factors] * 16, axis=0))
        lane = lax.broadcasted_iota(jnp.int32, (16, 128), 1)
        for j in range(2):
            rows = tall[pl.ds(pl.multiple_of(32 * core + 16 * j, 16), 16), :]
            for owner_gx in range(8):
                column = jnp.sum(jnp.where(lane == lax.rem(gx + 8 - owner_gx, 8), rows, 0.0), axis=1, keepdims=True)
                scale[128 * j + 16 * owner_gx : 128 * j + 16 * owner_gx + 16] = jnp.broadcast_to(column, (16, 128))

    def normalized(f, mine, first_row):
        block = gathered(f, mine).astype(F32)
        held = lax.rem(gy + 16 - (2 * f + (core if mine else 1 - core)), 16)
        gains = stats[held, first_row : first_row + 4]
        gain = jnp.concatenate([gains[i : i + 1] for i in range(4)], axis=1)
        factor = scale[...]
        return (block * jnp.concatenate([factor] * 4, axis=1) * gain).astype(BF)

    def gather_copy(name, v):
        src, dst, count, level, sign, arrival = GATHER[name]
        return remote(
            ag.at[v, pl.ds(src, count)], ag.at[v, pl.ds(dst, count)], ag_send.at[v], ag_recv.at[v, arrival],
            toward(v, level, sign),
        )

    def px_copy(j, k):
        return remote(
            ag.at[2 + j, pl.ds(16 * k, 16)], xb.at[j, pl.ds(16 * k, 16)], px_send.at[j], px_recv.at[j], partner
        )

    wave_a, wave_b, in_order = (0, 1), (2, 3), (0, 2, 1, 3)

    def units(body, which=in_order):
        for v in which:
            body(v)

    def gather_begin(v):
        for sign in (1, 3, 2):
            gather_copy(f"own1_{sign}", v).start()

    def gather_more(v):
        for sign in (1, 3):
            gather_copy(f"one3_0_{sign}", v).start()
        for sign in (1, 3, 2):
            gather_copy(f"own2_{sign}", v).start()

    def gather_start(v, *names):
        for n in names:
            gather_copy(n, v).start()

    def gather_arrive(v, *arrivals):
        for a in arrivals:
            wait_bytes(ag.at[v, pl.ds(0, ARRIVING[a])], ag_recv.at[v, a])

    def t1(v):
        gather_arrive(v, 0)
        gather_start(v, "row2_1", "row2_3", "row2_2", "row3_0_1", "row3_0_3")

    def t2(v):
        gather_arrive(v, 1)
        for k in (1, 2, 3):
            gather_start(v, f"one3_{k}_1", f"one3_{k}_3")

    def t3(v):
        gather_arrive(v, 4, 8)
        gather_start(v, "pass3_0_3", "pass3_0_1")

    def t4(v):
        gather_arrive(v, 2)
        for k in (1, 2, 3):
            gather_start(v, f"row3_{k}_1", f"row3_{k}_3")
        if v >= 2:
            px_copy(v - 2, 0).start()

    def passing(v):
        for k in (1, 2, 3):
            gather_arrive(v, 4 + k, 8 + k)
            gather_start(v, f"pass3_{k}_3", f"pass3_{k}_1")
        if v >= 2:
            px_copy(v - 2, 1).start()
            px_copy(v - 2, 2).start()

    def passing_k(k):
        def step(v):
            gather_arrive(v, 4 + k, 8 + k)
            gather_start(v, f"pass3_{k}_3", f"pass3_{k}_1")
            if v >= 2 and k == 3:
                px_copy(v - 2, 1).start()
                px_copy(v - 2, 2).start()

        return step

    def t5(v):
        gather_arrive(v, 3)
        if v >= 2:
            px_copy(v - 2, 3).start()

    def gather_own():
        for v in (2, 3, 0, 1):
            t5(v)

    def gather_other():
        for j in range(2):
            wait_bytes(xb.at[j], px_recv.at[j])

    def gather_drain():
        for v in range(4):
            blocks = ag.at[v, pl.ds(0, 63)]
            pltpu.make_async_copy(blocks, blocks, ag_send.at[v]).wait()
        for j in range(2):
            pltpu.make_async_copy(xb.at[j], xb.at[j], px_send.at[j]).wait()

    def gathered(f, mine):
        pieces = []
        for j in range(2):
            for at in places(unit_strides[j] if mine else other_strides[j], f):
                pieces.append(ag[j, at] if mine else xb[j, at])
        return jnp.concatenate(pieces, axis=0)

    def feature_columns(f, mine):
        return columns(f, core if mine else 1 - core)

    def scatter_copy(name, v):
        src, dst, count, level, sign, arrival = SCATTER[name]
        return remote(
            sb.at[v, pl.ds(src, count)], rb.at[v, pl.ds(dst, count)], rs_send.at[v], rs_recv.at[v, arrival],
            toward(v, level, sign),
        )

    def rs_start(v, *names):
        for n in names:
            scatter_copy(n, v).start()

    def rs_arrive(v, *arrivals):
        for a in arrivals:
            blocks = rb.at[v, pl.ds(0, SUMMED[a])]
            pltpu.make_async_copy(blocks, blocks, rs_recv.at[v, a]).wait()

    def cast(v, src, count=4):
        sb[v, pl.ds(src, count)] = part[v, pl.ds(src, count)].astype(BF)

    def cast_sum(v, src, place_at, count=4):
        sb[v, pl.ds(src, count)] = (
            part[v, pl.ds(src, count)] + rb[v, pl.ds(place_at, count)].astype(F32)
        ).astype(BF)

    def scatter_far(which):
        for k in (3, 1, 2, 0):
            for v in which:
                cast(v, 48 + 4 * k)
                rs_start(v, f"far3_{k}")

    def scatter_near():
        for v in in_order:
            cast(v, 32 + 4 * 3)
            rs_start(v, "down3_3")
        for v in in_order:
            cast(v, 16 + 4 * 1)
            rs_start(v, "up3_1")
        for v in in_order:
            cast(v, 32 + 4 * 2)
            rs_start(v, "down3_2")

    def scatter_relay():
        for k, other in ((3, 1), (2, 0)):
            for v in in_order:
                rs_arrive(v, k)
                cast_sum(v, 16 + 4 * k, 4 * (3 - k))
                rs_start(v, f"up3_{k}")
            for v in in_order:
                rs_arrive(v, other)
                cast_sum(v, 32 + 4 * other, 8 + 4 * (1 - other))
                rs_start(v, f"down3_{other}")
        for v in in_order:
            cast(v, 16)
            rs_start(v, "up3_0")

    def total3(v, k):
        rs_arrive(v, 4 + k)
        return (
            part[v, pl.ds(4 * k, 4)]
            + rb[v, pl.ds(16 + 4 * k, 4)].astype(F32)
            + rb[v, pl.ds(32 + 4 * k, 4)].astype(F32)
        )

    def s2(k):
        def step(v):
            sb[v, pl.ds(4 * k, 4)] = total3(v, k).astype(BF)
            rs_start(v, f"to2_{k}")

        return step

    def s3(v):
        total = total3(v, 0)
        rs_arrive(v, 8)
        for place_at in (48, 52, 56):
            total = total + rb[v, pl.ds(place_at, 4)].astype(F32)
        part[v, 0] = total[0]
        sb[v, 1:4] = total[1:].astype(BF)
        rs_start(v, "to1_1", "to1_2", "to1_3")

    def final_sum(v):
        rs_arrive(v, 9)
        total = part[v, 0]
        for place_at in (60, 61, 62):
            total = total + rb[v, place_at].astype(F32)
        return total

    def scatter_drain():
        for v in range(4):
            blocks = sb.at[v, pl.ds(0, 63)]
            pltpu.make_async_copy(blocks, blocks, rs_send.at[v]).wait()

    def spread(wave, f, product):
        for j, v in enumerate((2 * wave, 2 * wave + 1)):
            for i, at in enumerate(places(unit_strides[v], f)):
                row = 128 * j + 16 * i
                part[v, at] = product[row : row + 16]

    for v in range(4):
        ag[v, 0] = tok_ref[token_unit(v), :]
    square_sums = square_row(tok_ref[...].astype(F32))
    stats[0] = jnp.zeros((16, 128), F32)
    stats[0, 0:1] = square_sums
    stats[0, 1:2, 0:32] = segment_ref[...].astype(F32).reshape(1, 32)
    stats[0, 4:8] = gain_ref[...].astype(F32).reshape(4, 128)
    stats[0, 8:12] = ffn_gain_ref[...].astype(F32).reshape(4, 128)
    bias[0:8] = query_bias_ref[...].astype(F32).reshape(8, 128)
    bias[8:9] = value_bias_ref[...].astype(F32).reshape(1, 128)
    pl.semaphore_wait(barrier, len(greeted))
    units(gather_begin)
    units(gather_more)
    for d in range(1, 16):
        stat_copy(0, d).start()
    for copy in remote_copies[:3]:
        copy.start()

    units(t1)
    spread_roots(0)
    for copy in out_remote + remote_copies[3:] + down_remote:
        copy.start()
    units(t2)
    units(t4)
    units(t3)
    for k in (1, 2, 3):
        units(passing_k(k))
    collect_roots(0)
    gather_own()
    documents = jnp.sum(
        jnp.where(lax.broadcasted_iota(jnp.int32, (16, 16, 128), 1) == 1, stats[...], 0.0), axis=1
    )
    for copy in local_copies[:3] + table_copies:
        copy.wait()
    for copy in remote_copies[:3]:
        copy.wait_recv()

    acckv[...] = jnp.zeros_like(acckv)

    for mine in (True, False):
        if not mine:
            gather_other()

        @pl.loop(0, 8, unroll=4)
        def _(f):
            cols = feature_columns(f, mine)
            weights = [wkv[side, kind, :, cols].astype(F32) for kind in range(2) for side in range(2)]
            weights = jnp.concatenate(weights, axis=0).astype(BF)
            block = normalized(f, mine, 4)
            an[2 * f + (0 if mine else 1)] = block
            acckv[...] += dot_nt(weights, block)

    kvall[core, chip] = acckv[...]

    def kv_copy(d):
        there = lax.rem(gy + 2 * d, 16)
        return remote(kvall.at[core, chip], kvall.at[core, chip], kv_send, kv_recv, (gx, there))

    for d in range(1, 8):
        kv_copy(d).start()

    accq[...] = jnp.zeros_like(accq)

    @pl.loop(0, 8, unroll=4)
    def _(f):
        for mine in (True, False):
            cols = feature_columns(f, mine)
            weights = jnp.concatenate([wq[0, :, cols], wq[1, :, cols]], axis=0)
            accq[...] += dot_nt(an[2 * f + (0 if mine else 1)], weights)

    query = accq[...] + bias[pl.ds(chip, 1), :]
    own_rows = pl.ds(pl.multiple_of(256 * core, 256), 256)
    turned = jnp.concatenate([query[:, 64:], query[:, :64]], axis=1)
    queries = (query * cosq[own_rows, :] + turned * sinq[own_rows, :]).astype(BF)

    def token_parts(index, own_core):
        item, low, along, row = (
            (index >> 7) & 1, (index >> 6) & 1, (index >> 4) & 3, index & 15,
        )
        return 256 * low + 64 * along + 32 * own_core + 16 * item + row, 8 * low + 2 * along + own_core, 16 * item + row

    def owner(index):
        held = gy - index
        return jnp.where(held < 0, held + 16, held)

    docs = documents.astype(BF)
    key_index = lax.broadcasted_iota(jnp.int32, (128, 512), 1)
    _, _, key_lane = token_parts(key_index, key_index >> 8)
    pick = jnp.where(lax.broadcasted_iota(jnp.int32, (128, 512), 0) == key_lane, 1.0, 0.0).astype(BF)
    key_docs = dot_nn(docs, pick)
    key_index = lax.broadcasted_iota(jnp.int32, (16, 512), 1)
    _, key_owner, _ = token_parts(key_index, key_index >> 8)
    is_owner = owner(lax.broadcasted_iota(jnp.int32, (16, 512), 0)) == key_owner
    key_docs = jnp.sum(jnp.where(is_owner, key_docs, 0.0), axis=0, keepdims=True)
    query_index = lax.broadcasted_iota(jnp.int32, (256, 128), 0)
    _, _, query_lane = token_parts(query_index, core)
    pick = jnp.where(lax.broadcasted_iota(jnp.int32, (256, 128), 1) == query_lane, 1.0, 0.0).astype(BF)
    query_docs = dot_nt(pick, docs)
    query_index = lax.broadcasted_iota(jnp.int32, (256, 16), 0)
    _, query_owner, _ = token_parts(query_index, core)
    is_owner = owner(lax.broadcasted_iota(jnp.int32, (256, 16), 1)) == query_owner
    query_docs = jnp.sum(jnp.where(is_owner, query_docs, 0.0), axis=1, keepdims=True)
    key_index = lax.broadcasted_iota(jnp.int32, (256, 512), 1)
    key_position, _, _ = token_parts(key_index, key_index >> 8)
    query_position, _, _ = token_parts(lax.broadcasted_iota(jnp.int32, (256, 512), 0), core)
    allowed = (key_position <= query_position) & (key_docs == query_docs)

    value_bias = jnp.transpose(jnp.broadcast_to(bias[8:9], (128, 128)))
    value_bias = jnp.concatenate([value_bias] * 2, axis=1)
    wait_bytes(kvall.at[core, pl.ds(0, 7)], kv_recv)
    forward = remote(kvall.at[core], kvall.at[core], kf_send, kf_recv, partner)
    forward.start()
    remote(kvall.at[1 - core], kvall.at[1 - core], kf_send, kf_recv, partner).wait_recv()
    key_parts, value_parts = [], []
    for side in range(2):
        held = kvall[side]
        keys = held[:, :16].reshape(128, 256)
        first, second = keys[:64], keys[64:]
        cosine, sine = cosk[:, 256 * side : 256 * side + 256], sink[:, 256 * side : 256 * side + 256]
        key_parts.append(
            jnp.concatenate([first * cosine - second * sine, second * cosine + first * sine], axis=0).astype(BF)
        )
        value_parts.append((held[:, 16:].reshape(128, 256) + value_bias).astype(BF))
    keys = jnp.concatenate(key_parts, axis=1)
    values = jnp.concatenate(value_parts, axis=1)
    scores = dot_nn(queries, keys) / math.sqrt(HEAD_DIM)
    scores = jnp.where(allowed, scores, -jnp.inf)
    weights = jnp.where(allowed, jnp.exp(scores - jnp.max(scores, axis=1, keepdims=True)), 0.0)
    denominator = jnp.sum(weights, axis=1, keepdims=True)
    att[0] = (dot_nt(weights.astype(BF), values) / denominator).astype(BF)
    send_att = remote(att.at[0], att.at[1], at_send, at_recv, partner)
    send_att.start()

    wait_bytes(wo.at[core], ol_sem)
    wait_bytes(wo.at[1 - core], or_sem)

    def project_out(wave):
        @pl.loop(0, 8, unroll=4)
        def _(f):
            weights = jnp.concatenate([wo[0, f], wo[1, f]], axis=0)
            spread(wave, f, dot_nn(att[wave], weights))

    def finish_first(v):
        block = (tok_ref[token_unit(v), :].astype(F32) + final_sum(v)).astype(BF)
        resid[token_unit(v), :] = block
        ag[v, 0] = block
        gather_begin(v)

    project_out(0)
    scatter_far(wave_a)
    send_att.wait_recv()
    project_out(1)
    scatter_far(wave_b)
    scatter_near()
    gather_drain()
    scatter_relay()
    for k in (3, 2, 1):
        units(s2(k))
    units(s3)
    units(finish_first)
    units(gather_more)
    square_sums = square_row(resid[...].astype(F32))
    row = lax.broadcasted_iota(jnp.int32, (8, 128), 0)
    sums[0] = jnp.where(row == 0, square_sums, jnp.zeros((8, 128), F32))
    for d in range(1, 16):
        stat_copy(1, d).start()
    units(t1)
    units(t2)
    spread_roots(1)
    units(t4)
    units(t3)
    scatter_drain()
    for k in (1, 2, 3):
        units(passing_k(k))
    collect_roots(1)
    gather_own()
    for copy in local_copies[3:]:
        copy.wait()
    for copy in remote_copies[3:]:
        copy.wait_recv()

    accg[...] = jnp.zeros_like(accg)
    accu[...] = jnp.zeros_like(accu)

    for mine in (True, False):
        if not mine:
            gather_other()

        @pl.loop(0, 8, unroll=4)
        def _(f):
            block = normalized(f, mine, 8)
            cols = feature_columns(f, mine)
            for side in range(2):
                accg[side] += dot_nt(block, wg[side, :, cols])
                accu[side] += dot_nt(block, wu[side, :, cols])

    for side in range(2):
        gate = accg[side]
        hid[0, side] = (gate / (1.0 + jnp.exp(-gate)) * accu[side]).astype(BF)
    send_hid = remote(hid.at[0], hid.at[1], hd_send, hd_recv, partner)
    send_hid.start()
    wait_bytes(wd.at[core], dl_sem)
    wait_bytes(wd.at[1 - core], dr_sem)

    def project_down(wave):
        @pl.loop(0, 8, unroll=4)
        def _(f):
            spread(wave, f, dot_nn(hid[wave, 0], wd[0, f]) + dot_nn(hid[wave, 1], wd[1, f]))

    def finish_second(v):
        out_ref[token_unit(v), :] = (resid[token_unit(v), :].astype(F32) + final_sum(v)).astype(BF)

    project_down(0)
    scatter_far(wave_a)
    send_hid.wait_recv()
    project_down(1)
    scatter_far(wave_b)
    scatter_near()
    gather_drain()
    scatter_relay()
    for k in (3, 2, 1):
        units(s2(k))
    units(s3)
    units(finish_second)
    scatter_drain()

    wait_bytes(stats.at[pl.ds(1, 15)], st_send)
    wait_bytes(sums.at[pl.ds(1, 15)], su_send)
    for phase in range(2):
        wait_bytes(roots.at[phase, pl.ds(1, 7)], ro_send.at[phase])
    wait_bytes(kvall.at[core, pl.ds(0, 7)], kv_send)
    forward.wait_send()
    send_att.wait_send()
    send_hid.wait_send()
    for copy in remote_copies:
        copy.wait_send()
    wait_bytes(wo.at[core], os_sem)
    wait_bytes(wd.at[core], ds_sem)


def rotary_tables():
    half = HEAD_DIM // 2
    frequency = np.power(np.float32(ROTARY_BASE), -(np.arange(half, dtype=np.float32) * 2.0) / HEAD_DIM).astype(np.float32)
    index = np.arange(TOKENS)
    side, item, low, along, row = index >> 8, (index >> 7) & 1, (index >> 6) & 1, (index >> 4) & 3, index & 15
    position = 256 * low + 64 * along + 32 * side + 16 * item + row
    angles = (position.astype(np.float32)[:, None] * frequency[None, :]).astype(np.float32)
    cosine, sine = np.cos(angles).astype(np.float32), np.sin(angles).astype(np.float32)
    return (
        np.ascontiguousarray(cosine.T), np.ascontiguousarray(sine.T),
        np.concatenate([cosine, cosine], axis=1), np.concatenate([-sine, sine], axis=1),
    )


def shards(
    tokens, segment_ids, attn_gain, query_weight, query_bias, key_weight, value_weight, value_bias,
    out_weight, ffn_gain, gate_weight, up_weight, down_weight,
):
    units = gate_weight.shape[0]
    any_spec = pl.BlockSpec(memory_space=pl.ANY)
    vmem_spec = pl.BlockSpec(memory_space=pltpu.VMEM)
    dma = pltpu.SemaphoreType.DMA
    return pl.pallas_call(
        kernel,
        out_shape=jax.ShapeDtypeStruct((64, BLOCK), BF),
        in_specs=[vmem_spec] * 6 + [any_spec] * 11,
        out_specs=vmem_spec,
        scratch_shapes=[
            pltpu.VMEM((2, 64, MODEL), BF),
            pltpu.VMEM((2, 2, 8, MODEL), BF),
            pltpu.VMEM((2, 8, 64, BLOCK), BF),
            pltpu.VMEM((2, units, MODEL), BF),
            pltpu.VMEM((2, units, MODEL), BF),
            pltpu.VMEM((2, 8, units, BLOCK), BF),
            pltpu.VMEM((64, 512), F32),
            pltpu.VMEM((64, 512), F32),
            pltpu.VMEM((512, 128), F32),
            pltpu.VMEM((512, 128), F32),
            pltpu.VMEM((4, 64, ROWS, BLOCK), BF),
            pltpu.VMEM((2, 64, ROWS, BLOCK), BF),
            pltpu.VMEM((16, 256, BLOCK), BF),
            pltpu.VMEM((4, 64, ROWS, BLOCK), F32),
            pltpu.VMEM((4, 64, ROWS, BLOCK), BF),
            pltpu.VMEM((4, 63, ROWS, BLOCK), BF),
            pltpu.VMEM((16, 16, 128), F32),
            pltpu.VMEM((16, 8, 128), F32),
            pltpu.VMEM((2, 8, 8, 128), F32),
            pltpu.VMEM((128, 128), F32),
            pltpu.VMEM((256, 128), F32),
            pltpu.VMEM((16, 128), F32),
            pltpu.VMEM((2, 8, 32, 256), F32),
            pltpu.VMEM((2, 256, 128), BF),
            pltpu.VMEM((2, 2, 256, units), BF),
            pltpu.VMEM((256, 128), F32),
            pltpu.VMEM((32, 256), F32),
            pltpu.VMEM((2, 256, units), F32),
            pltpu.VMEM((2, 256, units), F32),
            pltpu.VMEM((64, BLOCK), BF),
            dma((4,)), dma((4, 12)),
            dma((2,)), dma((2,)),
            dma((4,)), dma((4, 10)),
            dma, dma, dma, dma, dma((2,)), dma((2,)),
            dma, dma,
            dma, dma, dma, dma, dma, dma,
            dma((9,)), dma((5,)), dma((5,)),
            dma, dma, dma, dma, dma, dma,
        ],
        compiler_params=pltpu.CompilerParams(
            collective_id=0, has_side_effects=True, vmem_limit_bytes=60 * 1024 * 1024
        ),
        name="layer",
    )(
        tokens, segment_ids, attn_gain, ffn_gain, query_bias, value_bias, query_weight, key_weight, value_weight,
        out_weight, gate_weight, up_weight, down_weight, *rotary_tables(),
    )


def solution(mesh):
    placed = (
        P("gx", "gy"),
        P("gy"),
        P("gy"),
        P(("gx", "gy"), None),
        P("gx"),
        P(("gx", "gy"), None),
        P(("gx", "gy"), None),
        P("gx"),
        P(("gx", "gy"), None),
        P("gy"),
        P(("gx", "gy"), None),
        P(("gx", "gy"), None),
        P(("gx", "gy"), None),
    )
    return jax.shard_map(
        shards, mesh=mesh, in_specs=placed, out_specs=P("gx", "gy"), check_vma=False
    )
```

```python
import functools
import math

import jax
import jax.numpy as jnp
import numpy as np
from jax import lax
from jax.experimental import pallas as pl
from jax.experimental.pallas import tpu as pltpu
from jax.sharding import PartitionSpec as P


HEAD_DIM = 128
EPSILON = 1e-06
ROTARY_BASE = 1000000.0
TOKENS = 512
MODEL = 8192
BLOCK = 512
ROWS = 16
BF = jnp.bfloat16
F32 = jnp.float32
MESH = pl.DeviceIdType.MESH


def dot_nt(left, right):
    return lax.dot_general(left, right, (((1,), (1,)), ((), ())), preferred_element_type=F32)


def dot_nn(left, right):
    return lax.dot_general(left, right, (((1,), (0,)), ((), ())), preferred_element_type=F32)


GATHER = {}
for _sign, _seen in ((1, 2), (3, 1), (2, 3)):
    GATHER[f"own1_{_sign}"] = (0, _seen, 1, 1, _sign, 0)
    GATHER[f"own2_{_sign}"] = (0, 4 * _seen, 1, 2, _sign, 1)
    GATHER[f"row2_{_sign}"] = (1, 4 * _seen + 1, 3, 2, _sign, 2)
for _sign, _seen in ((1, 2), (3, 1)):
    for _k in range(4):
        GATHER[f"one3_{_k}_{_sign}"] = (4 * _k, 16 * _seen + 4 * _k, 1, 3, _sign, 4 * _seen + _k)
        GATHER[f"row3_{_k}_{_sign}"] = (4 * _k + 1, 16 * _seen + 4 * _k + 1, 3, 3, _sign, 4 * _seen + _k)
for _k in range(4):
    GATHER[f"pass3_{_k}_3"] = (16 + 4 * _k, 48 + 4 * _k, 2, 3, 3, 3)
    GATHER[f"pass3_{_k}_1"] = (32 + 4 * _k + 2, 48 + 4 * _k + 2, 2, 3, 1, 3)
ARRIVING = {0: 3, 1: 3, 2: 9, 3: 16, **{i: 4 for i in range(4, 12)}}

SCATTER = {}
for _k in (3, 2):
    SCATTER[f"far3_{_k}"] = (48 + 4 * _k, 4 * (3 - _k), 4, 3, 1, _k)
for _k in (1, 0):
    SCATTER[f"far3_{_k}"] = (48 + 4 * _k, 8 + 4 * (1 - _k), 4, 3, 3, _k)
for _k in range(4):
    SCATTER[f"up3_{_k}"] = (16 + 4 * _k, 16 + 4 * _k, 4, 3, 1, 4 + _k)
    SCATTER[f"down3_{_k}"] = (32 + 4 * _k, 32 + 4 * _k, 4, 3, 3, 4 + _k)
for _k, _sign in ((1, 1), (2, 3), (3, 2)):
    SCATTER[f"to2_{_k}"] = (4 * _k, 44 + 4 * _k, 4, 2, _sign, 8)
    SCATTER[f"to1_{_k}"] = (_k, 59 + _k, 1, 1, _sign, 9)
SUMMED = {**{i: 4 for i in range(4)}, **{i: 8 for i in range(4, 8)}, 8: 12, 9: 3}


def one_hot3(value):
    second, third = lax.rem(value, 2), lax.div(value, 2)
    return 1 - second - third, second, third


def kernel(
    tok_ref, segment_ref, gain_ref, ffn_gain_ref, query_bias_ref, value_bias_ref,
    wq_hbm, wk_hbm, wv_hbm, wo_hbm, wg_hbm, wu_hbm, wd_hbm,
    cosk_hbm, sink_hbm, cosq_hbm, sinq_hbm,
    out_ref,
    wq, wkv, wo, wg, wu, wd, cosk, sink, cosq, sinq,
    ag, xb, an, part, sb, rb, stats, sums, roots, tall, scale, bias, kvall, att, hid, accq, acckv, accg, accu, resid,
    ag_send, ag_recv, px_send, px_recv, rs_send, rs_recv, st_send, st_recv, su_send, su_recv, ro_send, ro_recv,
    kv_send, kv_recv, kf_send, kf_recv, at_send, at_recv, hd_send, hd_recv,
    wl_sem, ws_sem, wr_sem, ol_sem, os_sem, or_sem, dl_sem, ds_sem, dr_sem,
):
    gx, gy = lax.axis_index("gx"), lax.axis_index("gy")
    x, y_lo = lax.rem(gx, 4), lax.div(gx, 4)
    core, z, y_hi = lax.rem(gy, 2), lax.rem(lax.div(gy, 2), 4), lax.div(gy, 8)
    y = y_hi * 2 + y_lo
    chip = y_hi * 4 + z
    partner = (gx, gy + 1 - 2 * core)

    def device(x, y, z):
        return (lax.rem(y, 2) * 4 + x, lax.div(y, 2) * 8 + z * 2 + core)

    own_orders = [(lax.rem(bulk + 2, 3), 0) for bulk in (core, 2 * core, 1 - core, 2 - core)]
    other_orders = [(lax.rem(bulk + 2, 3), 0) for bulk in (core, 1 + core)]

    def neighbour(v, level, sign):
        bulk, choice = own_orders[v]
        step = {3: 0, 2: 1 + choice, 1: 2 - choice}[level]
        e0, e1, e2 = one_hot3(lax.rem(jnp.int32(bulk + step), 3))
        return device(lax.rem(x + sign * e0, 4), lax.rem(y + sign * e1, 4), lax.rem(z + sign * e2, 4))

    neighbours = {
        (v, level, sign): neighbour(v, level, sign) for v in range(4) for level in (1, 2, 3) for sign in (1, 2, 3)
    }

    def toward(v, level, sign):
        return neighbours[v, level, sign]

    def slot(position, mine):
        d = lax.rem(position - mine + 4, 4)
        return d + lax.div(d, 2) - 2 * lax.div(d, 3)

    def strides(order):
        bulk, choice = order
        result = []
        for axis in range(3):
            e0, e1, e2 = one_hot3(lax.rem(jnp.int32(axis + 3 - bulk), 3))
            result.append(16 * e0 + (4 - 3 * choice) * e1 + (1 + 3 * choice) * e2)
        return result

    x_slots = [slot(position, x) for position in range(4)]
    unit_strides = [strides(order) for order in own_orders]
    other_strides = [strides(order) for order in other_orders]

    def places(stride, f):
        fy, fz = lax.div(f, 4), lax.rem(f, 4)
        z_part = stride[2] * slot(fz, z)
        y_parts = [stride[1] * slot(fy * 2 + ty, y) + z_part for ty in range(2)]
        return [y_parts[ty] + stride[0] * x_slots[tx] for ty in range(2) for tx in range(4)]

    def remote(src, dst, send, recv, target):
        return pltpu.make_async_remote_copy(
            src_ref=src, dst_ref=dst, send_sem=send, recv_sem=recv, device_id=target, device_id_type=MESH
        )

    barrier = pltpu.get_barrier_semaphore()
    greeted = (
        [device(x, lax.rem(y + 3 + 2 * y_lo, 4), z)]
        + [(lax.rem(gx + e, 8), gy) for e in range(1, 8)]
        + [(gx, lax.rem(gy + d, 16)) for d in range(1, 16)]
    )
    for target in greeted:
        pl.semaphore_signal(barrier, inc=1, device_id=target, device_id_type=MESH)

    whole = (
        (wq_hbm, wq.at[core]), (wk_hbm, wkv.at[core, 0]), (wv_hbm, wkv.at[core, 1]),
        (wg_hbm, wg.at[core]), (wu_hbm, wu.at[core]),
    )
    tables = ((cosk_hbm, cosk), (sink_hbm, sink), (cosq_hbm, cosq), (sinq_hbm, sinq))
    local_copies = [
        pltpu.make_async_copy(src, dst, wl_sem.at[i]) for i, (src, dst) in enumerate(whole)
    ]
    table_copies = [
        pltpu.make_async_copy(src, dst, wl_sem.at[5 + i]) for i, (src, dst) in enumerate(tables)
    ]
    remote_copies = [
        remote(src, dst, ws_sem.at[i], wr_sem.at[i], partner) for i, (src, dst) in enumerate(whole)
    ]
    def wait_bytes(ref, semaphore):
        pltpu.make_async_copy(ref, ref, semaphore).wait()

    columns = lambda f, side: pl.ds(pl.multiple_of((2 * f + side) * BLOCK, BLOCK), BLOCK)
    out_local = [pltpu.make_async_copy(wo_hbm.at[:, columns(f, core)], wo.at[core, f], ol_sem) for f in range(8)]
    down_local = [pltpu.make_async_copy(wd_hbm.at[:, columns(f, core)], wd.at[core, f], dl_sem) for f in range(8)]
    out_remote = [remote(wo_hbm.at[:, columns(f, 1 - core)], wo.at[core, f], os_sem, or_sem, partner) for f in range(8)]
    down_remote = [remote(wd_hbm.at[:, columns(f, 1 - core)], wd.at[core, f], ds_sem, dr_sem, partner) for f in range(8)]
    for copy in local_copies[:3] + table_copies + out_local + local_copies[3:] + down_local:
        copy.start()

    def token_unit(v):
        return pl.ds(pl.multiple_of(16 * lax.rem(v + 2 * core, 4), 16), 16)

    def square_row(values):
        squares = values * values
        folded = squares[:, :128] + squares[:, 128:256] + squares[:, 256:384] + squares[:, 384:]
        row = jnp.sum(jnp.transpose(folded), axis=0, keepdims=True)
        return jnp.concatenate([row, jnp.zeros((1, 64), F32)], axis=1)

    def stat_copy(phase, d):
        there = (gx, lax.rem(gy + d, 16))
        if phase == 0:
            return remote(stats.at[0], stats.at[d], st_send, st_recv, there)
        return remote(sums.at[0], sums.at[d], su_send, su_recv, there)

    def root_copy(phase, e):
        return remote(
            roots.at[phase, 0], roots.at[phase, e], ro_send.at[phase], ro_recv.at[phase], (lax.rem(gx + e, 8), gy)
        )

    def spread_roots(phase):
        wait_bytes(*((stats.at[pl.ds(1, 15)], st_recv) if phase == 0 else (sums.at[pl.ds(1, 15)], su_recv)))
        summed = jnp.sum(stats[:, :8] if phase == 0 else sums[...], axis=0)
        inverse = lax.rsqrt(summed / MODEL + EPSILON)
        roots[phase, 0] = inverse
        for e in range(1, 8):
            root_copy(phase, e).start()

    def collect_roots(phase):
        wait_bytes(roots.at[phase, pl.ds(1, 7)], ro_recv.at[phase])
        factors = jnp.concatenate([roots[phase, e, :1] for e in range(8)], axis=0)
        tall[...] = jnp.transpose(jnp.concatenate([factors] * 16, axis=0))
        lane = lax.broadcasted_iota(jnp.int32, (16, 128), 1)
        for j in range(2):
            rows = tall[pl.ds(pl.multiple_of(32 * core + 16 * j, 16), 16), :]
            for owner_gx in range(8):
                column = jnp.sum(jnp.where(lane == lax.rem(gx + 8 - owner_gx, 8), rows, 0.0), axis=1, keepdims=True)
                scale[128 * j + 16 * owner_gx : 128 * j + 16 * owner_gx + 16] = jnp.broadcast_to(column, (16, 128))

    def normalized(f, mine, first_row):
        block = gathered(f, mine).astype(F32)
        held = lax.rem(gy + 16 - (2 * f + (core if mine else 1 - core)), 16)
        gains = stats[held, first_row : first_row + 4]
        gain = jnp.concatenate([gains[i : i + 1] for i in range(4)], axis=1)
        factor = scale[...]
        return (block * jnp.concatenate([factor] * 4, axis=1) * gain).astype(BF)

    def gather_copy(name, v):
        src, dst, count, level, sign, arrival = GATHER[name]
        return remote(
            ag.at[v, pl.ds(src, count)], ag.at[v, pl.ds(dst, count)], ag_send.at[v], ag_recv.at[v, arrival],
            toward(v, level, sign),
        )

    def px_copy(j, k):
        return remote(
            ag.at[2 + j, pl.ds(16 * k, 16)], xb.at[j, pl.ds(16 * k, 16)], px_send.at[j], px_recv.at[j], partner
        )

    wave_a, wave_b, in_order = (0, 1), (2, 3), (0, 2, 1, 3)

    def units(body, which=in_order):
        for v in which:
            body(v)

    def gather_begin(v):
        for sign in (1, 3, 2):
            gather_copy(f"own1_{sign}", v).start()

    def gather_more(v):
        for sign in (1, 3):
            gather_copy(f"one3_0_{sign}", v).start()
        for sign in (1, 3, 2):
            gather_copy(f"own2_{sign}", v).start()

    def gather_start(v, *names):
        for n in names:
            gather_copy(n, v).start()

    def gather_arrive(v, *arrivals):
        for a in arrivals:
            wait_bytes(ag.at[v, pl.ds(0, ARRIVING[a])], ag_recv.at[v, a])

    def t1(v):
        gather_arrive(v, 0)
        gather_start(v, "row2_1", "row2_3", "row2_2", "row3_0_1", "row3_0_3")

    def t2(v):
        gather_arrive(v, 1)
        for k in (1, 2, 3):
            gather_start(v, f"one3_{k}_1", f"one3_{k}_3")

    def t3(v):
        gather_arrive(v, 4, 8)
        gather_start(v, "pass3_0_3", "pass3_0_1")

    def t4(v):
        gather_arrive(v, 2)
        for k in (1, 2, 3):
            gather_start(v, f"row3_{k}_1", f"row3_{k}_3")
        if v >= 2:
            px_copy(v - 2, 0).start()

    def passing(v):
        for k in (1, 2, 3):
            gather_arrive(v, 4 + k, 8 + k)
            gather_start(v, f"pass3_{k}_3", f"pass3_{k}_1")
        if v >= 2:
            px_copy(v - 2, 1).start()
            px_copy(v - 2, 2).start()

    def passing_k(k):
        def step(v):
            gather_arrive(v, 4 + k, 8 + k)
            gather_start(v, f"pass3_{k}_3", f"pass3_{k}_1")
            if v >= 2 and k == 3:
                px_copy(v - 2, 1).start()
                px_copy(v - 2, 2).start()

        return step

    def t5(v):
        gather_arrive(v, 3)
        if v >= 2:
            px_copy(v - 2, 3).start()

    def gather_own():
        for v in (2, 3, 0, 1):
            t5(v)

    def gather_other():
        for j in range(2):
            wait_bytes(xb.at[j], px_recv.at[j])

    def gather_drain():
        for v in range(4):
            blocks = ag.at[v, pl.ds(0, 63)]
            pltpu.make_async_copy(blocks, blocks, ag_send.at[v]).wait()
        for j in range(2):
            pltpu.make_async_copy(xb.at[j], xb.at[j], px_send.at[j]).wait()

    def gathered(f, mine):
        pieces = []
        for j in range(2):
            for at in places(unit_strides[j] if mine else other_strides[j], f):
                pieces.append(ag[j, at] if mine else xb[j, at])
        return jnp.concatenate(pieces, axis=0)

    def feature_columns(f, mine):
        return columns(f, core if mine else 1 - core)

    def scatter_copy(name, v):
        src, dst, count, level, sign, arrival = SCATTER[name]
        return remote(
            sb.at[v, pl.ds(src, count)], rb.at[v, pl.ds(dst, count)], rs_send.at[v], rs_recv.at[v, arrival],
            toward(v, level, sign),
        )

    def rs_start(v, *names):
        for n in names:
            scatter_copy(n, v).start()

    def rs_arrive(v, *arrivals):
        for a in arrivals:
            blocks = rb.at[v, pl.ds(0, SUMMED[a])]
            pltpu.make_async_copy(blocks, blocks, rs_recv.at[v, a]).wait()

    def cast(v, src, count=4):
        sb[v, pl.ds(src, count)] = part[v, pl.ds(src, count)].astype(BF)

    def cast_sum(v, src, place_at, count=4):
        sb[v, pl.ds(src, count)] = (
            part[v, pl.ds(src, count)] + rb[v, pl.ds(place_at, count)].astype(F32)
        ).astype(BF)

    def scatter_far(which):
        for k in (3, 1, 2, 0):
            for v in which:
                cast(v, 48 + 4 * k)
                rs_start(v, f"far3_{k}")

    def scatter_near():
        for v in in_order:
            cast(v, 32 + 4 * 3)
            rs_start(v, "down3_3")
        for v in in_order:
            cast(v, 16 + 4 * 1)
            rs_start(v, "up3_1")
        for v in in_order:
            cast(v, 32 + 4 * 2)
            rs_start(v, "down3_2")

    def scatter_relay():
        for k, other in ((3, 1), (2, 0)):
            for v in in_order:
                rs_arrive(v, k)
                cast_sum(v, 16 + 4 * k, 4 * (3 - k))
                rs_start(v, f"up3_{k}")
            for v in in_order:
                rs_arrive(v, other)
                cast_sum(v, 32 + 4 * other, 8 + 4 * (1 - other))
                rs_start(v, f"down3_{other}")
        for v in in_order:
            cast(v, 16)
            rs_start(v, "up3_0")

    def total3(v, k):
        rs_arrive(v, 4 + k)
        return (
            part[v, pl.ds(4 * k, 4)]
            + rb[v, pl.ds(16 + 4 * k, 4)].astype(F32)
            + rb[v, pl.ds(32 + 4 * k, 4)].astype(F32)
        )

    def s2(k):
        def step(v):
            sb[v, pl.ds(4 * k, 4)] = total3(v, k).astype(BF)
            rs_start(v, f"to2_{k}")

        return step

    def s3(v):
        total = total3(v, 0)
        rs_arrive(v, 8)
        for place_at in (48, 52, 56):
            total = total + rb[v, pl.ds(place_at, 4)].astype(F32)
        part[v, 0] = total[0]
        sb[v, 1:4] = total[1:].astype(BF)
        rs_start(v, "to1_1", "to1_2", "to1_3")

    def final_sum(v):
        rs_arrive(v, 9)
        total = part[v, 0]
        for place_at in (60, 61, 62):
            total = total + rb[v, place_at].astype(F32)
        return total

    def scatter_drain():
        for v in range(4):
            blocks = sb.at[v, pl.ds(0, 63)]
            pltpu.make_async_copy(blocks, blocks, rs_send.at[v]).wait()

    def spread(wave, f, product):
        for j, v in enumerate((2 * wave, 2 * wave + 1)):
            for i, at in enumerate(places(unit_strides[v], f)):
                row = 128 * j + 16 * i
                part[v, at] = product[row : row + 16]

    for v in range(4):
        ag[v, 0] = tok_ref[token_unit(v), :]
    square_sums = square_row(tok_ref[...].astype(F32))
    stats[0] = jnp.zeros((16, 128), F32)
    stats[0, 0:1] = square_sums
    stats[0, 1:2, 0:32] = segment_ref[...].astype(F32).reshape(1, 32)
    stats[0, 4:8] = gain_ref[...].astype(F32).reshape(4, 128)
    stats[0, 8:12] = ffn_gain_ref[...].astype(F32).reshape(4, 128)
    bias[0:8] = query_bias_ref[...].astype(F32).reshape(8, 128)
    bias[8:9] = value_bias_ref[...].astype(F32).reshape(1, 128)
    pl.semaphore_wait(barrier, len(greeted))
    units(gather_begin)
    units(gather_more)
    for d in range(1, 16):
        stat_copy(0, d).start()
    for copy in remote_copies[:3]:
        copy.start()

    units(t1)
    spread_roots(0)
    for copy in out_remote + remote_copies[3:] + down_remote:
        copy.start()
    units(t2)
    units(t4)
    units(t3)
    for k in (1, 2, 3):
        units(passing_k(k))
    collect_roots(0)
    gather_own()
    documents = jnp.sum(
        jnp.where(lax.broadcasted_iota(jnp.int32, (16, 16, 128), 1) == 1, stats[...], 0.0), axis=1
    )
    for copy in local_copies[:3] + table_copies:
        copy.wait()
    for copy in remote_copies[:3]:
        copy.wait_recv()

    acckv[...] = jnp.zeros_like(acckv)

    for mine in (True, False):
        if not mine:
            gather_other()

        @pl.loop(0, 8, unroll=4)
        def _(f):
            cols = feature_columns(f, mine)
            weights = [wkv[side, kind, :, cols].astype(F32) for kind in range(2) for side in range(2)]
            weights = jnp.concatenate(weights, axis=0).astype(BF)
            block = normalized(f, mine, 4)
            an[2 * f + (0 if mine else 1)] = block
            acckv[...] += dot_nt(weights, block)

    kvall[core, chip] = acckv[...]

    def kv_copy(d):
        there = lax.rem(gy + 2 * d, 16)
        return remote(kvall.at[core, chip], kvall.at[core, chip], kv_send, kv_recv, (gx, there))

    for d in range(1, 8):
        kv_copy(d).start()

    accq[...] = jnp.zeros_like(accq)

    @pl.loop(0, 8, unroll=4)
    def _(f):
        for mine in (True, False):
            cols = feature_columns(f, mine)
            weights = jnp.concatenate([wq[0, :, cols], wq[1, :, cols]], axis=0)
            accq[...] += dot_nt(an[2 * f + (0 if mine else 1)], weights)

    query = accq[...] + bias[pl.ds(chip, 1), :]
    own_rows = pl.ds(pl.multiple_of(256 * core, 256), 256)
    turned = jnp.concatenate([query[:, 64:], query[:, :64]], axis=1)
    queries = (query * cosq[own_rows, :] + turned * sinq[own_rows, :]).astype(BF)

    def token_parts(index, own_core):
        item, low, along, row = (
            (index >> 7) & 1, (index >> 6) & 1, (index >> 4) & 3, index & 15,
        )
        return 256 * low + 64 * along + 32 * own_core + 16 * item + row, 8 * low + 2 * along + own_core, 16 * item + row

    def owner(index):
        held = gy - index
        return jnp.where(held < 0, held + 16, held)

    docs = documents.astype(BF)
    key_index = lax.broadcasted_iota(jnp.int32, (128, 512), 1)
    _, _, key_lane = token_parts(key_index, key_index >> 8)
    pick = jnp.where(lax.broadcasted_iota(jnp.int32, (128, 512), 0) == key_lane, 1.0, 0.0).astype(BF)
    key_docs = dot_nn(docs, pick)
    key_index = lax.broadcasted_iota(jnp.int32, (16, 512), 1)
    _, key_owner, _ = token_parts(key_index, key_index >> 8)
    is_owner = owner(lax.broadcasted_iota(jnp.int32, (16, 512), 0)) == key_owner
    key_docs = jnp.sum(jnp.where(is_owner, key_docs, 0.0), axis=0, keepdims=True)
    query_index = lax.broadcasted_iota(jnp.int32, (256, 128), 0)
    _, _, query_lane = token_parts(query_index, core)
    pick = jnp.where(lax.broadcasted_iota(jnp.int32, (256, 128), 1) == query_lane, 1.0, 0.0).astype(BF)
    query_docs = dot_nt(pick, docs)
    query_index = lax.broadcasted_iota(jnp.int32, (256, 16), 0)
    _, query_owner, _ = token_parts(query_index, core)
    is_owner = owner(lax.broadcasted_iota(jnp.int32, (256, 16), 1)) == query_owner
    query_docs = jnp.sum(jnp.where(is_owner, query_docs, 0.0), axis=1, keepdims=True)
    key_index = lax.broadcasted_iota(jnp.int32, (256, 512), 1)
    key_position, _, _ = token_parts(key_index, key_index >> 8)
    query_position, _, _ = token_parts(lax.broadcasted_iota(jnp.int32, (256, 512), 0), core)
    allowed = (key_position <= query_position) & (key_docs == query_docs)

    value_bias = jnp.transpose(jnp.broadcast_to(bias[8:9], (128, 128)))
    value_bias = jnp.concatenate([value_bias] * 2, axis=1)
    wait_bytes(kvall.at[core, pl.ds(0, 7)], kv_recv)
    forward = remote(kvall.at[core], kvall.at[core], kf_send, kf_recv, partner)
    forward.start()
    remote(kvall.at[1 - core], kvall.at[1 - core], kf_send, kf_recv, partner).wait_recv()
    key_parts, value_parts = [], []
    for side in range(2):
        held = kvall[side]
        keys = held[:, :16].reshape(128, 256)
        first, second = keys[:64], keys[64:]
        cosine, sine = cosk[:, 256 * side : 256 * side + 256], sink[:, 256 * side : 256 * side + 256]
        key_parts.append(
            jnp.concatenate([first * cosine - second * sine, second * cosine + first * sine], axis=0).astype(BF)
        )
        value_parts.append((held[:, 16:].reshape(128, 256) + value_bias).astype(BF))
    keys = jnp.concatenate(key_parts, axis=1)
    values = jnp.concatenate(value_parts, axis=1)
    scores = dot_nn(queries, keys) / math.sqrt(HEAD_DIM)
    scores = jnp.where(allowed, scores, -jnp.inf)
    weights = jnp.where(allowed, jnp.exp(scores - jnp.max(scores, axis=1, keepdims=True)), 0.0)
    denominator = jnp.sum(weights, axis=1, keepdims=True)
    att[0] = (dot_nt(weights.astype(BF), values) / denominator).astype(BF)
    send_att = remote(att.at[0], att.at[1], at_send, at_recv, partner)
    send_att.start()

    wait_bytes(wo.at[core], ol_sem)
    wait_bytes(wo.at[1 - core], or_sem)

    def project_out(wave):
        @pl.loop(0, 8, unroll=4)
        def _(f):
            weights = jnp.concatenate([wo[0, f], wo[1, f]], axis=0)
            spread(wave, f, dot_nn(att[wave], weights))

    def finish_first(v):
        block = (tok_ref[token_unit(v), :].astype(F32) + final_sum(v)).astype(BF)
        resid[token_unit(v), :] = block
        ag[v, 0] = block
        gather_begin(v)

    project_out(0)
    scatter_far(wave_a)
    send_att.wait_recv()
    project_out(1)
    scatter_far(wave_b)
    scatter_near()
    gather_drain()
    scatter_relay()
    units(lambda v: [s2(k)(v) for k in (3, 2, 1)])
    units(s3)
    units(finish_first)
    units(gather_more)
    square_sums = square_row(resid[...].astype(F32))
    row = lax.broadcasted_iota(jnp.int32, (8, 128), 0)
    sums[0] = jnp.where(row == 0, square_sums, jnp.zeros((8, 128), F32))
    for d in range(1, 16):
        stat_copy(1, d).start()
    units(t1)
    units(t2)
    spread_roots(1)
    units(t4)
    units(t3)
    scatter_drain()
    for k in (1, 2, 3):
        units(passing_k(k))
    collect_roots(1)
    gather_own()
    for copy in local_copies[3:]:
        copy.wait()
    for copy in remote_copies[3:]:
        copy.wait_recv()

    accg[...] = jnp.zeros_like(accg)
    accu[...] = jnp.zeros_like(accu)

    for mine in (True, False):
        if not mine:
            gather_other()

        @pl.loop(0, 8, unroll=4)
        def _(f):
            block = normalized(f, mine, 8)
            cols = feature_columns(f, mine)
            for side in range(2):
                accg[side] += dot_nt(block, wg[side, :, cols])
                accu[side] += dot_nt(block, wu[side, :, cols])

    for side in range(2):
        gate = accg[side]
        hid[0, side] = (gate / (1.0 + jnp.exp(-gate)) * accu[side]).astype(BF)
    send_hid = remote(hid.at[0], hid.at[1], hd_send, hd_recv, partner)
    send_hid.start()
    wait_bytes(wd.at[core], dl_sem)
    wait_bytes(wd.at[1 - core], dr_sem)

    def project_down(wave):
        @pl.loop(0, 8, unroll=4)
        def _(f):
            spread(wave, f, dot_nn(hid[wave, 0], wd[0, f]) + dot_nn(hid[wave, 1], wd[1, f]))

    def finish_second(v):
        out_ref[token_unit(v), :] = (resid[token_unit(v), :].astype(F32) + final_sum(v)).astype(BF)

    project_down(0)
    scatter_far(wave_a)
    send_hid.wait_recv()
    project_down(1)
    scatter_far(wave_b)
    scatter_near()
    gather_drain()
    scatter_relay()
    units(lambda v: [s2(k)(v) for k in (3, 2, 1)])
    units(s3)
    units(finish_second)
    scatter_drain()

    wait_bytes(stats.at[pl.ds(1, 15)], st_send)
    wait_bytes(sums.at[pl.ds(1, 15)], su_send)
    for phase in range(2):
        wait_bytes(roots.at[phase, pl.ds(1, 7)], ro_send.at[phase])
    wait_bytes(kvall.at[core, pl.ds(0, 7)], kv_send)
    forward.wait_send()
    send_att.wait_send()
    send_hid.wait_send()
    for copy in remote_copies:
        copy.wait_send()
    wait_bytes(wo.at[core], os_sem)
    wait_bytes(wd.at[core], ds_sem)


def rotary_tables():
    half = HEAD_DIM // 2
    frequency = np.power(np.float32(ROTARY_BASE), -(np.arange(half, dtype=np.float32) * 2.0) / HEAD_DIM).astype(np.float32)
    index = np.arange(TOKENS)
    side, item, low, along, row = index >> 8, (index >> 7) & 1, (index >> 6) & 1, (index >> 4) & 3, index & 15
    position = 256 * low + 64 * along + 32 * side + 16 * item + row
    angles = (position.astype(np.float32)[:, None] * frequency[None, :]).astype(np.float32)
    cosine, sine = np.cos(angles).astype(np.float32), np.sin(angles).astype(np.float32)
    return (
        np.ascontiguousarray(cosine.T), np.ascontiguousarray(sine.T),
        np.concatenate([cosine, cosine], axis=1), np.concatenate([-sine, sine], axis=1),
    )


def shards(
    tokens, segment_ids, attn_gain, query_weight, query_bias, key_weight, value_weight, value_bias,
    out_weight, ffn_gain, gate_weight, up_weight, down_weight,
):
    units = gate_weight.shape[0]
    any_spec = pl.BlockSpec(memory_space=pl.ANY)
    vmem_spec = pl.BlockSpec(memory_space=pltpu.VMEM)
    dma = pltpu.SemaphoreType.DMA
    return pl.pallas_call(
        kernel,
        out_shape=jax.ShapeDtypeStruct((64, BLOCK), BF),
        in_specs=[vmem_spec] * 6 + [any_spec] * 11,
        out_specs=vmem_spec,
        scratch_shapes=[
            pltpu.VMEM((2, 64, MODEL), BF),
            pltpu.VMEM((2, 2, 8, MODEL), BF),
            pltpu.VMEM((2, 8, 64, BLOCK), BF),
            pltpu.VMEM((2, units, MODEL), BF),
            pltpu.VMEM((2, units, MODEL), BF),
            pltpu.VMEM((2, 8, units, BLOCK), BF),
            pltpu.VMEM((64, 512), F32),
            pltpu.VMEM((64, 512), F32),
            pltpu.VMEM((512, 128), F32),
            pltpu.VMEM((512, 128), F32),
            pltpu.VMEM((4, 64, ROWS, BLOCK), BF),
            pltpu.VMEM((2, 64, ROWS, BLOCK), BF),
            pltpu.VMEM((16, 256, BLOCK), BF),
            pltpu.VMEM((4, 64, ROWS, BLOCK), F32),
            pltpu.VMEM((4, 64, ROWS, BLOCK), BF),
            pltpu.VMEM((4, 63, ROWS, BLOCK), BF),
            pltpu.VMEM((16, 16, 128), F32),
            pltpu.VMEM((16, 8, 128), F32),
            pltpu.VMEM((2, 8, 8, 128), F32),
            pltpu.VMEM((128, 128), F32),
            pltpu.VMEM((256, 128), F32),
            pltpu.VMEM((16, 128), F32),
            pltpu.VMEM((2, 8, 32, 256), F32),
            pltpu.VMEM((2, 256, 128), BF),
            pltpu.VMEM((2, 2, 256, units), BF),
            pltpu.VMEM((256, 128), F32),
            pltpu.VMEM((32, 256), F32),
            pltpu.VMEM((2, 256, units), F32),
            pltpu.VMEM((2, 256, units), F32),
            pltpu.VMEM((64, BLOCK), BF),
            dma((4,)), dma((4, 12)),
            dma((2,)), dma((2,)),
            dma((4,)), dma((4, 10)),
            dma, dma, dma, dma, dma((2,)), dma((2,)),
            dma, dma,
            dma, dma, dma, dma, dma, dma,
            dma((9,)), dma((5,)), dma((5,)),
            dma, dma, dma, dma, dma, dma,
        ],
        compiler_params=pltpu.CompilerParams(
            collective_id=0, has_side_effects=True, vmem_limit_bytes=60 * 1024 * 1024
        ),
        name="layer",
    )(
        tokens, segment_ids, attn_gain, ffn_gain, query_bias, value_bias, query_weight, key_weight, value_weight,
        out_weight, gate_weight, up_weight, down_weight, *rotary_tables(),
    )


def solution(mesh):
    placed = (
        P("gx", "gy"),
        P("gy"),
        P("gy"),
        P(("gx", "gy"), None),
        P("gx"),
        P(("gx", "gy"), None),
        P(("gx", "gy"), None),
        P("gx"),
        P(("gx", "gy"), None),
        P("gy"),
        P(("gx", "gy"), None),
        P(("gx", "gy"), None),
        P(("gx", "gy"), None),
    )
    return jax.shard_map(
        shards, mesh=mesh, in_specs=placed, out_specs=P("gx", "gy"), check_vma=False
    )
```
